32 devices in a mesh: dp: 2 (over y), context: 4 (over x, core), expert: 4 (over z).
Axes of the slice: x: 2, y: 2, z: 4, core: 2. Of those that a mesh axis runs over, the one named last changes fastest.
Arguments:
- tokens: bfloat16 [8, 512, 2048], P(('dp', 'expert'), 'context'), may hold values from -6 to 6
- routes: int32 [8, 512, 6], P(('dp', 'expert'), 'context'), may hold values from 0 to 15, all different within a row; in each aligned block of 128 rows (0 to 127, 128 to 255, ..., all dimensions but the last counted through in order) at most 54 rows name the same one
- grad_out: bfloat16 [8, 512, 2048], P(('dp', 'expert'), 'context'), may hold values from -6 to 6
- attn_gain: bfloat16 [2048], P(('dp', 'context')), may hold values from 0.25 to 1.75
- query_weight: bfloat16 [2048, 3072], P(('dp', 'context'), 'expert'), may hold values from -0.125 to 0.125
- latent_down: bfloat16 [2048, 576], P(('dp', 'context')), may hold values from -0.125 to 0.125
- latent_gain: bfloat16 [512], P(('dp', 'context')), may hold values from 0.25 to 1.75
- latent_up: bfloat16 [512, 4096], P(('dp', 'context'), 'expert'), may hold values from -0.25 to 0.25
- out_weight: bfloat16 [2048, 2048], P('expert', ('dp', 'context')), may hold values from -1 to 1
- ffn_gain: bfloat16 [2048], P(('dp', 'context')), may hold values from 0.25 to 1.75
- router_weight: bfloat16 [2048, 16], P(('dp', 'context')), may hold values from -0.0625 to 0.0625
- shared_gate: bfloat16 [2048, 2816], P(('dp', 'context'), 'expert'), may hold values from -0.125 to 0.125
- shared_up: bfloat16 [2048, 2816], P(('dp', 'context'), 'expert'), may hold values from -0.125 to 0.125
- shared_down: bfloat16 [2816, 2048], P('expert', ('dp', 'context')), may hold values from -0.109375 to 0.109375
- expert_gate: bfloat16 [16, 2048, 1408], P('expert', ('dp', 'context')), may hold values from -0.125 to 0.125
- expert_up: bfloat16 [16, 2048, 1408], P('expert', ('dp', 'context')), may hold values from -0.125 to 0.125
- expert_down: bfloat16 [16, 1408, 2048], P('expert', ('dp', 'context')), may hold values from -1.25 to 1.25
Outputs:
- block_out: bfloat16 [8, 512, 2048], P(('dp', 'expert'), 'context')
- grad_tokens: float32 [8, 512, 2048], P(('dp', 'expert'), 'context')
- grad_attn_gain: float32 [2048], P(('dp', 'context', 'expert'))
- grad_query_weight: float32 [2048, 3072], P(('dp', 'context'), 'expert')
- grad_latent_down: float32 [2048, 576], P(('dp', 'context', 'expert'))
- grad_latent_gain: float32 [512], P(('dp', 'context', 'expert'))
- grad_latent_up: float32 [512, 4096], P(('dp', 'context'), 'expert')
- grad_out_weight: float32 [2048, 2048], P('expert', ('dp', 'context'))
- grad_ffn_gain: float32 [2048], P(('dp', 'context', 'expert'))
- grad_router_weight: float32 [2048, 16], P(('dp', 'context', 'expert'))
- grad_shared_gate: float32 [2048, 2816], P(('dp', 'context'), 'expert')
- grad_shared_up: float32 [2048, 2816], P(('dp', 'context'), 'expert')
- grad_shared_down: float32 [2816, 2048], P('expert', ('dp', 'context'))
- grad_expert_gate: float32 [16, 2048, 1408], P('expert', ('dp', 'context'))
- grad_expert_up: float32 [16, 2048, 1408], P('expert', ('dp', 'context'))
- grad_expert_down: float32 [16, 1408, 2048], P('expert', ('dp', 'context'))
The draws below stay inside these ranges and needn't reach their ends.
Inputs may be any that keep to these rules, and one draw needn't show every extreme that they name: `routes`: each token names 6 different experts. Among the tokens of one device (aligned blocks of 128 rows) no expert is named more than 54 times, and in every draw some expert is named exactly 54 times.
All inputs are finite; a program needn't handle non-finite values.
Results may differ from the reference program's by a relative error of at most 0.025.
Values may be sent and summed in bfloat16 or wider, within the bound.
A program may use at most 320 MiB of HBM per device.

```python
import math
import jax
import jax.numpy as jnp
import numpy as np
from jax import lax

D = 2048
HEADS = 16
NOPE = 128
ROPE = 64
VDIM = 128
LATENT = 512
FFN = 1408
SHARED = 2816
TOPK = 6
PROMPT_DEV = 64
TOK_DEV = 128
PROMPT_LEN = 256
ROWS = 512
GROUPS = 8
EXPERTS = 16
CAP = 54


def level_of(rng, dims, split, low, top_value):
    loudness = 1.0
    for dim, parts in split:
        draws = jax.random.uniform(jax.random.fold_in(jax.random.fold_in(rng, 6), dim), (parts,), jnp.float32, low / len(split), top_value / len(split))
        loudness = loudness * jnp.repeat(jnp.exp(draws), dims[dim] // parts).reshape((-1,) + (1,) * (len(dims) - 1 - dim))
    return loudness


def assign_block(key, own, number, rows, amount, top, most, slope):
    sequence = jax.random.permutation(key, amount)
    crowded, usual = portions_of(amount, rows * top, most, slope, True), portions_of(amount, rows * top, most, slope, False)
    places = jnp.arange(amount)

    def named(lengths, rotation):
        used = int((lengths > 0).sum())
        fixed = max(1, used // 4)
        passed = fixed + (places - fixed + rotation * (used - fixed)) % max(1, amount - fixed)
        return jnp.zeros((amount,), jnp.int32).at[sequence[jnp.where(places < fixed, places, passed)]].set(jnp.asarray(lengths, jnp.int32))

    lengths = jnp.where(number % 4 == 0, named(crowded, number // 4), named(usual, number - number // 4 - 1))
    mixed = jax.random.permutation(jax.random.fold_in(own, 3), amount)
    donor, taker = mixed[0:amount // 2 * 2:2], mixed[1:amount // 2 * 2:2]
    slack = jnp.minimum(lengths[donor] - 1, most - lengths[taker]) // 2
    slack = jnp.where((donor == sequence[0]) | (taker == sequence[0]) | (lengths[taker] == 0), 0, jnp.maximum(slack, 0))
    passed = jax.random.randint(jax.random.fold_in(own, 4), (amount // 2,), 0, 1 << 20) % (slack + 1)
    lengths = lengths.at[donor].add(-passed).at[taker].add(passed)
    members = jnp.searchsorted(jnp.cumsum(lengths), jnp.arange(rows * top), side="right").astype(jnp.int32)
    table = members.reshape(top, rows).T
    table = table[jax.random.permutation(jax.random.fold_in(own, 1), rows)]
    rotation = jax.random.randint(jax.random.fold_in(own, 2), (rows, 1), 0, top)
    return jnp.take_along_axis(table, (jnp.arange(top)[None, :] + rotation) % top, axis=1)


def portions_of(count, total, reach, skew, full):
    portions = [(1 << 20) // math.isqrt(standing ** skew) + 1 for standing in range(1, count + 1)]
    largest = reach if full else min(reach, max(-(-total // count), total * portions[0] // sum(portions)))
    least = 1 if total - largest >= count - 1 else 0
    given, surplus = [largest] + [least] * (count - 1), total - largest - least * (count - 1)
    while surplus > 0:
        free = [i for i in range(1, count) if given[i] < largest] or [i for i in range(1, count) if given[i] < reach]
        mass, remaining = sum([portions[i] for i in free]), surplus
        for i in free:
            more = min(reach - given[i], max(1, remaining * portions[i] // mass), surplus)
            given[i] = given[i] + more
            surplus = surplus - more
    return np.array(given)


def scatter_about(stream_key, dims, deviation, reach, cuts=(), held_as=jnp.bfloat16):
    factor_of = level_of(stream_key, dims, cuts, -0.22, 0.18) if cuts else 1.0
    drawn = jax.random.normal(stream_key, dims, jnp.float32) * deviation * factor_of
    return jnp.minimum(jnp.maximum(drawn, -reach), reach).astype(held_as)


def setup_inputs(seed: int = 0) -> dict:
    arg_keys = jax.random.split(jax.random.key(seed), 18)
    tokens = scatter_about(arg_keys[0], (GROUPS, ROWS, D), 1.0, 6.0, ((0, 8), (1, 4)))
    routes_keys = jax.random.split(jax.random.fold_in(arg_keys[1], 1), GROUPS * ROWS // TOK_DEV)
    routes_turns = jax.random.permutation(jax.random.fold_in(arg_keys[1], 3), GROUPS * ROWS // TOK_DEV)
    routes = jax.vmap(lambda own, number: assign_block(jax.random.fold_in(arg_keys[1], 2), own, number, TOK_DEV, EXPERTS, TOPK, CAP, 2))(routes_keys, routes_turns).reshape((GROUPS, ROWS, TOPK))
    grad_out = scatter_about(arg_keys[2], (GROUPS, ROWS, D), 1.0, 6.0, ((0, 8), (1, 4)))
    attn_gain = jnp.clip(1.0 + 0.15 * jax.random.normal(arg_keys[3], (D,), jnp.float32), 0.25, 1.75).astype(jnp.bfloat16)
    query_weight = scatter_about(arg_keys[4], (D, HEADS * (NOPE + ROPE)), D ** -0.5, 0.125, ((0, 8), (1, 4)))
    latent_down = scatter_about(arg_keys[5], (D, LATENT + ROPE), D ** -0.5, 0.125, ((0, 8),))
    latent_gain = jnp.clip(1.0 + 0.15 * jax.random.normal(arg_keys[6], (LATENT,), jnp.float32), 0.25, 1.75).astype(jnp.bfloat16)
    latent_up = scatter_about(arg_keys[7], (LATENT, HEADS * (NOPE + VDIM)), LATENT ** -0.5, 0.25, ((0, 8), (1, 4)))
    out_weight = scatter_about(arg_keys[8], (HEADS * VDIM, D), (HEADS * VDIM // 64) ** -0.5, 1.0, ((0, 4), (1, 8)))
    ffn_gain = jnp.clip(1.0 + 0.15 * jax.random.normal(arg_keys[9], (D,), jnp.float32), 0.25, 1.75).astype(jnp.bfloat16)
    router_weight = scatter_about(arg_keys[10], (D, EXPERTS), (4 * D) ** -0.5, 0.0625, ((0, 8),))
    shared_gate = scatter_about(arg_keys[11], (D, SHARED), D ** -0.5, 0.125, ((0, 8), (1, 4)))
    shared_up = scatter_about(arg_keys[12], (D, SHARED), D ** -0.5, 0.125, ((0, 8), (1, 4)))
    shared_down = scatter_about(arg_keys[13], (SHARED, D), SHARED ** -0.5, 0.109375, ((0, 4), (1, 8)))
    expert_gate = scatter_about(arg_keys[14], (EXPERTS, D, FFN), D ** -0.5, 0.125, ((0, 4), (1, 8)))
    expert_up = scatter_about(arg_keys[15], (EXPERTS, D, FFN), D ** -0.5, 0.125, ((0, 4), (1, 8)))
    expert_down = scatter_about(arg_keys[16], (EXPERTS, FFN, D), (max(FFN // 64, 1)) ** -0.5, 1.25, ((0, 4), (1, 8)))
    return {"tokens": tokens, "routes": routes, "grad_out": grad_out, "attn_gain": attn_gain, "query_weight": query_weight, "latent_down": latent_down, "latent_gain": latent_gain, "latent_up": latent_up, "out_weight": out_weight, "ffn_gain": ffn_gain, "router_weight": router_weight, "shared_gate": shared_gate, "shared_up": shared_up, "shared_down": shared_down, "expert_gate": expert_gate, "expert_up": expert_up, "expert_down": expert_down}


@jax.custom_vjp
def low(v):
    return lax.optimization_barrier(v.astype(jnp.bfloat16)).astype(jnp.float32)

@jax.custom_vjp
def low_back(v):
    return v

def low_keep(v):
    return (low(v), None)

def low_pass(kept, grad):
    return (grad,)

def back_keep(v):
    return (v, None)

def back_low(kept, grad):
    return (low(grad),)
low.defvjp(low_keep, low_pass)
low_back.defvjp(back_keep, back_low)
epsilon = 1e-06

def matmul(left_side, right_side):
    return jnp.dot(left_side, right_side, precision=lax.Precision.HIGHEST)

def norm_rows(values, scale_gain):
    return values * lax.rsqrt(lax.optimization_barrier(jnp.mean(values * values, axis=-1, keepdims=True)) + epsilon) * scale_gain

def rotary(values, places):
    half_size = values.shape[-1] // 2
    frequency = 10000.0 ** (-jnp.arange(half_size, dtype=jnp.float32) / half_size)
    angles = places[:, None] * frequency[None, :]
    target_shape = (values.shape[0],) + (1,) * (values.ndim - 2) + (half_size,)
    cosine = jnp.cos(angles).reshape(target_shape)
    sine_part = jnp.sin(angles).reshape(target_shape)
    lower_half = values[..., :half_size]
    upper_half = values[..., half_size:]
    return jnp.concatenate([lower_half * cosine - upper_half * sine_part, upper_half * cosine + lower_half * sine_part], axis=-1)

def group_layout():
    row_ids = jnp.arange(ROWS, dtype=jnp.int32)
    holder = row_ids // TOK_DEV
    within = row_ids % TOK_DEV
    prompt_row = within < PROMPT_DEV
    places = jnp.where(prompt_row, holder * PROMPT_DEV + within, PROMPT_LEN + within - PROMPT_DEV)
    allowed = (places[None, :] <= places[:, None]) & (prompt_row[None, :] | (holder[None, :] == holder[:, None]))
    return (places.astype(jnp.float32), allowed)

def attention_group(tokens_group, attn_gain, query_weight, latent_down, latent_gain, latent_up, out_weight):
    places, allowed = group_layout()
    normed = low(norm_rows(tokens_group, attn_gain))
    query_raw = low_back(matmul(normed, query_weight)).reshape(ROWS, HEADS, NOPE + ROPE)
    query = low(jnp.concatenate([query_raw[..., :NOPE], rotary(query_raw[..., NOPE:], places)], axis=-1))
    compressed = low_back(matmul(normed, latent_down))
    packed = low(jnp.concatenate([norm_rows(compressed[:, :LATENT], latent_gain), rotary(compressed[:, LATENT:], places)], axis=-1))
    expanded = low(matmul(packed[:, :LATENT], latent_up)).reshape(ROWS, HEADS, NOPE + VDIM)
    raw_scores = jnp.einsum('qhd,khd->hqk', query[..., :NOPE], expanded[..., :NOPE], precision=lax.Precision.HIGHEST)
    raw_scores = raw_scores + jnp.einsum('qhd,kd->hqk', query[..., NOPE:], packed[:, LATENT:], precision=lax.Precision.HIGHEST)
    raw_scores = low_back(raw_scores)
    scores = jnp.where(allowed[None], raw_scores * (NOPE + ROPE) ** (-0.5), -1e+30)
    probs = jax.nn.softmax(scores, axis=-1)
    mixed = jnp.einsum('hqk,khd->qhd', low(probs), expanded[..., NOPE:], precision=lax.Precision.HIGHEST)
    mixed = low_back(low(mixed.reshape(ROWS, HEADS * VDIM)))
    return tokens_group + low_back(matmul(mixed, out_weight))

def expert_rows(inputs):
    rows_in, gate_matrix, up_matrix, down_matrix = inputs
    gate_part = low_back(matmul(rows_in, gate_matrix))
    up_part = low_back(matmul(rows_in, up_matrix))
    return low(matmul(low(jax.nn.silu(gate_part) * up_part), down_matrix))

def feed_forward(middle, route_rows, ffn_gain, router_weight, shared_gate, shared_up, shared_down, expert_gate, expert_up, expert_down):
    count = middle.shape[0]
    blocks = count // TOK_DEV
    hidden = low(norm_rows(middle, ffn_gain))
    logits = matmul(hidden, router_weight)
    gates = jnp.take_along_axis(jax.nn.softmax(logits, axis=-1), route_rows, axis=1)
    gate_shared = low_back(matmul(hidden, shared_gate))
    up_shared = low_back(matmul(hidden, shared_up))
    shared_out = low_back(matmul(low(jax.nn.silu(gate_shared) * up_shared), shared_down))
    pairs = low_back(jnp.repeat(hidden, TOPK, axis=0))
    chosen_ids = route_rows.reshape(blocks, TOK_DEV * TOPK)
    onehot = (chosen_ids[..., None] == jnp.arange(EXPERTS, dtype=jnp.int32)).astype(jnp.int32)
    within_rank = lax.optimization_barrier(jnp.sum(onehot * (jnp.cumsum(onehot, axis=1) - 1), axis=-1))
    slots = (chosen_ids * (blocks * CAP) + jnp.arange(blocks, dtype=jnp.int32)[:, None] * CAP + within_rank).reshape(-1).astype(jnp.int32)
    sources = jnp.zeros((EXPERTS * blocks * CAP,), jnp.int32).at[slots].set(jnp.arange(count * TOPK, dtype=jnp.int32) + 1)
    filled = (sources > 0)[:, None]
    gathered = jnp.where(filled, pairs[jnp.maximum(sources - 1, 0)], 0.0).reshape(EXPERTS, blocks * CAP, D)
    results = lax.map(jax.checkpoint(expert_rows), (gathered, expert_gate, expert_up, expert_down))
    returned = low_back(results.reshape(EXPERTS * blocks * CAP, D)[slots]).reshape(count, TOPK, D)
    return middle + shared_out + lax.optimization_barrier(jnp.sum(gates[..., None] * returned, axis=1))

def reference(tokens, routes, grad_out, attn_gain, query_weight, latent_down, latent_gain, latent_up, out_weight, ffn_gain, router_weight, shared_gate, shared_up, shared_down, expert_gate, expert_up, expert_down):
    weights = tuple((weight_arg.astype(jnp.float32) for weight_arg in (attn_gain, query_weight, latent_down, latent_gain, latent_up, out_weight, ffn_gain, router_weight, shared_gate, shared_up, shared_down, expert_gate, expert_up, expert_down)))
    route_rows = routes.reshape(GROUPS * ROWS, TOPK).astype(jnp.int32)

    def forward(tokens_f, attn_gain, query_weight, latent_down, latent_gain, latent_up, out_weight, ffn_gain, router_weight, shared_gate, shared_up, shared_down, expert_gate, expert_up, expert_down):

        def one_group(tokens_group):
            return attention_group(tokens_group, attn_gain, query_weight, latent_down, latent_gain, latent_up, out_weight)
        middle = lax.map(jax.checkpoint(one_group), tokens_f)
        final = feed_forward(middle.reshape(GROUPS * ROWS, D), route_rows, ffn_gain, router_weight, shared_gate, shared_up, shared_down, expert_gate, expert_up, expert_down)
        return final.reshape(GROUPS, ROWS, D)
    final, backward = jax.vjp(forward, tokens.astype(jnp.float32), *weights)
    grads = backward(grad_out.astype(jnp.float32))
    return (final.astype(jnp.bfloat16), grads[0], grads[1], grads[2], grads[3], grads[4], grads[5], grads[6], grads[7], grads[8], grads[9], grads[10], grads[11], grads[12], grads[13], grads[14])
```

```python
import jax
import jax.numpy as jnp
from jax import lax
from jax.experimental.layout import Layout, with_layout_constraint
from jax.sharding import PartitionSpec as P

D = 2048
NOPE = 128
ROPE = 64
VDIM = 128
LATENT = 512
TOPK = 6
PROMPT_DEV = 64
CONT_LEN = 64
TOK_DEV = 128


epsilon = 1e-06


def norm_rows(values, scale_gain):
    return (
        values * lax.rsqrt(jnp.mean(values * values, axis=-1, keepdims=True) + epsilon) * scale_gain
    )


def rotary_tables(places, half_size):
    frequency = 10000.0 ** (-jnp.arange(half_size, dtype=jnp.float32) / half_size)
    angles = places[:, None] * frequency[None, :]
    return (jnp.cos(angles), jnp.sin(angles))


def rotate(values, cosine, sine_part):
    half_size = values.shape[-1] // 2
    lower_half = values[..., :half_size]
    upper_half = values[..., half_size:]
    return jnp.concatenate(
        [
            lower_half * cosine - upper_half * sine_part,
            upper_half * cosine + lower_half * sine_part,
        ],
        axis=-1,
    )


def product(left_side, right_side):
    return jnp.dot(left_side, right_side, preferred_element_type=jnp.float32)


def product_left(left_side, right_side):
    return lax.dot_general(
        left_side, right_side, (((0,), (0,)), ((), ())), preferred_element_type=jnp.float32
    )


def product_right(left_side, right_side):
    return lax.dot_general(
        left_side, right_side, (((1,), (1,)), ((), ())), preferred_element_type=jnp.float32
    )


def against_rows(left_side, right_side):
    return lax.dot_general(
        left_side,
        right_side,
        (((left_side.ndim - 1,), (1,)), ((), ())),
        preferred_element_type=jnp.float32,
    )


PLANE = ("dp", "context")


def swap(values, axis, mask):
    count = lax.axis_size(axis)
    return lax.ppermute(values, axis, [(i, i ^ mask) for i in range(count)])


def place_pieces(pieces, index, count):
    first = pieces[0]
    whole = jnp.zeros((count,) + first.shape, first.dtype)
    for mask, piece in pieces.items():
        whole = lax.dynamic_update_slice(whole, piece[None], (index ^ mask,) + (0,) * first.ndim)
    return with_layout_constraint(whole, Layout(tuple(range(whole.ndim))))


def halves(values):
    middle_row = values.shape[0] // 2
    return values[:middle_row], values[middle_row:]


def plane_pieces(values):
    count = lax.axis_size(PLANE)
    if count == 8:
        by_two = swap(values, PLANE, 2)
        by_four = swap(values, PLANE, 4)
        upper = swap(halves(by_two)[0], PLANE, 4)
        lower = swap(halves(by_four)[1], PLANE, 2)
        pieces = {0: values, 2: by_two, 4: by_four, 6: jnp.concatenate([upper, lower], axis=0)}
        for mask in (0, 2, 4, 6):
            pieces[mask + 1] = swap(pieces[mask], PLANE, 1)
        return pieces
    pieces = {0: values}
    bit = 1
    while bit < count:
        for mask in range(bit):
            pieces[mask + bit] = swap(pieces[mask], PLANE, bit)
        bit *= 2
    return pieces


def plane_gather(values):
    count = lax.axis_size(PLANE)
    whole = place_pieces(plane_pieces(values), lax.axis_index(PLANE), count)
    return whole.reshape((count * values.shape[0],) + values.shape[1:])


def low(values):
    return values.astype(jnp.bfloat16)


def wide(values):
    return values.astype(jnp.float32)


def plane_scatter(values):
    count = lax.axis_size(PLANE)
    index = lax.axis_index(PLANE)
    blocks = values.reshape((count, values.shape[0] // count) + values.shape[1:])

    def part(mask):
        return lax.dynamic_index_in_dim(blocks, index ^ mask, 0, keepdims=False)

    sums = {}
    for mask in range(0, count, 2):
        sums[mask] = wide(part(mask)) + wide(swap(part(mask + 1), PLANE, 1))
    if count == 8:
        upper, lower = halves(low(sums[6]))
        by_four = jnp.concatenate(
            [
                low(halves(sums[4])[0] + wide(swap(upper, PLANE, 2))),
                low(halves(sums[4])[1]),
            ],
            axis=0,
        )
        by_two = jnp.concatenate(
            [
                low(halves(sums[2])[0]),
                low(halves(sums[2])[1] + wide(swap(lower, PLANE, 4))),
            ],
            axis=0,
        )
        return sums[0] + wide(swap(by_four, PLANE, 4)) + wide(swap(by_two, PLANE, 2))
    total = sums[0]
    for mask in range(2, count, 2):
        total = total + wide(swap(low(sums[mask]), PLANE, mask))
    return total


def axis_gather(values, axis):
    count = lax.axis_size(axis)
    pieces = {mask: swap(values, axis, mask) if mask else values for mask in range(count)}
    return place_pieces(pieces, lax.axis_index(axis), count)


def axis_scatter(blocks, axis):
    count = lax.axis_size(axis)
    index = lax.axis_index(axis)

    def part(mask):
        return lax.dynamic_index_in_dim(blocks, index ^ mask, 0, keepdims=False)

    total = wide(part(0))
    for mask in range(1, count):
        total = total + wide(swap(low(part(mask)), axis, mask))
    return total


def body(
    tokens,
    routes,
    grad_out,
    attn_gain,
    query_weight,
    latent_down,
    latent_gain,
    latent_up,
    out_weight,
    ffn_gain,
    router_weight,
    shared_gate,
    shared_up,
    shared_down,
    expert_gate,
    expert_up,
    expert_down,
):
    contexts = lax.axis_size("context")
    context_index = lax.axis_index("context")
    groups_local = lax.axis_size("expert")
    expert_index = lax.axis_index("expert")
    plane_count = lax.axis_size(PLANE)
    plane_index = lax.axis_index(PLANE)
    local_experts = expert_gate.shape[0]
    experts_all = router_weight.shape[1]
    copies = plane_count // local_experts
    expert_own = plane_index // copies
    query_cols = query_weight.shape[1]
    heads_local = query_cols // (NOPE + ROPE)
    down_cols = LATENT + ROPE
    shard_rows = query_weight.shape[0]
    latent_rows = latent_up.shape[0]
    prompt_len = PROMPT_DEV * contexts
    capacity = (TOK_DEV * TOPK * 9 + 8 * experts_all - 1) // (8 * experts_all)
    slots = groups_local * capacity
    token_count = groups_local * TOK_DEV
    score_scale = (NOPE + ROPE) ** (-0.5)

    used_cols = query_cols + down_cols
    extra_cols = experts_all + 3
    pad_cols = -(used_cols + extra_cols) % 128
    latent_gain_col = jnp.concatenate(
        [latent_gain, jnp.zeros((shard_rows - latent_gain.shape[0],), jnp.bfloat16)]
    )
    first_local = jnp.concatenate(
        [
            query_weight,
            latent_down,
            router_weight,
            attn_gain[:, None],
            ffn_gain[:, None],
            latent_gain_col[:, None],
            jnp.zeros((shard_rows, pad_cols), jnp.bfloat16),
        ],
        axis=1,
    )
    first_full = plane_gather(first_local)
    up_local = plane_gather(latent_up)
    out_local = plane_gather(out_weight.T)
    full_router = first_full[:, used_cols : used_cols + experts_all]
    full_attn_gain = first_full[:, used_cols + experts_all]
    full_ffn_gain = first_full[:, used_cols + experts_all + 1]
    full_latent_gain = first_full[:, used_cols + experts_all + 2].reshape(plane_count, shard_rows)
    full_latent_gain = full_latent_gain[:, : latent_gain.shape[0]].reshape(LATENT)

    within = jnp.arange(TOK_DEV, dtype=jnp.int32)
    query_places = jnp.where(
        within < PROMPT_DEV, context_index * PROMPT_DEV + within, prompt_len + within - PROMPT_DEV
    )
    key_places = jnp.arange(prompt_len + CONT_LEN, dtype=jnp.int32)
    allowed = key_places[None, :] <= query_places[:, None]
    cosine, sine_part = rotary_tables(query_places.astype(jnp.float32), ROPE // 2)
    cosine_heads = cosine[None, :, None, :]
    sine_heads = sine_part[None, :, None, :]
    source = wide(tokens[0])
    normed_low = low(norm_rows(source, wide(full_attn_gain)))

    def pack_latent(comp_rows, latent_scale):
        return jnp.concatenate(
            [
                norm_rows(comp_rows[..., :LATENT], latent_scale),
                rotate(comp_rows[..., LATENT:], cosine[None], sine_part[None]),
            ],
            axis=-1,
        )

    normed_all = axis_gather(normed_low, "expert")
    grad_all = axis_gather(grad_out[0], "expert")
    routes_all = axis_gather(routes[0], "expert")
    first_product = product(normed_all, first_full)
    compressed = first_product[..., query_cols:used_cols]
    packed = low(pack_latent(compressed, wide(full_latent_gain)))
    prompt_keys = axis_gather(packed[:, :PROMPT_DEV], "context")
    cont_keys = packed[:, PROMPT_DEV:]
    query_raw = first_product[..., :query_cols].reshape(
        groups_local, TOK_DEV, heads_local, NOPE + ROPE
    )
    query_rows = low(
        jnp.concatenate(
            [query_raw[..., :NOPE], rotate(query_raw[..., NOPE:], cosine_heads, sine_heads)], axis=-1
        )
    )
    query_nope = query_rows[..., :NOPE]
    query_rope = query_rows[..., NOPE:]
    prompt_latent = prompt_keys[..., :LATENT]
    prompt_rope = prompt_keys[..., LATENT:]
    cont_latent = cont_keys[..., :LATENT]
    cont_rope = cont_keys[..., LATENT:]
    prompt_exp = low(product(prompt_latent, up_local)).reshape(
        contexts, groups_local, PROMPT_DEV, heads_local, NOPE + VDIM
    )
    cont_exp = low(product(cont_latent, up_local)).reshape(
        groups_local, CONT_LEN, heads_local, NOPE + VDIM
    )
    prompt_knope = prompt_exp[..., :NOPE]
    prompt_values = prompt_exp[..., NOPE:]
    cont_knope = cont_exp[..., :NOPE]
    cont_values = cont_exp[..., NOPE:]

    def split_keys(values):
        return (
            values[..., :prompt_len].reshape(
                groups_local, heads_local, TOK_DEV, contexts, PROMPT_DEV
            ),
            values[..., prompt_len:],
        )

    def score_all():
        prompt_part = jnp.einsum(
            "gqhd,cgphd->ghqcp", query_nope, prompt_knope, preferred_element_type=jnp.float32
        )
        prompt_part = prompt_part + jnp.einsum(
            "gqhd,cgpd->ghqcp", query_rope, prompt_rope, preferred_element_type=jnp.float32
        )
        prompt_part = prompt_part.reshape(groups_local, heads_local, TOK_DEV, prompt_len)
        cont_part = jnp.einsum(
            "gqhd,gphd->ghqp", query_nope, cont_knope, preferred_element_type=jnp.float32
        )
        cont_part = cont_part + jnp.einsum(
            "gqhd,gpd->ghqp", query_rope, cont_rope, preferred_element_type=jnp.float32
        )
        raw_scores = jnp.concatenate([prompt_part, cont_part], axis=-1)
        return jnp.where(allowed, raw_scores * score_scale, -1e30)

    scores = score_all()
    top_score = jnp.max(scores, axis=-1, keepdims=True)
    exp_scores = jnp.exp(scores - top_score)
    totals = jnp.sum(exp_scores, axis=-1, keepdims=True)
    probs_all = exp_scores / totals
    probs_low = low(probs_all)
    probs_prompt, probs_cont = split_keys(probs_low)
    mixed_rows = jnp.einsum(
        "ghqcp,cgphd->gqhd", probs_prompt, prompt_values, preferred_element_type=jnp.float32
    )
    mixed_rows = mixed_rows + jnp.einsum(
        "ghqp,gphd->gqhd", probs_cont, cont_values, preferred_element_type=jnp.float32
    )
    mixed_all = low(mixed_rows.reshape(groups_local, TOK_DEV, heads_local * VDIM))
    partial_sum = against_rows(mixed_all, out_local)
    middle = source + axis_scatter(low(partial_sum), "expert")
    hidden_own = low(norm_rows(middle, wide(full_ffn_gain)))
    hidden_all = axis_gather(hidden_own, "expert")
    hidden_flat = hidden_all.reshape(token_count, D)
    grad_flat = grad_all.reshape(token_count, D)

    def fetch_expert(weight):
        pieces = {}
        for k in range(local_experts):
            part = lax.dynamic_index_in_dim(weight, expert_own ^ k, 0, keepdims=False)
            pieces[k * copies] = swap(part, PLANE, k * copies) if k else part
        for k in range(local_experts):
            for other in range(1, copies):
                pieces[k * copies + other] = swap(pieces[k * copies], PLANE, other)
        whole = place_pieces(pieces, plane_index, plane_count)
        return whole.reshape(plane_count * weight.shape[1], weight.shape[2])

    def return_expert(partial):
        rows = partial.shape[0] // plane_count
        blocks = partial.reshape(plane_count, rows, partial.shape[1])

        def part(mask):
            return lax.dynamic_index_in_dim(blocks, plane_index ^ mask, 0, keepdims=False)

        received = []
        for k in range(local_experts):
            total = wide(part(k * copies))
            for other in range(1, copies):
                total = total + wide(swap(part(k * copies + other), PLANE, other))
            received.append(wide(swap(low(total), PLANE, k * copies)) if k else total)
        order = []
        for e in range(local_experts):
            chosen = received[0]
            for k in range(1, local_experts):
                chosen = jnp.where(expert_own ^ k == e, received[k], chosen)
            order.append(chosen)
        return jnp.stack(order)

    def exchange(blocks):
        return [swap(blocks[k], PLANE, k * copies) if k else blocks[k] for k in range(local_experts)]

    slot_experts = expert_index * local_experts + (
        expert_own ^ jnp.arange(local_experts, dtype=jnp.int32)
    )
    expert_cols = jnp.arange(experts_all, dtype=jnp.int32)[:, None] == slot_experts[None, :]
    chosen_slots = jnp.any(routes_all[..., None] == slot_experts, axis=2)
    before = (within[:, None] > within[None, :]).astype(jnp.bfloat16)
    rank = jnp.einsum(
        "ts,gsl->gtl",
        before,
        chosen_slots.astype(jnp.bfloat16),
        preferred_element_type=jnp.float32,
    ).astype(jnp.int32)
    slot_of = jnp.where(
        chosen_slots,
        rank + capacity * jnp.arange(groups_local, dtype=jnp.int32)[:, None, None],
        -1,
    ).reshape(token_count, local_experts)
    picked = (
        slot_of.T[:, None, :] == jnp.arange(slots, dtype=jnp.int32)[None, :, None]
    )
    picked_low = picked.astype(jnp.bfloat16).reshape(local_experts * slots, token_count)
    gate_full = fetch_expert(expert_gate)
    up_full = fetch_expert(expert_up)
    down_full = fetch_expert(expert_down)
    grad_slots = low(product(picked_low, grad_flat)).reshape(local_experts, slots, D)
    grad_rows = jnp.concatenate(exchange(grad_slots), axis=0)
    hidden_slots = low(product(picked_low, hidden_flat)).reshape(local_experts, slots, D)
    hidden_rows = jnp.concatenate(exchange(hidden_slots), axis=0)
    logits = product(hidden_flat, full_router)
    expert_probs = jax.nn.softmax(logits, axis=-1)
    gate_tokens = jnp.sum(
        jnp.where(expert_cols[None], expert_probs[:, :, None], 0.0), axis=1
    )
    gate_slots = jnp.sum(jnp.where(picked, gate_tokens.T[:, None, :], 0.0), axis=-1)
    gate_rows = jnp.concatenate(exchange(gate_slots), axis=0)[:, None]
    grad_act = product_right(grad_rows, down_full)
    gate_expert = product(hidden_rows, gate_full)
    up_expert = product(hidden_rows, up_full)
    sigmoid_part = jax.nn.sigmoid(gate_expert)
    silu_part = gate_expert * sigmoid_part
    act_expert = silu_part * up_expert
    grad_gate_rows = jnp.sum(act_expert * grad_act, axis=-1)
    act_low = low(act_expert * gate_rows)
    grad_act = grad_act * gate_rows
    grad_gate_expert = low(
        grad_act * up_expert * sigmoid_part * (1.0 + gate_expert * (1.0 - sigmoid_part))
    )
    grad_up_expert = low(grad_act * silu_part)
    result = low(product(act_low, down_full)).reshape(local_experts, slots, D)
    result_back = jnp.concatenate(exchange(result), axis=0)
    routed_term = product_left(picked_low, result_back)
    grad_pair = low(
        product_right(grad_gate_expert, gate_full) + product_right(grad_up_expert, up_full)
    ).reshape(local_experts, slots, D)
    grad_pair_back = jnp.concatenate(exchange(grad_pair), axis=0)
    grad_routed = product_left(picked_low, grad_pair_back)
    grad_gate_back = jnp.stack(exchange(grad_gate_rows.reshape(local_experts, slots)))
    grad_expert_gate = return_expert(low(product_left(hidden_rows, grad_gate_expert)))
    grad_expert_up = return_expert(low(product_left(hidden_rows, grad_up_expert)))
    grad_expert_down = return_expert(low(product_left(act_low, grad_rows)))

    shared_full = plane_gather(jnp.concatenate([shared_gate, shared_up], axis=1))
    shared_cols = shared_gate.shape[1]
    shared_down_local = plane_gather(shared_down.T)
    shared_product = product(hidden_flat, shared_full)
    gate_shared = shared_product[:, :shared_cols]
    up_shared = shared_product[:, shared_cols:]
    sigmoid_shared = jax.nn.sigmoid(gate_shared)
    silu_shared = gate_shared * sigmoid_shared
    act_shared = low(silu_shared * up_shared)
    branch_out = low(product_right(act_shared, shared_down_local) + routed_term)
    final_rows = middle + axis_scatter(branch_out.reshape(groups_local, TOK_DEV, D), "expert")
    block_out = low(final_rows)
    grad_final = wide(grad_out[0])

    grad_gate_tokens = jnp.sum(jnp.where(picked, grad_gate_back[:, :, None], 0.0), axis=1).T
    grad_spread = jnp.sum(
        jnp.where(expert_cols[None], grad_gate_tokens[:, None, :], 0.0), axis=-1
    )
    weighted = jnp.sum(expert_probs * grad_spread, axis=-1, keepdims=True)
    grad_logits = expert_probs * (grad_spread - weighted)
    grad_router = lax.dot_general(
        wide(hidden_flat),
        grad_logits,
        (((0,), (0,)), ((), ())),
        precision=lax.Precision.HIGHEST,
    )
    grad_from_router = lax.dot_general(
        grad_logits,
        wide(full_router),
        (((1,), (1,)), ((), ())),
        precision=lax.Precision.HIGHEST,
    )
    grad_shared_down = low(product_left(grad_flat, act_shared))
    grad_act_shared = product(grad_flat, shared_down_local)
    grad_gate_shared = low(
        grad_act_shared * up_shared * sigmoid_shared * (1.0 + gate_shared * (1.0 - sigmoid_shared))
    )
    grad_up_shared = low(grad_act_shared * silu_shared)
    grad_shared = jnp.concatenate([grad_gate_shared, grad_up_shared], axis=1)
    grad_shared_first = low(product_left(hidden_flat, grad_shared))
    grad_hidden_part = low(
        product_right(grad_shared, shared_full) + grad_routed + grad_from_router
    )
    grad_hidden = axis_scatter(grad_hidden_part.reshape(groups_local, TOK_DEV, D), "expert")
    _, ffn_norm_back = jax.vjp(norm_rows, middle, wide(full_ffn_gain))
    grad_middle_norm, grad_ffn_gain = ffn_norm_back(grad_hidden)
    grad_middle = grad_final + grad_middle_norm
    branch_all = axis_gather(low(grad_middle), "expert")
    grad_out_weight = low(
        product_left(
            branch_all.reshape(token_count, D), mixed_all.reshape(token_count, heads_local * VDIM)
        )
    )
    grad_mixed = low(product(branch_all, out_local)).reshape(
        groups_local, TOK_DEV, heads_local, VDIM
    )
    grad_probs_prompt = jnp.einsum(
        "gqhd,cgphd->ghqcp", grad_mixed, prompt_values, preferred_element_type=jnp.float32
    )
    grad_probs_cont = jnp.einsum(
        "gqhd,gphd->ghqp", grad_mixed, cont_values, preferred_element_type=jnp.float32
    )
    grad_probs = jnp.concatenate(
        [
            grad_probs_prompt.reshape(groups_local, heads_local, TOK_DEV, prompt_len),
            grad_probs_cont,
        ],
        axis=-1,
    )
    delta_rows = jnp.sum(probs_all * grad_probs, axis=-1, keepdims=True)
    grad_raw = low(probs_all * (grad_probs - delta_rows) * score_scale)
    raw_prompt, raw_cont = split_keys(grad_raw)
    value_prompt = jnp.einsum(
        "ghqcp,gqhd->cgphd", probs_prompt, grad_mixed, preferred_element_type=jnp.float32
    )
    value_cont = jnp.einsum(
        "ghqp,gqhd->gphd", probs_cont, grad_mixed, preferred_element_type=jnp.float32
    )
    knope_prompt = jnp.einsum(
        "ghqcp,gqhd->cgphd", raw_prompt, query_nope, preferred_element_type=jnp.float32
    )
    knope_cont = jnp.einsum(
        "ghqp,gqhd->gphd", raw_cont, query_nope, preferred_element_type=jnp.float32
    )
    krope_prompt = jnp.einsum(
        "ghqcp,gqhd->cgpd", raw_prompt, query_rope, preferred_element_type=jnp.float32
    )
    krope_cont = jnp.einsum(
        "ghqp,gqhd->gpd", raw_cont, query_rope, preferred_element_type=jnp.float32
    )
    grad_query_nope = jnp.einsum(
        "ghqcp,cgphd->gqhd", raw_prompt, prompt_knope, preferred_element_type=jnp.float32
    )
    grad_query_nope = grad_query_nope + jnp.einsum(
        "ghqp,gphd->gqhd", raw_cont, cont_knope, preferred_element_type=jnp.float32
    )
    grad_query_rope = jnp.einsum(
        "ghqcp,cgpd->gqhd", raw_prompt, prompt_rope, preferred_element_type=jnp.float32
    )
    grad_query_rope = grad_query_rope + jnp.einsum(
        "ghqp,gpd->gqhd", raw_cont, cont_rope, preferred_element_type=jnp.float32
    )
    grad_query_raw = jnp.concatenate(
        [grad_query_nope, rotate(grad_query_rope, cosine_heads, -sine_heads)], axis=-1
    )
    grad_query_raw = low(
        grad_query_raw.reshape(groups_local, TOK_DEV, heads_local * (NOPE + ROPE))
    )
    grad_exp_prompt = low(
        jnp.concatenate([knope_prompt, value_prompt], axis=-1).reshape(
            contexts, groups_local, PROMPT_DEV, heads_local * (NOPE + VDIM)
        )
    )
    grad_exp_cont = low(
        jnp.concatenate([knope_cont, value_cont], axis=-1).reshape(
            groups_local, CONT_LEN, heads_local * (NOPE + VDIM)
        )
    )
    latent_prompt = jnp.einsum(
        "cgpf,lf->cgpl", grad_exp_prompt, up_local, preferred_element_type=jnp.float32
    )
    latent_cont = jnp.einsum(
        "gpf,lf->gpl", grad_exp_cont, up_local, preferred_element_type=jnp.float32
    )
    grad_prompt_keys = jnp.concatenate([latent_prompt, krope_prompt], axis=-1)
    grad_cont_keys = jnp.concatenate([latent_cont, krope_cont], axis=-1)
    prompt_sum = axis_scatter(grad_prompt_keys, "context")
    grad_packed = jnp.concatenate([prompt_sum, grad_cont_keys], axis=1)
    _, pack_back = jax.vjp(pack_latent, compressed, wide(full_latent_gain))
    grad_compressed, grad_latent_gain = pack_back(grad_packed)
    grad_first = jnp.concatenate(
        [
            grad_query_raw,
            low(grad_compressed),
            jnp.zeros((groups_local, TOK_DEV, first_full.shape[1] - used_cols), jnp.bfloat16),
        ],
        axis=-1,
    )
    grad_normed = axis_scatter(low(against_rows(grad_first, first_full)), "expert")
    _, attn_norm_back = jax.vjp(norm_rows, source, wide(full_attn_gain))
    grad_source_norm, grad_attn_gain = attn_norm_back(grad_normed)
    grad_tokens = grad_middle + grad_source_norm

    grad_latent_up = jnp.einsum(
        "cgpl,cgpf->lf", prompt_latent, grad_exp_prompt, preferred_element_type=jnp.float32
    )
    grad_latent_up = grad_latent_up + jnp.einsum(
        "gpl,gpf->lf", cont_latent, grad_exp_cont, preferred_element_type=jnp.float32
    )
    first_back = product_left(
        normed_all.reshape(token_count, D), grad_first.reshape(token_count, first_full.shape[1])
    )
    latent_gain_back = jnp.concatenate(
        [
            grad_latent_gain.reshape(plane_count, LATENT // plane_count),
            jnp.zeros((plane_count, shard_rows - LATENT // plane_count), jnp.float32),
        ],
        axis=1,
    ).reshape(D)
    extra_back = jnp.concatenate(
        [
            grad_router,
            grad_attn_gain[:, None],
            grad_ffn_gain[:, None],
            latent_gain_back[:, None],
            jnp.zeros((D, pad_cols), jnp.float32),
        ],
        axis=1,
    )
    first_back = low(jnp.concatenate([first_back[:, :used_cols], extra_back], axis=1))
    first_sum = plane_scatter(first_back)
    small_sum = first_sum[:, query_cols:]
    small_rows = shard_rows // groups_local
    small_own = axis_scatter(
        small_sum.reshape(groups_local, small_rows, small_sum.shape[1]), "expert"
    )
    latent_small = first_sum[: LATENT // plane_count, used_cols + experts_all + 2]
    latent_own = axis_scatter(
        latent_small.reshape(groups_local, LATENT // plane_count // groups_local), "expert"
    )
    up_sum = plane_scatter(low(grad_latent_up))
    out_sum = plane_scatter(grad_out_weight)
    shared_sum = plane_scatter(grad_shared_first)
    shared_down_sum = plane_scatter(grad_shared_down)
    return (
        block_out[None],
        grad_tokens[None],
        small_own[:, down_cols + experts_all],
        first_sum[:, :query_cols],
        small_own[:, :down_cols],
        latent_own,
        up_sum,
        out_sum.T,
        small_own[:, down_cols + experts_all + 1],
        small_own[:, down_cols : down_cols + experts_all],
        shared_sum[:, :shared_cols],
        shared_sum[:, shared_cols:],
        shared_down_sum.T,
        grad_expert_gate,
        grad_expert_up,
        grad_expert_down,
    )


def solution(mesh):
    in_specs = (
        P(("dp", "expert"), "context", None),
        P(("dp", "expert"), "context", None),
        P(("dp", "expert"), "context", None),
        P(("dp", "context")),
        P(("dp", "context"), "expert"),
        P(("dp", "context"), None),
        P(("dp", "context")),
        P(("dp", "context"), "expert"),
        P("expert", ("dp", "context")),
        P(("dp", "context")),
        P(("dp", "context"), None),
        P(("dp", "context"), "expert"),
        P(("dp", "context"), "expert"),
        P("expert", ("dp", "context")),
        P("expert", ("dp", "context"), None),
        P("expert", ("dp", "context"), None),
        P("expert", ("dp", "context"), None),
    )
    out_specs = (
        P(("dp", "expert"), "context", None),
        P(("dp", "expert"), "context", None),
        P(("dp", "context", "expert")),
        P(("dp", "context"), "expert"),
        P(("dp", "context", "expert"), None),
        P(("dp", "context", "expert")),
        P(("dp", "context"), "expert"),
        P("expert", ("dp", "context")),
        P(("dp", "context", "expert")),
        P(("dp", "context", "expert"), None),
        P(("dp", "context"), "expert"),
        P(("dp", "context"), "expert"),
        P("expert", ("dp", "context")),
        P("expert", ("dp", "context"), None),
        P("expert", ("dp", "context"), None),
        P("expert", ("dp", "context"), None),
    )
    return jax.shard_map(body, mesh=mesh, in_specs=in_specs, out_specs=out_specs, check_vma=False)
```

```python
import jax
import jax.numpy as jnp
from jax import lax
from jax.experimental import pallas as pl
from jax.experimental.pallas import tpu as pltpu
from jax.experimental.layout import Layout, with_layout_constraint
from jax.sharding import PartitionSpec as P

D = 2048
NOPE = 128
ROPE = 64
VDIM = 128
LATENT = 512
TOPK = 6
PROMPT_DEV = 64
CONT_LEN = 64
TOK_DEV = 128


epsilon = 1e-06


def norm_rows(values, scale_gain):
    return (
        values * lax.rsqrt(jnp.mean(values * values, axis=-1, keepdims=True) + epsilon) * scale_gain
    )


def rotary_tables(places, half_size):
    frequency = 10000.0 ** (-jnp.arange(half_size, dtype=jnp.float32) / half_size)
    angles = places[:, None] * frequency[None, :]
    return (jnp.cos(angles), jnp.sin(angles))


def rotate(values, cosine, sine_part):
    half_size = values.shape[-1] // 2
    lower_half = values[..., :half_size]
    upper_half = values[..., half_size:]
    return jnp.concatenate(
        [
            lower_half * cosine - upper_half * sine_part,
            upper_half * cosine + lower_half * sine_part,
        ],
        axis=-1,
    )


def product(left_side, right_side):
    return jnp.dot(left_side, right_side, preferred_element_type=jnp.float32)


def product_left(left_side, right_side):
    return lax.dot_general(
        left_side, right_side, (((0,), (0,)), ((), ())), preferred_element_type=jnp.float32
    )


def product_right(left_side, right_side):
    return lax.dot_general(
        left_side, right_side, (((1,), (1,)), ((), ())), preferred_element_type=jnp.float32
    )


def against_rows(left_side, right_side):
    return lax.dot_general(
        left_side,
        right_side,
        (((left_side.ndim - 1,), (1,)), ((), ())),
        preferred_element_type=jnp.float32,
    )


DP_AXIS, CONTEXT_AXIS, EXPERT_AXIS = "dp", "context", "expert"
PLANE = (DP_AXIS, CONTEXT_AXIS)


def swap(values, axis, mask):
    count = lax.axis_size(axis)
    return lax.ppermute(values, axis, [(i, i ^ mask) for i in range(count)])


def place_pieces(pieces, index, count):
    first = pieces[0]
    whole = jnp.zeros((count,) + first.shape, first.dtype)
    for mask, piece in pieces.items():
        whole = lax.dynamic_update_slice(whole, piece[None], (index ^ mask,) + (0,) * first.ndim)
    return with_layout_constraint(whole, Layout(tuple(range(whole.ndim))))


def low(values):
    return values.astype(jnp.bfloat16)


def wide(values):
    return values.astype(jnp.float32)


def axis_gather(values, axis):
    count = lax.axis_size(axis)
    pieces = {mask: swap(values, axis, mask) if mask else values for mask in range(count)}
    return place_pieces(pieces, lax.axis_index(axis), count)


def axis_scatter(blocks, axis):
    count = lax.axis_size(axis)
    index = lax.axis_index(axis)

    def part(mask):
        return lax.dynamic_index_in_dim(blocks, index ^ mask, 0, keepdims=False)

    total = wide(part(0))
    for mask in range(1, count):
        total = total + wide(swap(low(part(mask)), axis, mask))
    return total


MESH_ID = pl.DeviceIdType.MESH
ANY = pl.BlockSpec(memory_space=pl.ANY)
INSIDE = pl.BlockSpec(memory_space=pltpu.VMEM)


def plane_here():
    return lax.axis_index(DP_AXIS) * lax.axis_size(CONTEXT_AXIS) + lax.axis_index(CONTEXT_AXIS)


def plane_device(mask):
    contexts = lax.axis_size(CONTEXT_AXIS)
    other = jnp.bitwise_xor(plane_here(), mask)
    return {DP_AXIS: other // contexts, CONTEXT_AXIS: lax.rem(other, contexts)}


def line_device(offset):
    return {EXPERT_AXIS: lax.axis_index(EXPERT_AXIS) + offset}


def signal(device):
    pl.semaphore_signal(
        pltpu.get_barrier_semaphore(), inc=1, device_id=device, device_id_type=MESH_ID
    )


def meet(masks, line):
    count = len(masks)
    for mask in masks:
        signal(plane_device(mask))
    if line:
        place, last = lax.axis_index(EXPERT_AXIS), lax.axis_size(EXPERT_AXIS) - 1
        pl.when(place > 0)(lambda: signal(line_device(-1)))
        pl.when(place < last)(lambda: signal(line_device(1)))
        count = count + jnp.where(place > 0, 1, 0) + jnp.where(place < last, 1, 0)
    pl.semaphore_wait(pltpu.get_barrier_semaphore(), count)


def remote(source, target, send, recv, device):
    return pltpu.make_async_remote_copy(
        src_ref=source,
        dst_ref=target,
        send_sem=send,
        recv_sem=recv,
        device_id=device,
        device_id_type=MESH_ID,
    )


def arrived(target, send, recv):
    remote(target, target, send, recv, plane_device(1)).wait_recv()


def run_tasks(*tasks):
    active = list(tasks)
    while active:
        for task in list(active):
            if next(task, None) is None:
                active.remove(task)


def plane_gather_task(source, target, own, send, recv):
    rows = source.shape[0]
    half = rows // 2
    here = plane_here()

    def slot(mask, first=0, count=rows):
        start = pl.multiple_of(jnp.bitwise_xor(here, mask) * rows + first, 16)
        return target.at[pl.ds(start, count)]

    def go(number, source_ref, target_ref, mask):
        copy = remote(source_ref, target_ref, send.at[number], recv.at[number], plane_device(mask))
        copy.start()
        return copy

    def got(number, ref):
        arrived(ref, send.at[number], recv.at[number])

    local = pltpu.make_async_copy(source, slot(0), own)
    copies = [go(0, source, slot(0), 2), go(1, source, slot(0), 4)]
    yield 1
    copies.append(go(4, source, slot(0), 1))
    local.start()
    yield 1
    got(0, slot(2))
    copies.append(go(2, slot(2, 0, half), slot(2, 0, half), 4))
    copies.append(go(5, slot(2), slot(2), 1))
    yield 1
    got(1, slot(4))
    copies.append(go(3, slot(4, half, half), slot(4, half, half), 2))
    copies.append(go(6, slot(4), slot(4), 1))
    yield 1
    got(2, slot(6, 0, half))
    copies.append(go(7, slot(6, 0, half), slot(6, 0, half), 1))
    yield 1
    got(3, slot(6, half, half))
    copies.append(go(8, slot(6, half, half), slot(6, half, half), 1))
    yield 1
    got(4, slot(1))
    got(5, slot(3))
    got(6, slot(5))
    got(7, slot(7, 0, half))
    got(8, slot(7, half, half))
    local.wait()
    for copy in copies:
        copy.wait_send()


def expert_fetch_task(source, target, stage, own, send, recv):
    if source.shape[0] == 1:
        load = pltpu.make_async_copy(source.at[0], stage, own)
        load.start()
        load.wait()
        yield from plane_gather_task(stage, target, own, send, recv)
        return
    rows = source.shape[1]
    here = plane_here()
    expert_own = here // 2

    def slot(mask):
        start = pl.multiple_of(jnp.bitwise_xor(here, mask) * rows, 16)
        return target.at[pl.ds(start, rows)]

    def go(number, source_ref, target_ref, mask):
        copy = remote(source_ref, target_ref, send.at[number], recv.at[number], plane_device(mask))
        copy.start()
        return copy

    def got(number, ref):
        arrived(ref, send.at[number], recv.at[number])

    copies = []
    for k in (3, 1, 2):
        copies.append(go(k, source.at[jnp.bitwise_xor(expert_own, k)], slot(0), 2 * k))
    load = pltpu.make_async_copy(source.at[expert_own], stage, own)
    load.start()
    yield 1
    load.wait()
    local = pltpu.make_async_copy(stage, slot(0), own)
    local.start()
    copies.append(go(0, stage, slot(0), 1))
    for k in (1, 2, 3):
        yield 1
        got(k, slot(2 * k))
        copies.append(go(4 + k, slot(2 * k), slot(2 * k), 1))
    yield 1
    got(0, slot(1))
    for k in (1, 2, 3):
        got(4 + k, slot(2 * k + 1))
    local.wait()
    for copy in copies:
        copy.wait_send()


LINE_PARTS = 4


def line_gather_steps(target, send, recv, rows):
    place, count = lax.axis_index(EXPERT_AXIS), lax.axis_size(EXPERT_AXIS)
    part = rows // LINE_PARTS

    def piece(block, c):
        return target.at[block, pl.ds(c * part, part)]

    def copy(way, distance, c, source=None):
        block = place - way * distance
        ref = piece(block, c)
        return remote(
            ref if source is None else source,
            ref,
            send.at[(way + 1) // 2, distance, c],
            recv.at[(way + 1) // 2, distance, c],
            line_device(way),
        )

    def has_next(way):
        return place < count - 1 if way == 1 else place > 0

    def has_block(way, distance):
        return place - distance >= 0 if way == 1 else place + distance < count

    def begin(c, source):
        for way in (1, -1):
            pl.when(has_next(way))(lambda way=way: copy(way, 0, c, source).start())

    def forward(c, distance):
        for way in (1, -1):

            @pl.when(has_block(way, distance))
            def _(way=way):
                ref = piece(place - way * distance, c)
                arrived(
                    ref,
                    send.at[(way + 1) // 2, distance - 1, c],
                    recv.at[(way + 1) // 2, distance - 1, c],
                )
                if distance < count - 1:
                    pl.when(has_next(way))(lambda: copy(way, distance, c).start())

    def finish(source):
        for c in range(LINE_PARTS):
            for way in (1, -1):
                for distance in range(count - 1):

                    @pl.when(jnp.logical_and(has_next(way), has_block(way, distance)))
                    def _(way=way, distance=distance, c=c):
                        copy(way, distance, c, source(c) if distance == 0 else None).wait_send()

    return begin, forward, finish


def line_gather_task(source, target, own, send, recv):
    rows = source.shape[0]
    part = rows // LINE_PARTS
    count = lax.axis_size(EXPERT_AXIS)
    begin, forward, finish = line_gather_steps(target, send, recv, rows)
    local = pltpu.make_async_copy(source, target.at[lax.axis_index(EXPERT_AXIS)], own)
    for c in range(LINE_PARTS):
        begin(c, source.at[pl.ds(c * part, part)])
    local.start()
    yield 1
    for distance in range(1, count):
        for c in range(LINE_PARTS):
            forward(c, distance)
        yield 1
    local.wait()
    finish(lambda c: source.at[pl.ds(c * part, part)])


def line_semaphores():
    count = lax.axis_size(EXPERT_AXIS)
    return [pltpu.SemaphoreType.DMA((2, count, LINE_PARTS))] * 2


def line_reduce_steps(partial, inbox, send, recv):
    place, count = lax.axis_index(EXPERT_AXIS), lax.axis_size(EXPERT_AXIS)
    rows = partial.shape[1]
    part = rows // LINE_PARTS

    def span(c):
        return pl.ds(c * part, part)

    def box(way, distance, c):
        return inbox.at[distance if way == 1 else count - distance, span(c)]

    def copy(way, distance, c, source):
        side = (way + 1) // 2
        return remote(
            source,
            box(way, distance - 1, c),
            send.at[side, distance, c],
            recv.at[side, distance - 1, c],
            line_device(way),
        )

    def wait_inbox(way, distance, c):
        side = (way + 1) // 2
        arrived(box(way, distance, c), send.at[side, distance, c], recv.at[side, distance, c])

    def has_source(way):
        return place > 0 if way == 1 else place < count - 1

    def has_target(way, distance):
        return place + distance < count if way == 1 else place - distance >= 0

    def step(c, distance):
        for way in (1, -1):
            mine = partial.at[place + way * distance, span(c)]

            def pass_on(way=way, mine=mine):
                came = box(way, distance, c)
                wait_inbox(way, distance, c)
                came[...] = low(wide(mine[...]) + wide(came[...]))
                copy(way, distance, c, came).start()

            def send_first(way=way, mine=mine):
                copy(way, distance, c, mine).start()

            valid = has_target(way, distance)
            if distance < count - 1:
                pl.when(jnp.logical_and(valid, has_source(way)))(pass_on)
                pl.when(jnp.logical_and(valid, jnp.logical_not(has_source(way))))(send_first)
            else:
                pl.when(valid)(send_first)

    def total(c, result):
        result[span(c)] = result[span(c)] + wide(partial[place, span(c)])
        for way in (1, -1):

            @pl.when(has_source(way))
            def _(way=way):
                wait_inbox(way, 0, c)
                result[span(c)] = result[span(c)] + wide(box(way, 0, c)[...])

    def stages(result, done):
        for t in range(LINE_PARTS + count - 1):
            for c in range(LINE_PARTS):
                distance = count - 1 - (t - c)
                if 1 <= distance <= count - 1:
                    step(c, distance)
                elif distance == 0:
                    total(c, result)
                    done(span(c), c)
            yield 1

    def finish():
        for c in range(LINE_PARTS):
            for way in (1, -1):
                for distance in range(1, count):
                    pl.when(has_target(way, distance))(
                        lambda way=way, distance=distance, c=c: copy(
                            way, distance, c, partial.at[place + way * distance, span(c)]
                        ).wait_send()
                    )

    return stages, finish


def gather_semaphores():
    return [
        pltpu.SemaphoreType.DMA(()),
        pltpu.SemaphoreType.DMA((9,)),
        pltpu.SemaphoreType.DMA((9,)),
    ]


def kernel_params(number):
    return pltpu.CompilerParams(
        collective_id=number,
        has_side_effects=True,
        vmem_limit_bytes=(52 if lax.axis_size(EXPERT_AXIS) <= 4 else 60) << 20,
    )


def opening(tokens, gains, matrices):
    count = lax.axis_size(EXPERT_AXIS)
    rows, width = tokens.shape
    number = len(matrices)
    planes = lax.axis_size(PLANE)
    depth = gains.shape[1]

    def kernel(*refs):
        tokens_ref, gains_ref = refs[:2]
        sources = refs[2 : 2 + number]
        gains_all, normed_all = refs[2 + number : 4 + number]
        targets = refs[4 + number : 4 + 2 * number]
        scratch = list(refs[4 + 2 * number :])
        normed, gain_box, gain_send, gain_recv = scratch[:4]
        line = scratch[4:7]
        semaphores = scratch[7:]
        meet(range(1, planes), True)
        here = plane_here()
        sends = []
        for mask in range(1, planes):
            copy = remote(
                gains_ref,
                gain_box.at[here],
                gain_send.at[mask],
                gain_recv.at[mask],
                plane_device(mask),
            )
            copy.start()
            sends.append(copy)
        tasks = [
            plane_gather_task(sources[i], targets[i], *semaphores[3 * i : 3 * i + 3])
            for i in range(number)
        ]
        for task in tasks:
            next(task)
        for task in tasks:
            next(task)
        gain_box[here] = gains_ref[...]
        values = wide(tokens_ref[...])
        scale = lax.rsqrt(jnp.mean(values * values, axis=-1, keepdims=True) + epsilon)
        for mask in range(1, planes):
            other = gain_box.at[jnp.bitwise_xor(here, mask)]
            arrived(other, gain_send.at[mask], gain_recv.at[mask])
        for i in range(planes):
            columns = slice(i * depth, (i + 1) * depth)
            normed[:, columns] = low(
                wide(tokens_ref[:, columns]) * scale * gain_box[i, 0:1, :]
            )
        gains_all[...] = gain_box[...]
        rows_task = line_gather_task(normed, normed_all, *line)
        next(rows_task)
        next(rows_task)
        for task in tasks:
            next(task)
        for task in tasks:
            next(task)
        run_tasks(rows_task, *tasks)
        for copy in sends:
            copy.wait_send()

    shapes = [
        jax.ShapeDtypeStruct((planes,) + gains.shape, jnp.float32),
        jax.ShapeDtypeStruct((count, rows, width), jnp.bfloat16),
    ] + [jax.ShapeDtypeStruct((planes * m.shape[0], m.shape[1]), m.dtype) for m in matrices]
    scratch = [
        pltpu.VMEM((rows, width), jnp.bfloat16),
        pltpu.VMEM((planes,) + gains.shape, jnp.float32),
        pltpu.SemaphoreType.DMA((planes,)),
        pltpu.SemaphoreType.DMA((planes,)),
        pltpu.SemaphoreType.DMA(()),
    ]
    scratch += line_semaphores()
    for _ in matrices:
        scratch += gather_semaphores()
    results = pl.pallas_call(
        kernel,
        out_shape=shapes,
        in_specs=[INSIDE] * (2 + number),
        out_specs=[INSIDE, ANY] + [ANY] * number,
        scratch_shapes=scratch,
        compiler_params=kernel_params(1),
        cost_estimate=pl.CostEstimate(
            flops=60_000_000, bytes_accessed=150_000_000, transcendentals=0
        ),
        name="opening",
    )(tokens, gains, *matrices)
    return results[0], results[1], results[2:]


def middle_sum(partial, source, gain, matrices, experts, before):
    count, rows, width = partial.shape
    planes = lax.axis_size(PLANE)
    number, routed = len(matrices), len(experts)

    def kernel(*refs):
        position = 3 + number + routed + 1
        partial_ref, source_ref, gain_ref = refs[:3]
        sources = refs[3 : 3 + number]
        expert_refs = refs[3 + number : position - 1]
        middle_ref, hidden_all = refs[position : position + 2]
        targets = refs[position + 2 : position + 2 + number + routed]
        scratch = list(refs[position + 2 + number + routed :])
        inbox, hidden, reduce_send, reduce_recv, own, line_send, line_recv = scratch[:7]
        stages = scratch[7 : 7 + routed]
        semaphores = scratch[7 + routed :]
        meet((1, 2, 4, 6), True)
        reduce_stages, reduce_finish = line_reduce_steps(
            partial_ref, inbox, reduce_send, reduce_recv
        )
        begin, forward, finish = line_gather_steps(hidden_all, line_send, line_recv, rows)
        part = rows // LINE_PARTS

        def ready(span, c):
            values = middle_ref[span]
            scale = lax.rsqrt(jnp.mean(values * values, axis=-1, keepdims=True) + epsilon)
            hidden[span] = low(values * scale * gain_ref[...])
            begin(c, hidden.at[span])

        def line_task():
            middle_ref[...] = wide(source_ref[...])
            yield from reduce_stages(middle_ref, ready)
            local = pltpu.make_async_copy(hidden, hidden_all.at[lax.axis_index(EXPERT_AXIS)], own)
            local.start()
            for distance in range(1, count):
                for c in range(LINE_PARTS):
                    forward(c, distance)
                yield 1
            local.wait()
            finish(lambda c: hidden.at[pl.ds(c * part, part)])
            reduce_finish()

        tasks = [
            plane_gather_task(sources[i], targets[i], *semaphores[3 * i : 3 * i + 3])
            for i in range(number)
        ] + [
            expert_fetch_task(
                expert_refs[i],
                targets[number + i],
                stages[i],
                *semaphores[3 * (number + i) : 3 * (number + i) + 3],
            )
            for i in range(routed)
        ]
        for task in tasks:
            next(task)
        for task in tasks:
            next(task)
        run_tasks(line_task())
        run_tasks(*tasks)

    shapes = (
        [
            jax.ShapeDtypeStruct((rows, width), jnp.float32),
            jax.ShapeDtypeStruct((count, rows, width), jnp.bfloat16),
        ]
        + [jax.ShapeDtypeStruct((planes * m.shape[0], m.shape[1]), m.dtype) for m in matrices]
        + [jax.ShapeDtypeStruct((planes * e.shape[1], e.shape[2]), e.dtype) for e in experts]
    )
    scratch = [
        pltpu.VMEM((count + 1, rows, width), jnp.bfloat16),
        pltpu.VMEM((rows, width), jnp.bfloat16),
    ]
    scratch += line_semaphores() + [pltpu.SemaphoreType.DMA(())] + line_semaphores()
    scratch += [pltpu.VMEM(e.shape[1:], e.dtype) for e in experts]
    for _ in range(number + routed):
        scratch += gather_semaphores()
    results = pl.pallas_call(
        kernel,
        out_shape=shapes,
        in_specs=[INSIDE] * (3 + number) + [ANY] * (routed + 1),
        out_specs=[INSIDE] + [ANY] * (1 + number + routed),
        scratch_shapes=scratch,
        compiler_params=kernel_params(2),
        cost_estimate=pl.CostEstimate(
            flops=60_000_000, bytes_accessed=300_000_000, transcendentals=0
        ),
        name="middle_sum",
    )(partial, source, gain, *matrices, *experts, before)
    return results[0], results[1], results[2 : 2 + number], results[2 + number :]


def add_rows(target, first, second):
    def tile(i, carry):
        span = pl.ds(pl.multiple_of(i * 16, 16), 16)
        target[span] = (wide(first[span]) + wide(second[span])).astype(target.dtype)
        return carry

    lax.fori_loop(0, target.shape[0] // 16, tile, 0)


def expert_return_task(source, result, mine, came, load, send, recv):
    rows = mine.shape[1]
    here = plane_here()
    expert_own = here // 2

    def slot(mask):
        return source.at[pl.ds(pl.multiple_of(jnp.bitwise_xor(here, mask) * rows, 16), rows)]

    def go(number, source_ref, target_ref, mask):
        copy = remote(source_ref, target_ref, send.at[number], recv.at[number], plane_device(mask))
        copy.start()
        return copy

    copies, loads = [], {}

    def cross(k):
        copies.append(go(k, slot(2 * k + 1), came.at[k], 1))
        loads[k] = pltpu.make_async_copy(slot(2 * k), mine.at[k], load.at[k])
        loads[k].start()

    cross(3)
    yield 1
    for k, following in ((3, 1), (1, 2), (2, 0), (0, None)):
        if following is not None:
            cross(following)
        arrived(came.at[k], send.at[k], recv.at[k])
        loads[k].wait()
        add_rows(mine.at[k], mine.at[k], came.at[k])
        if k:
            copies.append(go(4 + k, mine.at[k], result.at[expert_own], 2 * k))
        else:
            local = pltpu.make_async_copy(mine.at[0], result.at[expert_own], load.at[0])
            local.start()
        yield 1
    for k in (3, 1, 2):
        arrived(
            result.at[jnp.bitwise_xor(expert_own, k)], send.at[4 + k], recv.at[4 + k]
        )
    local.wait()
    for copy in copies:
        copy.wait_send()


def expert_return_scratch(rows, columns):
    return [
        pltpu.VMEM((4, rows, columns), jnp.bfloat16),
        pltpu.VMEM((4, rows, columns), jnp.bfloat16),
        pltpu.SemaphoreType.DMA((4,)),
        pltpu.SemaphoreType.DMA((8,)),
        pltpu.SemaphoreType.DMA((8,)),
    ]


def plane_scatter_task(source, result, mine, came, box, last, load, send, recv):
    rows = mine.shape[1]
    half = rows // 2
    here = plane_here()
    upper, lower = pl.ds(0, half), pl.ds(half, half)

    def slot(mask):
        return source.at[pl.ds(pl.multiple_of(jnp.bitwise_xor(here, mask) * rows, 16), rows)]

    def go(number, source_ref, target_ref, mask):
        copy = remote(source_ref, target_ref, send.at[number], recv.at[number], plane_device(mask))
        copy.start()
        return copy

    def got(number, ref):
        arrived(ref, send.at[number], recv.at[number])

    copies, loads = [], {}

    def cross(k):
        copies.append(go(k, slot(2 * k + 1), came.at[k], 1))
        loads[k] = pltpu.make_async_copy(slot(2 * k), mine.at[k], load.at[k])
        loads[k].start()

    cross(3)
    yield 1
    for k, following in ((3, 1), (1, 2), (2, 0)):
        cross(following)
        got(k, came.at[k])
        loads[k].wait()
        add_rows(mine.at[k], mine.at[k], came.at[k])
        if k == 3:
            copies.append(go(4, mine.at[3, upper], box.at[0], 2))
            copies.append(go(5, mine.at[3, lower], box.at[1], 4))
        elif k == 1:
            copies.append(go(6, mine.at[1, upper], last.at[0, upper], 2))
        else:
            copies.append(go(7, mine.at[2, lower], last.at[1, lower], 4))
        yield 1
    got(4, box.at[0])
    add_rows(mine.at[2, upper], mine.at[2, upper], box.at[0])
    copies.append(go(8, mine.at[2, upper], last.at[1, upper], 4))
    yield 1
    got(5, box.at[1])
    add_rows(mine.at[1, lower], mine.at[1, lower], box.at[1])
    copies.append(go(9, mine.at[1, lower], last.at[0, lower], 2))
    yield 1
    got(0, came.at[0])
    loads[0].wait()
    add_rows(result, mine.at[0], came.at[0])
    got(6, last.at[0, upper])
    got(7, last.at[1, lower])
    yield 1
    got(9, last.at[0, lower])
    add_rows(result, result, last.at[0])
    got(8, last.at[1, upper])
    add_rows(result, result, last.at[1])
    for copy in copies:
        copy.wait_send()


def plane_scatter_scratch(rows, columns):
    return [
        pltpu.VMEM((4, rows, columns), jnp.bfloat16),
        pltpu.VMEM((4, rows, columns), jnp.bfloat16),
        pltpu.VMEM((2, rows // 2, columns), jnp.bfloat16),
        pltpu.VMEM((2, rows, columns), jnp.bfloat16),
        pltpu.SemaphoreType.DMA((4,)),
        pltpu.SemaphoreType.DMA((10,)),
        pltpu.SemaphoreType.DMA((10,)),
    ]


def norm_back(values, gain, grad):
    scale = lax.rsqrt(jnp.mean(values * values, axis=-1, keepdims=True) + epsilon)
    scaled = gain * grad
    mean = jnp.mean(values * scaled, axis=-1, keepdims=True)
    part = jnp.sum(values * scale * grad, axis=0, keepdims=True)
    return scale * scaled - values * (scale * scale * scale * mean), part


def branch_sum(partial, middle, gain, grad_out, experts, local_experts, later):
    count, rows, width = partial.shape
    planes = lax.axis_size(PLANE)
    routed, waiting = len(experts), len(later)

    def kernel(*refs):
        partial_ref, middle_ref, gain_ref, grad_ref = refs[:4]
        expert_refs = refs[4 : 4 + routed]
        outputs = refs[4 + routed + waiting :]
        grad_middle, grad_gain, branch_all = outputs[:3]
        results = outputs[3 : 3 + routed]
        scratch = list(outputs[3 + routed + waiting :])
        inbox, branch, reduce_send, reduce_recv, own, line_send, line_recv = scratch[:7]
        rest = scratch[7:]
        meet((1, 2, 4, 6), True)
        reduce_stages, reduce_finish = line_reduce_steps(
            partial_ref, inbox, reduce_send, reduce_recv
        )
        begin, forward, finish = line_gather_steps(branch_all, line_send, line_recv, rows)
        part = rows // LINE_PARTS

        def ready(span, c):
            back, gain_part = norm_back(middle_ref[span], gain_ref[...], grad_middle[span])
            grad_gain[...] = gain_part if c == 0 else grad_gain[...] + gain_part
            back = wide(grad_ref[span]) + back
            grad_middle[span] = back
            branch[span] = low(back)
            begin(c, branch.at[span])

        def line_task():
            grad_middle[...] = jnp.zeros((rows, width), jnp.float32)
            yield from reduce_stages(grad_middle, ready)
            local = pltpu.make_async_copy(branch, branch_all.at[lax.axis_index(EXPERT_AXIS)], own)
            local.start()
            for distance in range(1, count):
                for c in range(LINE_PARTS):
                    forward(c, distance)
                yield 1
            local.wait()
            finish(lambda c: branch.at[pl.ds(c * part, part)])
            reduce_finish()

        task_kind = plane_scatter_task if local_experts == 1 else expert_return_task
        size = len(rest) // routed
        tasks = [
            task_kind(
                expert_refs[i], results[i], *rest[size * i : size * (i + 1)]
            )
            for i in range(routed)
        ]
        line = line_task()
        for stage in range(5):
            for task in tasks:
                next(task)
            if stage:
                next(line)
        run_tasks(line)
        run_tasks(*tasks)

    shapes = [
        jax.ShapeDtypeStruct((rows, width), jnp.float32),
        jax.ShapeDtypeStruct((1, width), jnp.float32),
        jax.ShapeDtypeStruct((count, rows, width), jnp.bfloat16),
    ]
    scratch = [
        pltpu.VMEM((count + 1, rows, width), jnp.bfloat16),
        pltpu.VMEM((rows, width), jnp.bfloat16),
    ]
    scratch += line_semaphores() + [pltpu.SemaphoreType.DMA(())] + line_semaphores()
    for expert in experts:
        shard, columns = expert.shape[0] // planes, expert.shape[1]
        if local_experts == 1:
            shapes.append(jax.ShapeDtypeStruct((shard, columns), jnp.float32))
            scratch += plane_scatter_scratch(shard, columns)
        else:
            shapes.append(jax.ShapeDtypeStruct((local_experts, shard, columns), jnp.bfloat16))
            scratch += expert_return_scratch(shard, columns)
    shapes += [jax.ShapeDtypeStruct(x.shape, x.dtype) for x in later]
    results = pl.pallas_call(
        kernel,
        out_shape=shapes,
        in_specs=[INSIDE] * 4 + [ANY] * (routed + waiting),
        out_specs=[INSIDE, INSIDE, ANY]
        + [INSIDE if local_experts == 1 else ANY] * routed
        + [ANY] * waiting,
        input_output_aliases={4 + routed + i: 3 + routed + i for i in range(waiting)},
        scratch_shapes=scratch,
        compiler_params=kernel_params(3),
        cost_estimate=pl.CostEstimate(
            flops=60_000_000, bytes_accessed=300_000_000, transcendentals=0
        ),
        name="branch_sum",
    )(partial, middle, gain, grad_out, *experts, *later)
    grads = [
        wide(r).reshape((local_experts,) + r.shape[-2:]) for r in results[3 : 3 + routed]
    ]
    return results[0], results[1][0], results[2], grads, results[3 + routed :]


def meet_all():
    planes, count = lax.axis_size(PLANE), lax.axis_size(EXPERT_AXIS)
    for mask in range(1, planes):
        signal(plane_device(mask))
    for mask in range(1, count):
        signal({EXPERT_AXIS: jnp.bitwise_xor(lax.axis_index(EXPERT_AXIS), mask)})
    pl.semaphore_wait(pltpu.get_barrier_semaphore(), planes + count - 2)


def closing(partial, ready_before, source, gain, grad_middle, gain_grads, matrices, spread):
    count, rows, width = partial.shape
    planes = lax.axis_size(PLANE)
    number = len(matrices)
    depth = gain_grads.shape[2]
    shard, columns = matrices[0].shape[0] // planes, matrices[0].shape[1]
    thin = shard // count

    def kernel(*refs):
        partial_ref, _, source_ref, gain_ref, middle_ref, gains_ref = refs[:6]
        sources = refs[6 : 6 + number]
        grad_tokens, gains_out, thin_out = refs[6 + number : 9 + number]
        results = refs[9 + number : 9 + 2 * number]
        scratch = list(refs[9 + 2 * number :])
        inbox, reduce_send, reduce_recv, gain_row = scratch[:4]
        gain_part, gain_box, gain_send, gain_recv = scratch[4:8]
        gain_held, gain_far, far_send, far_recv, thin_box, thin_send, thin_recv = scratch[8:15]
        rest = scratch[15:]
        meet_all()
        place = lax.axis_index(EXPERT_AXIS)
        here = plane_here()
        reduce_stages, reduce_finish = line_reduce_steps(
            partial_ref, inbox, reduce_send, reduce_recv
        )

        def ready(span, c):
            back, row = norm_back(wide(source_ref[span]), gain_ref[...], grad_tokens[span])
            gain_row[...] = row if c == 0 else gain_row[...] + row
            grad_tokens[span] = middle_ref[span] + back

        def line_task():
            grad_tokens[...] = jnp.zeros((rows, width), jnp.float32)
            yield from reduce_stages(grad_tokens, ready)
            gain_part[...] = gains_ref[...]
            for i in range(planes):
                gain_part[i, 0:1, :] = gain_row[:, i * depth : (i + 1) * depth]
            copies = []
            for mask in range(1, planes):
                copy = remote(
                    gain_part.at[jnp.bitwise_xor(here, mask)],
                    gain_box.at[mask],
                    gain_send.at[mask],
                    gain_recv.at[mask],
                    plane_device(mask),
                )
                copy.start()
                copies.append(copy)
            gain_total = gain_part[here]
            yield 1
            for mask in range(1, planes):
                arrived(gain_box.at[mask], gain_send.at[mask], gain_recv.at[mask])
                gain_total = gain_total + gain_box[mask]
            gain_held[...] = gain_total
            for mask in range(1, count):
                copy = remote(
                    gain_held,
                    gain_far.at[mask],
                    far_send.at[mask],
                    far_recv.at[mask],
                    {EXPERT_AXIS: jnp.bitwise_xor(place, mask)},
                )
                copy.start()
                copies.append(copy)
            yield 1
            for mask in range(1, count):
                arrived(gain_far.at[mask], far_send.at[mask], far_recv.at[mask])
                gain_total = gain_total + gain_far[mask]
            gains_out[...] = gain_total
            for copy in copies:
                copy.wait_send()
            reduce_finish()

        def first_task(task):
            yield from task
            copies = []

            def piece(mask):
                start = pl.multiple_of(jnp.bitwise_xor(place, mask) * thin, 8 if thin % 8 == 0 else thin)
                return results[0].at[pl.ds(start, thin), pl.ds(spread, columns - spread)]

            for mask in range(1, count):
                copy = remote(
                    piece(mask),
                    thin_box.at[mask],
                    thin_send.at[mask],
                    thin_recv.at[mask],
                    {EXPERT_AXIS: jnp.bitwise_xor(place, mask)},
                )
                copy.start()
                copies.append(copy)
            yield 1
            total = piece(0)[...]
            for mask in range(1, count):
                arrived(thin_box.at[mask], thin_send.at[mask], thin_recv.at[mask])
                total = total + thin_box[mask]
            thin_out[...] = total
            for copy in copies:
                copy.wait_send()

        size = len(rest) // number
        tasks = [
            plane_scatter_task(sources[i], results[i], *rest[size * i : size * (i + 1)])
            for i in range(number)
        ]
        tasks[0] = first_task(tasks[0])
        line = line_task()
        for stage in range(6):
            for task in tasks:
                next(task)
            if stage:
                next(line)
        run_tasks(line, *tasks)

    shapes = [
        jax.ShapeDtypeStruct((rows, width), jnp.float32),
        jax.ShapeDtypeStruct(gain_grads.shape[1:], jnp.float32),
        jax.ShapeDtypeStruct((thin, columns - spread), jnp.float32),
    ] + [jax.ShapeDtypeStruct((m.shape[0] // planes, m.shape[1]), jnp.float32) for m in matrices]
    scratch = [pltpu.VMEM((count + 1, rows, width), jnp.bfloat16)]
    scratch += line_semaphores()
    scratch += [
        pltpu.VMEM((1, width), jnp.float32),
        pltpu.VMEM(gain_grads.shape, jnp.float32),
        pltpu.VMEM(gain_grads.shape, jnp.float32),
        pltpu.SemaphoreType.DMA((planes,)),
        pltpu.SemaphoreType.DMA((planes,)),
        pltpu.VMEM(gain_grads.shape[1:], jnp.float32),
        pltpu.VMEM((count,) + gain_grads.shape[1:], jnp.float32),
        pltpu.SemaphoreType.DMA((count,)),
        pltpu.SemaphoreType.DMA((count,)),
        pltpu.VMEM((count, thin, columns - spread), jnp.float32),
        pltpu.SemaphoreType.DMA((count,)),
        pltpu.SemaphoreType.DMA((count,)),
    ]
    for m in matrices:
        scratch += plane_scatter_scratch(m.shape[0] // planes, m.shape[1])
    results = pl.pallas_call(
        kernel,
        out_shape=shapes,
        in_specs=[INSIDE, ANY] + [INSIDE] * 4 + [ANY] * number,
        out_specs=[INSIDE] * (3 + number),
        scratch_shapes=scratch,
        compiler_params=kernel_params(4),
        cost_estimate=pl.CostEstimate(
            flops=60_000_000, bytes_accessed=200_000_000, transcendentals=0
        ),
        name="closing",
    )(partial, ready_before, source, gain, grad_middle, gain_grads, *matrices)
    return results[:3], results[3:]


def silu_back(gate, up, grad):
    sigmoid_part = 1.0 / (1.0 + jnp.exp(-gate))
    silu_part = gate * sigmoid_part
    slope = sigmoid_part * (1.0 + gate * (1.0 - sigmoid_part))
    return silu_part * up, grad * up * slope, grad * silu_part


def row_copies(source, target, send, recv, copies):
    return [
        remote(source(k), target(k), send.at[k], recv.at[k], plane_device(k * copies))
        for k in (3, 1, 2)
    ]


def shared_and_rows(hidden, grads, weights, hidden_slots, grad_slots, gates, copies):
    tokens, width = hidden.shape
    columns = weights.shape[1] // 3
    pieces, slots = hidden_slots.shape[:2]
    exchanged = copies > 0
    tall = max(t for t in (256, 128, tokens) if tokens % t == 0)
    wide_part = 256

    def kernel(*refs):
        hidden_any, grads_any, weights_any, rows_any, grad_rows_any, gates_ref = refs[:6]
        act_out, back_out, weight_grads = refs[6:9]
        outputs = refs[9:12]
        scratch = refs[12:] if exchanged else refs[9:]
        hid, grd, wts, both, load = scratch[:5]
        loads = [
            pltpu.make_async_copy(hidden_any, hid, load.at[0]),
            pltpu.make_async_copy(weights_any, wts, load.at[1]),
            pltpu.make_async_copy(grads_any, grd, load.at[2]),
        ]
        moves = []
        if exchanged:
            semaphores = scratch[5:]
            meet([k * copies for k in (1, 2, 3)], False)
            for i, source in enumerate((gates_ref, rows_any, grad_rows_any)):
                moves += row_copies(
                    lambda k, source=source: source.at[k],
                    lambda k, i=i: outputs[i].at[k - 1],
                    semaphores[2 * i],
                    semaphores[2 * i + 1],
                    copies,
                )
            for move in moves:
                move.start()
        for copy in loads:
            copy.start()
        for copy in loads:
            copy.wait()

        def rows_tile(i, carry):
            span = pl.ds(pl.multiple_of(i * tall, 16), tall)
            gate = product(hid[span], wts[:, :columns])
            up = product(hid[span], wts[:, columns : 2 * columns])
            grad = product(grd[span], wts[:, 2 * columns :])
            act, dgate, dup = silu_back(gate, up, grad)
            act_out[span] = low(act)
            both[span, :columns] = low(dgate)
            both[span, columns:] = low(dup)
            back_out[span] = product_right(both[span], wts[:, : 2 * columns])
            return carry

        lax.fori_loop(0, tokens // tall, rows_tile, 0)

        def weights_tile(i, carry):
            span = pl.ds(pl.multiple_of(i * wide_part, wide_part), wide_part)
            weight_grads[span, : 2 * columns] = low(product_left(hid[:, span], both[...]))
            weight_grads[span, 2 * columns :] = low(product_left(grd[:, span], act_out[...]))
            return carry

        lax.fori_loop(0, width // wide_part, weights_tile, 0)
        for move in moves:
            move.wait()

    shapes = [
        jax.ShapeDtypeStruct((tokens, columns), jnp.bfloat16),
        jax.ShapeDtypeStruct((tokens, width), jnp.float32),
        jax.ShapeDtypeStruct(weights.shape, jnp.bfloat16),
    ]
    out_specs = [INSIDE] * 3
    scratch = [
        pltpu.VMEM(hidden.shape, jnp.bfloat16),
        pltpu.VMEM(grads.shape, jnp.bfloat16),
        pltpu.VMEM(weights.shape, jnp.bfloat16),
        pltpu.VMEM((tokens, 2 * columns), jnp.bfloat16),
        pltpu.SemaphoreType.DMA((3,)),
    ]
    if exchanged:
        shapes += [jax.ShapeDtypeStruct((3,) + x.shape[1:], x.dtype) for x in (gates, hidden_slots, grad_slots)]
        out_specs += [INSIDE, ANY, ANY]
        scratch += [pltpu.SemaphoreType.DMA((4,))] * 6
    results = pl.pallas_call(
        kernel,
        out_shape=shapes,
        in_specs=[ANY] * 5 + [INSIDE],
        out_specs=out_specs,
        scratch_shapes=scratch,
        compiler_params=kernel_params(5) if exchanged else pltpu.CompilerParams(vmem_limit_bytes=60 << 20),
        cost_estimate=pl.CostEstimate(
            flops=12 * tokens * width * columns, bytes_accessed=120_000_000, transcendentals=0
        ),
        name="shared_and_rows",
    )(hidden, grads, weights, hidden_slots, grad_slots, gates)
    return results[:3], results[3:]


def routed_expert(hidden_slots, grad_slots, hidden_far, grad_far, gates, weights, copies):
    slots, width = hidden_slots.shape[1:]
    gate_full, up_full, down_full = weights
    units = gate_full.shape[1]
    exchanged = copies > 0

    def kernel(*refs):
        far = 2 if exchanged else 0
        hidden_any, grad_any = refs[:2]
        hidden_far_any, grad_far_any = refs[2:4] if exchanged else (None, None)
        gates_ref, wg_any, wu_any, wd_any = refs[2 + far : 6 + far]
        pair_back, result_back, scale_back, dwg, dwu, dwd = refs[6 + far : 12 + far]
        scratch = refs[12 + far :]
        wg, wu, wd, hid, grd, act, dgate, dup, pair, result, scale = scratch[:11]
        tile_up, tile_down, load, own, store = scratch[11:16]
        semaphores = scratch[16:]

        def piece(ref, ref_far, k):
            return ref.at[k] if k == 0 or not exchanged else ref_far.at[k - 1]

        if exchanged:
            meet([k * copies for k in (1, 2, 3)], False)
        loads = {}

        def fetch(number, source, target):
            loads[number] = pltpu.make_async_copy(source, target, load.at[number])
            loads[number].start()

        fetch(0, wg_any, wg)
        for k in range(4):
            fetch(3 + k, piece(hidden_any, hidden_far_any, k), hid.at[pl.ds(k * slots, slots)])
        fetch(1, wu_any, wu)
        fetch(2, wd_any, wd)
        for k in range(4):
            fetch(7 + k, piece(grad_any, grad_far_any, k), grd.at[pl.ds(k * slots, slots)])
        for number in (0, 3, 4, 5, 6, 1, 2, 7, 8, 9, 10):
            loads[number].wait()

        def back(k, which):
            source, target = ((pair, pair_back), (result, result_back), (scale, scale_back))[which]
            return remote(
                source.at[k],
                target.at[k],
                semaphores[2 * which].at[k],
                semaphores[2 * which + 1].at[k],
                plane_device(k * copies),
            )

        def deliver(k, which):
            if exchanged:
                pl.when(k > 0)(lambda: back(k, which).start())

        def first(i, carry):
            k = 3 - i
            span = pl.ds(pl.multiple_of(k * slots, 16), slots)
            gate = product(hid[span], wg[...])
            up = product(hid[span], wu[...])
            grad = product_right(grd[span], wd[...])
            gates_here = gates_ref[span]
            act_part, dgate_part, dup_part = silu_back(gate, up, grad)
            scale[k] = jnp.broadcast_to(
                jnp.sum(act_part * grad, axis=-1, keepdims=True), scale.shape[1:]
            )
            act[span] = low(act_part * gates_here)
            dgate[span] = low(dgate_part * gates_here)
            dup[span] = low(dup_part * gates_here)
            pair[k] = low(product_right(dgate[span], wg[...]) + product_right(dup[span], wu[...]))
            deliver(k, 0)
            deliver(k, 2)
            return carry

        lax.fori_loop(0, 4, first, 0)

        def second(i, carry):
            k = 3 - i
            span = pl.ds(pl.multiple_of(k * slots, 16), slots)
            result[k] = low(product(act[span], wd[...]))
            deliver(k, 1)
            return carry

        lax.fori_loop(0, 4, second, 0)
        kept = []
        for which, (source, target) in enumerate(
            ((pair, pair_back), (result, result_back), (scale, scale_back))
        ):
            for k in range(1 if exchanged else 4):
                copy = pltpu.make_async_copy(source.at[k], target.at[k], own.at[which, k])
                copy.start()
                kept.append(copy)

        def tiles(count, rows, buffer, target, compute):
            def put(i, slot):
                start = pl.multiple_of(i * rows, 16)
                return pltpu.make_async_copy(
                    buffer.at[slot], target.at[pl.ds(start, rows)], store.at[slot]
                )

            def tile(i, carry):
                slot = lax.rem(i, 2)
                pl.when(i >= 2)(lambda: put(i - 2, slot).wait())
                buffer[slot] = compute(pl.ds(pl.multiple_of(i * rows, rows), rows))
                put(i, slot).start()
                return carry

            lax.fori_loop(0, count, tile, 0)
            for i in (count - 2, count - 1):
                put(i, i % 2).wait()

        tiles(width // 256, 256, tile_up, dwg, lambda s: low(product_left(hid[:, s], dgate[...])))
        tiles(width // 256, 256, tile_up, dwu, lambda s: low(product_left(hid[:, s], dup[...])))
        tiles(units // 128, 128, tile_down, dwd, lambda s: low(product_left(act[:, s], grd[...])))
        for copy in kept:
            copy.wait()
        if exchanged:
            for which in (0, 2, 1):
                for k in (3, 2, 1):
                    back(k, which).wait()

    shapes = [
        jax.ShapeDtypeStruct((4, slots, width), jnp.bfloat16),
        jax.ShapeDtypeStruct((4, slots, width), jnp.bfloat16),
        jax.ShapeDtypeStruct((4, slots, 128), jnp.float32),
    ] + [jax.ShapeDtypeStruct(w.shape, jnp.bfloat16) for w in weights]
    rows = 4 * slots
    scratch = [pltpu.VMEM(w.shape, jnp.bfloat16) for w in weights]
    scratch += [pltpu.VMEM((rows, width), jnp.bfloat16)] * 2
    scratch += [pltpu.VMEM((rows, units), jnp.bfloat16)] * 3
    scratch += [pltpu.VMEM((4, slots, width), jnp.bfloat16)] * 2
    scratch += [pltpu.VMEM((4, slots, 128), jnp.float32)]
    scratch += [
        pltpu.VMEM((2, 256, units), jnp.bfloat16),
        pltpu.VMEM((2, 128, width), jnp.bfloat16),
        pltpu.SemaphoreType.DMA((11,)),
        pltpu.SemaphoreType.DMA((3, 4)),
        pltpu.SemaphoreType.DMA((2,)),
    ]
    if exchanged:
        scratch += [pltpu.SemaphoreType.DMA((4,))] * 6
    operands = [hidden_slots, grad_slots] + ([hidden_far, grad_far] if exchanged else [])
    results = pl.pallas_call(
        kernel,
        out_shape=shapes,
        in_specs=[ANY] * len(operands) + [INSIDE] + [ANY] * 3,
        out_specs=[ANY] * 6,
        scratch_shapes=scratch,
        compiler_params=pltpu.CompilerParams(
            collective_id=6, has_side_effects=True, vmem_limit_bytes=60 << 20
        )
        if exchanged
        else pltpu.CompilerParams(vmem_limit_bytes=60 << 20),
        cost_estimate=pl.CostEstimate(
            flops=18 * rows * units * width, bytes_accessed=200_000_000, transcendentals=0
        ),
        name="routed_expert",
    )(*operands, gates, *weights)
    return results


def body(
    tokens,
    routes,
    grad_out,
    attn_gain,
    query_weight,
    latent_down,
    latent_gain,
    latent_up,
    out_weight,
    ffn_gain,
    router_weight,
    shared_gate,
    shared_up,
    shared_down,
    expert_gate,
    expert_up,
    expert_down,
):
    contexts = lax.axis_size(CONTEXT_AXIS)
    context_index = lax.axis_index(CONTEXT_AXIS)
    groups_local = lax.axis_size(EXPERT_AXIS)
    expert_index = lax.axis_index(EXPERT_AXIS)
    plane_count = lax.axis_size(PLANE)
    plane_index = lax.axis_index(PLANE)
    local_experts = expert_gate.shape[0]
    experts_all = router_weight.shape[1]
    copies = plane_count // local_experts
    expert_own = plane_index // copies
    query_cols = query_weight.shape[1]
    heads_local = query_cols // (NOPE + ROPE)
    down_cols = LATENT + ROPE
    shard_rows = query_weight.shape[0]
    latent_rows = latent_up.shape[0]
    prompt_len = PROMPT_DEV * contexts
    capacity = (TOK_DEV * TOPK * 9 + 8 * experts_all - 1) // (8 * experts_all)
    slots = groups_local * capacity
    slots = -(-slots // 16) * 16 if local_experts > 1 else -(-slots // 64) * 64
    token_count = groups_local * TOK_DEV
    score_scale = (NOPE + ROPE) ** (-0.5)

    used_cols = query_cols + down_cols
    extra_cols = experts_all + 3
    pad_cols = -(used_cols + extra_cols) % 128
    gains = jnp.stack(
        [
            wide(attn_gain),
            wide(ffn_gain),
            jnp.pad(wide(latent_gain), (0, shard_rows - latent_gain.shape[0])),
        ]
        + [jnp.zeros((shard_rows,), jnp.float32)] * 5
    )
    first_local = jnp.concatenate(
        [
            query_weight,
            latent_down,
            router_weight,
            jnp.zeros((shard_rows, 3 + pad_cols), jnp.bfloat16),
        ],
        axis=1,
    )
    gains_all, normed_all, (first_full, up_local, out_local) = opening(
        tokens[0], gains, [first_local, latent_up, out_weight.T]
    )
    full_router = first_full[:, used_cols : used_cols + experts_all]
    full_attn_gain = gains_all[:, 0].reshape(D)
    full_ffn_gain = gains_all[:, 1].reshape(D)
    full_latent_gain = gains_all[:, 2, : latent_gain.shape[0]].reshape(LATENT)

    within = jnp.arange(TOK_DEV, dtype=jnp.int32)
    query_places = jnp.where(
        within < PROMPT_DEV, context_index * PROMPT_DEV + within, prompt_len + within - PROMPT_DEV
    )
    key_places = jnp.arange(prompt_len + CONT_LEN, dtype=jnp.int32)
    allowed = key_places[None, :] <= query_places[:, None]
    cosine, sine_part = rotary_tables(query_places.astype(jnp.float32), ROPE // 2)
    cosine_heads = cosine[None, :, None, :]
    sine_heads = sine_part[None, :, None, :]
    source = wide(tokens[0])

    def pack_latent(comp_rows, latent_scale):
        return jnp.concatenate(
            [
                norm_rows(comp_rows[..., :LATENT], latent_scale),
                rotate(comp_rows[..., LATENT:], cosine[None], sine_part[None]),
            ],
            axis=-1,
        )

    grad_own, routes_own, _ = lax.optimization_barrier((grad_out[0], routes[0], gains_all))
    grad_all = axis_gather(grad_own, EXPERT_AXIS)
    routes_all = axis_gather(routes_own, EXPERT_AXIS)
    first_product = product(normed_all, first_full)
    compressed = first_product[..., query_cols:used_cols]
    packed = low(pack_latent(compressed, wide(full_latent_gain)))
    prompt_keys = axis_gather(packed[:, :PROMPT_DEV], CONTEXT_AXIS)
    cont_keys = packed[:, PROMPT_DEV:]
    query_raw = first_product[..., :query_cols].reshape(
        groups_local, TOK_DEV, heads_local, NOPE + ROPE
    )
    query_rows = low(
        jnp.concatenate(
            [query_raw[..., :NOPE], rotate(query_raw[..., NOPE:], cosine_heads, sine_heads)], axis=-1
        )
    )
    query_nope = query_rows[..., :NOPE]
    query_rope = query_rows[..., NOPE:]
    prompt_latent = prompt_keys[..., :LATENT]
    prompt_rope = prompt_keys[..., LATENT:]
    cont_latent = cont_keys[..., :LATENT]
    cont_rope = cont_keys[..., LATENT:]
    prompt_exp = low(product(prompt_latent, up_local)).reshape(
        contexts, groups_local, PROMPT_DEV, heads_local, NOPE + VDIM
    )
    cont_exp = low(product(cont_latent, up_local)).reshape(
        groups_local, CONT_LEN, heads_local, NOPE + VDIM
    )
    prompt_knope = prompt_exp[..., :NOPE]
    prompt_values = prompt_exp[..., NOPE:]
    cont_knope = cont_exp[..., :NOPE]
    cont_values = cont_exp[..., NOPE:]

    def split_keys(values):
        return (
            values[..., :prompt_len].reshape(
                groups_local, heads_local, TOK_DEV, contexts, PROMPT_DEV
            ),
            values[..., prompt_len:],
        )

    def score_all():
        prompt_part = jnp.einsum(
            "gqhd,cgphd->ghqcp", query_nope, prompt_knope, preferred_element_type=jnp.float32
        )
        prompt_part = prompt_part + jnp.einsum(
            "gqhd,cgpd->ghqcp", query_rope, prompt_rope, preferred_element_type=jnp.float32
        )
        prompt_part = prompt_part.reshape(groups_local, heads_local, TOK_DEV, prompt_len)
        cont_part = jnp.einsum(
            "gqhd,gphd->ghqp", query_nope, cont_knope, preferred_element_type=jnp.float32
        )
        cont_part = cont_part + jnp.einsum(
            "gqhd,gpd->ghqp", query_rope, cont_rope, preferred_element_type=jnp.float32
        )
        raw_scores = jnp.concatenate([prompt_part, cont_part], axis=-1)
        return jnp.where(allowed, raw_scores * score_scale, -1e30)

    scores = score_all()
    top_score = jnp.max(scores, axis=-1, keepdims=True)
    exp_scores = jnp.exp(scores - top_score)
    totals = jnp.sum(exp_scores, axis=-1, keepdims=True)
    probs_all = exp_scores / totals
    probs_low = low(probs_all)
    probs_prompt, probs_cont = split_keys(probs_low)
    mixed_rows = jnp.einsum(
        "ghqcp,cgphd->gqhd", probs_prompt, prompt_values, preferred_element_type=jnp.float32
    )
    mixed_rows = mixed_rows + jnp.einsum(
        "ghqp,gphd->gqhd", probs_cont, cont_values, preferred_element_type=jnp.float32
    )
    mixed_all = low(mixed_rows.reshape(groups_local, TOK_DEV, heads_local * VDIM))
    partial_sum = against_rows(mixed_all, out_local)
    shared_cols = shared_gate.shape[1]
    shared_pad = -(-shared_cols // 128) * 128

    def padded(weight):
        return jnp.pad(weight, ((0, 0), (0, shared_pad - shared_cols)))

    shared_own, _ = lax.optimization_barrier(
        (
            jnp.concatenate(
                [padded(shared_gate), padded(shared_up), padded(shared_down.T)], axis=1
            ),
            gains_all,
        )
    )
    shared_whole = lax.all_gather(shared_own, PLANE, axis=0, tiled=True)
    grad_flat = grad_all.reshape(token_count, D)
    slot_experts = expert_index * local_experts + (
        expert_own ^ jnp.arange(local_experts, dtype=jnp.int32)
    )
    expert_cols = jnp.arange(experts_all, dtype=jnp.int32)[:, None] == slot_experts[None, :]
    chosen_slots = jnp.any(routes_all[..., None] == slot_experts, axis=2)
    before = (within[:, None] > within[None, :]).astype(jnp.bfloat16)
    rank = jnp.einsum(
        "ts,gsl->gtl",
        before,
        chosen_slots.astype(jnp.bfloat16),
        preferred_element_type=jnp.float32,
    ).astype(jnp.int32)
    slot_of = jnp.where(
        chosen_slots,
        rank + capacity * jnp.arange(groups_local, dtype=jnp.int32)[:, None, None],
        -1,
    ).reshape(token_count, local_experts)
    picked = (
        slot_of.T[:, None, :] == jnp.arange(slots, dtype=jnp.int32)[None, :, None]
    )
    picked_low = picked.astype(jnp.bfloat16).reshape(local_experts * slots, token_count)
    piece_slots = slots * local_experts // 4
    grad_slots = low(product(picked_low, grad_flat)).reshape(4, piece_slots, D)
    middle, hidden_all, _, (gate_full, up_full, down_full) = middle_sum(
        low(partial_sum),
        tokens[0],
        full_ffn_gain[None],
        [],
        [expert_gate, expert_up, expert_down],
        grad_slots,
    )
    hidden_flat = hidden_all.reshape(token_count, D)

    hidden_slots = low(product(picked_low, hidden_flat)).reshape(4, piece_slots, D)
    logits = product(hidden_flat, full_router)
    expert_probs = jax.nn.softmax(logits, axis=-1)
    gate_tokens = jnp.sum(jnp.where(expert_cols[None], expert_probs[:, :, None], 0.0), axis=1)
    gate_slots = jnp.sum(jnp.where(picked, gate_tokens.T[:, None, :], 0.0), axis=-1)
    gate_slots = gate_slots.reshape(4, piece_slots)
    gates_padded = jnp.broadcast_to(
        jnp.pad(gate_slots, ((0, 0), (0, -piece_slots % 128)))[:, None], (4, 8, -(-piece_slots // 128) * 128)
    )
    row_hops = copies if local_experts > 1 else 0
    (act_shared, shared_hidden, shared_grads), far = shared_and_rows(
        hidden_flat, grad_flat, shared_whole, hidden_slots, grad_slots, gates_padded, row_hops
    )
    gates_far, hidden_far, grad_far = far if far else (None, None, None)
    if far:
        gate_slots = jnp.concatenate([gate_slots[:1], gates_far[:, 0, :piece_slots]], axis=0)
    pair_back, result, scale_back, *expert_partials = routed_expert(
        hidden_slots,
        grad_slots,
        hidden_far,
        grad_far,
        gate_slots.reshape(-1, 1),
        [gate_full, up_full, down_full],
        row_hops,
    )
    grad_gate_back = scale_back[:, :, 0].reshape(local_experts, slots)
    grad_routed = product_left(picked_low, pair_back.reshape(-1, D))
    grad_gate_tokens = jnp.sum(jnp.where(picked, grad_gate_back[:, :, None], 0.0), axis=1).T
    grad_spread = jnp.sum(
        jnp.where(expert_cols[None], grad_gate_tokens[:, None, :], 0.0), axis=-1
    )
    weighted = jnp.sum(expert_probs * grad_spread, axis=-1, keepdims=True)
    grad_logits = expert_probs * (grad_spread - weighted)
    grad_router = lax.dot_general(
        grad_logits,
        wide(hidden_flat),
        (((0,), (0,)), ((), ())),
        precision=lax.Precision.HIGHEST,
    )
    grad_from_router = lax.dot_general(
        grad_logits,
        wide(full_router),
        (((1,), (1,)), ((), ())),
        precision=lax.Precision.HIGHEST,
    )
    grad_hidden_part = low(
        shared_hidden + grad_routed + grad_from_router
    )
    grad_middle, grad_ffn_gain, branch_all, expert_grads, (result, shared_grads) = branch_sum(
        grad_hidden_part.reshape(groups_local, TOK_DEV, D),
        middle,
        full_ffn_gain[None],
        grad_out[0],
        expert_partials,
        local_experts,
        [result.reshape(-1, D), shared_grads],
    )
    shared_grads = wide(lax.psum_scatter(shared_grads, PLANE, scatter_dimension=0, tiled=True))
    routed_term = product_left(picked_low, result)
    branch_out = low(
        product_right(act_shared, shared_whole[:, 2 * shared_pad :]) + routed_term
    )
    grad_out_weight = low(
        product_left(
            branch_all.reshape(token_count, D), mixed_all.reshape(token_count, heads_local * VDIM)
        )
    )
    grad_mixed = low(product(branch_all, out_local)).reshape(
        groups_local, TOK_DEV, heads_local, VDIM
    )
    grad_probs_prompt = jnp.einsum(
        "gqhd,cgphd->ghqcp", grad_mixed, prompt_values, preferred_element_type=jnp.float32
    )
    grad_probs_cont = jnp.einsum(
        "gqhd,gphd->ghqp", grad_mixed, cont_values, preferred_element_type=jnp.float32
    )
    grad_probs = jnp.concatenate(
        [
            grad_probs_prompt.reshape(groups_local, heads_local, TOK_DEV, prompt_len),
            grad_probs_cont,
        ],
        axis=-1,
    )
    delta_rows = jnp.sum(probs_all * grad_probs, axis=-1, keepdims=True)
    grad_raw = low(probs_all * (grad_probs - delta_rows) * score_scale)
    raw_prompt, raw_cont = split_keys(grad_raw)
    value_prompt = jnp.einsum(
        "ghqcp,gqhd->cgphd", probs_prompt, grad_mixed, preferred_element_type=jnp.float32
    )
    value_cont = jnp.einsum(
        "ghqp,gqhd->gphd", probs_cont, grad_mixed, preferred_element_type=jnp.float32
    )
    knope_prompt = jnp.einsum(
        "ghqcp,gqhd->cgphd", raw_prompt, query_nope, preferred_element_type=jnp.float32
    )
    knope_cont = jnp.einsum(
        "ghqp,gqhd->gphd", raw_cont, query_nope, preferred_element_type=jnp.float32
    )
    krope_prompt = jnp.einsum(
        "ghqcp,gqhd->cgpd", raw_prompt, query_rope, preferred_element_type=jnp.float32
    )
    krope_cont = jnp.einsum(
        "ghqp,gqhd->gpd", raw_cont, query_rope, preferred_element_type=jnp.float32
    )
    grad_query_nope = jnp.einsum(
        "ghqcp,cgphd->gqhd", raw_prompt, prompt_knope, preferred_element_type=jnp.float32
    )
    grad_query_nope = grad_query_nope + jnp.einsum(
        "ghqp,gphd->gqhd", raw_cont, cont_knope, preferred_element_type=jnp.float32
    )
    grad_query_rope = jnp.einsum(
        "ghqcp,cgpd->gqhd", raw_prompt, prompt_rope, preferred_element_type=jnp.float32
    )
    grad_query_rope = grad_query_rope + jnp.einsum(
        "ghqp,gpd->gqhd", raw_cont, cont_rope, preferred_element_type=jnp.float32
    )
    grad_query_raw = jnp.concatenate(
        [grad_query_nope, rotate(grad_query_rope, cosine_heads, -sine_heads)], axis=-1
    )
    grad_query_raw = low(
        grad_query_raw.reshape(groups_local, TOK_DEV, heads_local * (NOPE + ROPE))
    )
    grad_exp_prompt = low(
        jnp.concatenate([knope_prompt, value_prompt], axis=-1).reshape(
            contexts, groups_local, PROMPT_DEV, heads_local * (NOPE + VDIM)
        )
    )
    grad_exp_cont = low(
        jnp.concatenate([knope_cont, value_cont], axis=-1).reshape(
            groups_local, CONT_LEN, heads_local * (NOPE + VDIM)
        )
    )
    latent_prompt = jnp.einsum(
        "cgpf,lf->cgpl", grad_exp_prompt, up_local, preferred_element_type=jnp.float32
    )
    latent_cont = jnp.einsum(
        "gpf,lf->gpl", grad_exp_cont, up_local, preferred_element_type=jnp.float32
    )
    grad_prompt_keys = jnp.concatenate([latent_prompt, krope_prompt], axis=-1)
    grad_cont_keys = jnp.concatenate([latent_cont, krope_cont], axis=-1)
    prompt_sum = axis_scatter(grad_prompt_keys, CONTEXT_AXIS)
    grad_packed = jnp.concatenate([prompt_sum, grad_cont_keys], axis=1)
    _, pack_back = jax.vjp(pack_latent, compressed, wide(full_latent_gain))
    grad_compressed, grad_latent_gain = pack_back(grad_packed)
    grad_first = jnp.concatenate(
        [
            grad_query_raw,
            low(grad_compressed),
            jnp.zeros((groups_local, TOK_DEV, first_full.shape[1] - used_cols), jnp.bfloat16),
        ],
        axis=-1,
    )
    grad_normed_part = low(against_rows(grad_first, first_full))

    grad_latent_up = jnp.einsum(
        "cgpl,cgpf->lf", prompt_latent, grad_exp_prompt, preferred_element_type=jnp.float32
    )
    grad_latent_up = grad_latent_up + jnp.einsum(
        "gpl,gpf->lf", cont_latent, grad_exp_cont, preferred_element_type=jnp.float32
    )
    first_back = product_left(
        normed_all.reshape(token_count, D), grad_first.reshape(token_count, first_full.shape[1])
    )
    gain_rows = jnp.concatenate(
        [
            jnp.zeros((plane_count, 1, shard_rows), jnp.float32),
            grad_ffn_gain.reshape(plane_count, 1, shard_rows),
            jnp.pad(
                grad_latent_gain.reshape(plane_count, 1, latent_rows),
                ((0, 0), (0, 0), (0, shard_rows - latent_rows)),
            ),
            grad_router.reshape(experts_all, plane_count, shard_rows).transpose(1, 0, 2),
            jnp.zeros((plane_count, -(3 + experts_all) % 8, shard_rows), jnp.float32),
        ],
        axis=1,
    )
    block_out = low(
        middle + axis_scatter(branch_out.reshape(groups_local, TOK_DEV, D), EXPERT_AXIS)
    )
    (grad_tokens, gain_sum, down_own), sums = closing(
        grad_normed_part,
        block_out,
        tokens[0],
        full_attn_gain[None],
        grad_middle,
        gain_rows,
        [low(first_back), low(grad_latent_up), grad_out_weight],
        query_cols // 128 * 128,
    )
    first_sum, up_sum, out_sum = sums
    small_rows = shard_rows // groups_local
    small_own = lax.dynamic_slice_in_dim(gain_sum, expert_index * small_rows, small_rows, 1)
    latent_small = latent_rows // groups_local
    latent_own = lax.dynamic_slice_in_dim(gain_sum[2], expert_index * latent_small, latent_small, 0)
    down_start = query_cols % 128
    return (
        block_out[None],
        grad_tokens[None],
        small_own[0],
        first_sum[:, :query_cols],
        down_own[:, down_start : down_start + down_cols],
        latent_own,
        up_sum,
        out_sum.T,
        small_own[1],
        small_own[3 : 3 + experts_all].T,
        shared_grads[:, :shared_cols],
        shared_grads[:, shared_pad : shared_pad + shared_cols],
        shared_grads[:, 2 * shared_pad : 2 * shared_pad + shared_cols].T,
        *expert_grads,
    )


def solution(mesh):
    in_specs = (
        P((DP_AXIS, EXPERT_AXIS), CONTEXT_AXIS, None),
        P((DP_AXIS, EXPERT_AXIS), CONTEXT_AXIS, None),
        P((DP_AXIS, EXPERT_AXIS), CONTEXT_AXIS, None),
        P((DP_AXIS, CONTEXT_AXIS)),
        P((DP_AXIS, CONTEXT_AXIS), EXPERT_AXIS),
        P((DP_AXIS, CONTEXT_AXIS), None),
        P((DP_AXIS, CONTEXT_AXIS)),
        P((DP_AXIS, CONTEXT_AXIS), EXPERT_AXIS),
        P(EXPERT_AXIS, (DP_AXIS, CONTEXT_AXIS)),
        P((DP_AXIS, CONTEXT_AXIS)),
        P((DP_AXIS, CONTEXT_AXIS), None),
        P((DP_AXIS, CONTEXT_AXIS), EXPERT_AXIS),
        P((DP_AXIS, CONTEXT_AXIS), EXPERT_AXIS),
        P(EXPERT_AXIS, (DP_AXIS, CONTEXT_AXIS)),
        P(EXPERT_AXIS, (DP_AXIS, CONTEXT_AXIS), None),
        P(EXPERT_AXIS, (DP_AXIS, CONTEXT_AXIS), None),
        P(EXPERT_AXIS, (DP_AXIS, CONTEXT_AXIS), None),
    )
    out_specs = (
        P((DP_AXIS, EXPERT_AXIS), CONTEXT_AXIS, None),
        P((DP_AXIS, EXPERT_AXIS), CONTEXT_AXIS, None),
        P((DP_AXIS, CONTEXT_AXIS, EXPERT_AXIS)),
        P((DP_AXIS, CONTEXT_AXIS), EXPERT_AXIS),
        P((DP_AXIS, CONTEXT_AXIS, EXPERT_AXIS), None),
        P((DP_AXIS, CONTEXT_AXIS, EXPERT_AXIS)),
        P((DP_AXIS, CONTEXT_AXIS), EXPERT_AXIS),
        P(EXPERT_AXIS, (DP_AXIS, CONTEXT_AXIS)),
        P((DP_AXIS, CONTEXT_AXIS, EXPERT_AXIS)),
        P((DP_AXIS, CONTEXT_AXIS, EXPERT_AXIS), None),
        P((DP_AXIS, CONTEXT_AXIS), EXPERT_AXIS),
        P((DP_AXIS, CONTEXT_AXIS), EXPERT_AXIS),
        P(EXPERT_AXIS, (DP_AXIS, CONTEXT_AXIS)),
        P(EXPERT_AXIS, (DP_AXIS, CONTEXT_AXIS), None),
        P(EXPERT_AXIS, (DP_AXIS, CONTEXT_AXIS), None),
        P(EXPERT_AXIS, (DP_AXIS, CONTEXT_AXIS), None),
    )
    return jax.shard_map(body, mesh=mesh, in_specs=in_specs, out_specs=out_specs, check_vma=False)
```

```python
import jax
import jax.numpy as jnp
from jax import lax
from jax.experimental import pallas as pl
from jax.experimental.pallas import tpu as pltpu
from jax.experimental.layout import Layout, with_layout_constraint
from jax.sharding import PartitionSpec as P

D = 2048
NOPE = 128
ROPE = 64
VDIM = 128
LATENT = 512
TOPK = 6
PROMPT_DEV = 64
CONT_LEN = 64
TOK_DEV = 128


epsilon = 1e-06


def norm_rows(values, scale_gain):
    return (
        values * lax.rsqrt(jnp.mean(values * values, axis=-1, keepdims=True) + epsilon) * scale_gain
    )


def rotary_tables(places, half_size):
    frequency = 10000.0 ** (-jnp.arange(half_size, dtype=jnp.float32) / half_size)
    angles = places[:, None] * frequency[None, :]
    return (jnp.cos(angles), jnp.sin(angles))


def rotate(values, cosine, sine_part):
    half_size = values.shape[-1] // 2
    lower_half = values[..., :half_size]
    upper_half = values[..., half_size:]
    return jnp.concatenate(
        [
            lower_half * cosine - upper_half * sine_part,
            upper_half * cosine + lower_half * sine_part,
        ],
        axis=-1,
    )


def product(left_side, right_side):
    return jnp.dot(left_side, right_side, preferred_element_type=jnp.float32)


def product_left(left_side, right_side):
    return lax.dot_general(
        left_side, right_side, (((0,), (0,)), ((), ())), preferred_element_type=jnp.float32
    )


def product_right(left_side, right_side):
    return lax.dot_general(
        left_side, right_side, (((1,), (1,)), ((), ())), preferred_element_type=jnp.float32
    )


def against_rows(left_side, right_side):
    return lax.dot_general(
        left_side,
        right_side,
        (((left_side.ndim - 1,), (1,)), ((), ())),
        preferred_element_type=jnp.float32,
    )


DP_AXIS, CONTEXT_AXIS, EXPERT_AXIS = "dp", "context", "expert"
PLANE = (DP_AXIS, CONTEXT_AXIS)


def swap(values, axis, mask):
    count = lax.axis_size(axis)
    return lax.ppermute(values, axis, [(i, i ^ mask) for i in range(count)])


def place_pieces(pieces, index, count):
    first = pieces[0]
    whole = jnp.zeros((count,) + first.shape, first.dtype)
    for mask, piece in pieces.items():
        whole = lax.dynamic_update_slice(whole, piece[None], (index ^ mask,) + (0,) * first.ndim)
    return with_layout_constraint(whole, Layout(tuple(range(whole.ndim))))


def low(values):
    return values.astype(jnp.bfloat16)


def wide(values):
    return values.astype(jnp.float32)


def axis_gather(values, axis):
    count = lax.axis_size(axis)
    pieces = {mask: swap(values, axis, mask) if mask else values for mask in range(count)}
    return place_pieces(pieces, lax.axis_index(axis), count)


def axis_scatter(blocks, axis):
    count = lax.axis_size(axis)
    index = lax.axis_index(axis)

    def part(mask):
        return lax.dynamic_index_in_dim(blocks, index ^ mask, 0, keepdims=False)

    total = wide(part(0))
    for mask in range(1, count):
        total = total + wide(swap(low(part(mask)), axis, mask))
    return total


MESH_ID = pl.DeviceIdType.MESH
ANY = pl.BlockSpec(memory_space=pl.ANY)
INSIDE = pl.BlockSpec(memory_space=pltpu.VMEM)


def plane_here():
    return lax.axis_index(DP_AXIS) * lax.axis_size(CONTEXT_AXIS) + lax.axis_index(CONTEXT_AXIS)


def plane_device(mask):
    contexts = lax.axis_size(CONTEXT_AXIS)
    other = jnp.bitwise_xor(plane_here(), mask)
    return {DP_AXIS: other // contexts, CONTEXT_AXIS: lax.rem(other, contexts)}


def line_device(offset):
    return {EXPERT_AXIS: lax.axis_index(EXPERT_AXIS) + offset}


def signal(device):
    pl.semaphore_signal(
        pltpu.get_barrier_semaphore(), inc=1, device_id=device, device_id_type=MESH_ID
    )


def meet(masks, line):
    count = len(masks)
    for mask in masks:
        signal(plane_device(mask))
    if line:
        place, last = lax.axis_index(EXPERT_AXIS), lax.axis_size(EXPERT_AXIS) - 1
        pl.when(place > 0)(lambda: signal(line_device(-1)))
        pl.when(place < last)(lambda: signal(line_device(1)))
        count = count + jnp.where(place > 0, 1, 0) + jnp.where(place < last, 1, 0)
    pl.semaphore_wait(pltpu.get_barrier_semaphore(), count)


def remote(source, target, send, recv, device):
    return pltpu.make_async_remote_copy(
        src_ref=source,
        dst_ref=target,
        send_sem=send,
        recv_sem=recv,
        device_id=device,
        device_id_type=MESH_ID,
    )


def arrived(target, send, recv):
    remote(target, target, send, recv, plane_device(1)).wait_recv()


def run_tasks(*tasks):
    active = list(tasks)
    while active:
        for task in list(active):
            if next(task, None) is None:
                active.remove(task)


def plane_gather_task(source, target, own, send, recv):
    rows = source.shape[0]
    half = rows // 2
    here = plane_here()

    def slot(mask, first=0, count=rows):
        start = pl.multiple_of(jnp.bitwise_xor(here, mask) * rows + first, 16)
        return target.at[pl.ds(start, count)]

    def go(number, source_ref, target_ref, mask):
        copy = remote(source_ref, target_ref, send.at[number], recv.at[number], plane_device(mask))
        copy.start()
        return copy

    def got(number, ref):
        arrived(ref, send.at[number], recv.at[number])

    local = pltpu.make_async_copy(source, slot(0), own)
    copies = [go(0, source, slot(0), 2), go(1, source, slot(0), 4)]
    yield 1
    copies.append(go(4, source, slot(0), 1))
    local.start()
    yield 1
    got(0, slot(2))
    copies.append(go(2, slot(2, 0, half), slot(2, 0, half), 4))
    copies.append(go(5, slot(2), slot(2), 1))
    yield 1
    got(1, slot(4))
    copies.append(go(3, slot(4, half, half), slot(4, half, half), 2))
    copies.append(go(6, slot(4), slot(4), 1))
    yield 1
    got(2, slot(6, 0, half))
    copies.append(go(7, slot(6, 0, half), slot(6, 0, half), 1))
    yield 1
    got(3, slot(6, half, half))
    copies.append(go(8, slot(6, half, half), slot(6, half, half), 1))
    yield 1
    got(4, slot(1))
    got(5, slot(3))
    got(6, slot(5))
    got(7, slot(7, 0, half))
    got(8, slot(7, half, half))
    local.wait()
    for copy in copies:
        copy.wait_send()


def expert_fetch_task(source, target, stage, own, send, recv):
    if source.shape[0] == 1:
        load = pltpu.make_async_copy(source.at[0], stage, own)
        load.start()
        load.wait()
        yield from plane_gather_task(stage, target, own, send, recv)
        return
    rows = source.shape[1]
    here = plane_here()
    expert_own = here // 2

    def slot(mask):
        start = pl.multiple_of(jnp.bitwise_xor(here, mask) * rows, 16)
        return target.at[pl.ds(start, rows)]

    def go(number, source_ref, target_ref, mask):
        copy = remote(source_ref, target_ref, send.at[number], recv.at[number], plane_device(mask))
        copy.start()
        return copy

    def got(number, ref):
        arrived(ref, send.at[number], recv.at[number])

    copies = []
    for k in (3, 1, 2):
        copies.append(go(k, source.at[jnp.bitwise_xor(expert_own, k)], slot(0), 2 * k))
    load = pltpu.make_async_copy(source.at[expert_own], stage, own)
    load.start()
    yield 1
    load.wait()
    local = pltpu.make_async_copy(stage, slot(0), own)
    local.start()
    copies.append(go(0, stage, slot(0), 1))
    for k in (1, 2, 3):
        yield 1
        got(k, slot(2 * k))
        copies.append(go(4 + k, slot(2 * k), slot(2 * k), 1))
    yield 1
    got(0, slot(1))
    for k in (1, 2, 3):
        got(4 + k, slot(2 * k + 1))
    local.wait()
    for copy in copies:
        copy.wait_send()


LINE_PARTS = 4


def line_gather_steps(target, send, recv, rows):
    place, count = lax.axis_index(EXPERT_AXIS), lax.axis_size(EXPERT_AXIS)
    part = rows // LINE_PARTS

    def piece(block, c):
        return target.at[block, pl.ds(c * part, part)]

    def copy(way, distance, c, source=None):
        block = place - way * distance
        ref = piece(block, c)
        return remote(
            ref if source is None else source,
            ref,
            send.at[(way + 1) // 2, distance, c],
            recv.at[(way + 1) // 2, distance, c],
            line_device(way),
        )

    def has_next(way):
        return place < count - 1 if way == 1 else place > 0

    def has_block(way, distance):
        return place - distance >= 0 if way == 1 else place + distance < count

    def begin(c, source):
        for way in (1, -1):
            pl.when(has_next(way))(lambda way=way: copy(way, 0, c, source).start())

    def forward(c, distance):
        for way in (1, -1):

            @pl.when(has_block(way, distance))
            def _(way=way):
                ref = piece(place - way * distance, c)
                arrived(
                    ref,
                    send.at[(way + 1) // 2, distance - 1, c],
                    recv.at[(way + 1) // 2, distance - 1, c],
                )
                if distance < count - 1:
                    pl.when(has_next(way))(lambda: copy(way, distance, c).start())

    def finish(source):
        for c in range(LINE_PARTS):
            for way in (1, -1):
                for distance in range(count - 1):

                    @pl.when(jnp.logical_and(has_next(way), has_block(way, distance)))
                    def _(way=way, distance=distance, c=c):
                        copy(way, distance, c, source(c) if distance == 0 else None).wait_send()

    return begin, forward, finish


def line_gather_task(source, target, own, send, recv):
    rows = source.shape[0]
    part = rows // LINE_PARTS
    count = lax.axis_size(EXPERT_AXIS)
    begin, forward, finish = line_gather_steps(target, send, recv, rows)
    local = pltpu.make_async_copy(source, target.at[lax.axis_index(EXPERT_AXIS)], own)
    for c in range(LINE_PARTS):
        begin(c, source.at[pl.ds(c * part, part)])
    local.start()
    yield 1
    for distance in range(1, count):
        for c in range(LINE_PARTS):
            forward(c, distance)
        yield 1
    local.wait()
    finish(lambda c: source.at[pl.ds(c * part, part)])


def line_semaphores():
    count = lax.axis_size(EXPERT_AXIS)
    return [pltpu.SemaphoreType.DMA((2, count, LINE_PARTS))] * 2


def line_reduce_steps(partial, inbox, send, recv):
    place, count = lax.axis_index(EXPERT_AXIS), lax.axis_size(EXPERT_AXIS)
    rows = partial.shape[1]
    part = rows // LINE_PARTS

    def span(c):
        return pl.ds(c * part, part)

    def box(way, distance, c):
        return inbox.at[distance if way == 1 else count - distance, span(c)]

    def copy(way, distance, c, source):
        side = (way + 1) // 2
        return remote(
            source,
            box(way, distance - 1, c),
            send.at[side, distance, c],
            recv.at[side, distance - 1, c],
            line_device(way),
        )

    def wait_inbox(way, distance, c):
        side = (way + 1) // 2
        arrived(box(way, distance, c), send.at[side, distance, c], recv.at[side, distance, c])

    def has_source(way):
        return place > 0 if way == 1 else place < count - 1

    def has_target(way, distance):
        return place + distance < count if way == 1 else place - distance >= 0

    def step(c, distance):
        for way in (1, -1):
            mine = partial.at[place + way * distance, span(c)]

            def pass_on(way=way, mine=mine):
                came = box(way, distance, c)
                wait_inbox(way, distance, c)
                came[...] = low(wide(mine[...]) + wide(came[...]))
                copy(way, distance, c, came).start()

            def send_first(way=way, mine=mine):
                copy(way, distance, c, mine).start()

            valid = has_target(way, distance)
            if distance < count - 1:
                pl.when(jnp.logical_and(valid, has_source(way)))(pass_on)
                pl.when(jnp.logical_and(valid, jnp.logical_not(has_source(way))))(send_first)
            else:
                pl.when(valid)(send_first)

    def total(c, result):
        result[span(c)] = result[span(c)] + wide(partial[place, span(c)])
        for way in (1, -1):

            @pl.when(has_source(way))
            def _(way=way):
                wait_inbox(way, 0, c)
                result[span(c)] = result[span(c)] + wide(box(way, 0, c)[...])

    def stages(result, done):
        for t in range(LINE_PARTS + count - 1):
            for c in range(LINE_PARTS):
                distance = count - 1 - (t - c)
                if 1 <= distance <= count - 1:
                    step(c, distance)
                elif distance == 0:
                    total(c, result)
                    done(span(c), c)
            yield 1

    def finish():
        for c in range(LINE_PARTS):
            for way in (1, -1):
                for distance in range(1, count):
                    pl.when(has_target(way, distance))(
                        lambda way=way, distance=distance, c=c: copy(
                            way, distance, c, partial.at[place + way * distance, span(c)]
                        ).wait_send()
                    )

    return stages, finish


def gather_semaphores():
    return [
        pltpu.SemaphoreType.DMA(()),
        pltpu.SemaphoreType.DMA((9,)),
        pltpu.SemaphoreType.DMA((9,)),
    ]


def kernel_params(number):
    return pltpu.CompilerParams(
        collective_id=number,
        has_side_effects=True,
        vmem_limit_bytes=(52 if lax.axis_size(EXPERT_AXIS) <= 4 else 60) << 20,
    )


def opening(tokens, gains, matrices):
    count = lax.axis_size(EXPERT_AXIS)
    rows, width = tokens.shape
    number = len(matrices)
    planes = lax.axis_size(PLANE)
    depth = gains.shape[1]

    def kernel(*refs):
        tokens_ref, gains_ref = refs[:2]
        sources = refs[2 : 2 + number]
        gains_all, normed_all = refs[2 + number : 4 + number]
        targets = refs[4 + number : 4 + 2 * number]
        scratch = list(refs[4 + 2 * number :])
        normed, gain_box, gain_send, gain_recv = scratch[:4]
        line = scratch[4:7]
        semaphores = scratch[7:]
        meet(range(1, planes), True)
        here = plane_here()
        sends = []
        for mask in range(1, planes):
            copy = remote(
                gains_ref,
                gain_box.at[here],
                gain_send.at[mask],
                gain_recv.at[mask],
                plane_device(mask),
            )
            copy.start()
            sends.append(copy)
        tasks = [
            plane_gather_task(sources[i], targets[i], *semaphores[3 * i : 3 * i + 3])
            for i in range(number)
        ]
        for task in tasks:
            next(task)
        for task in tasks:
            next(task)
        gain_box[here] = gains_ref[...]
        values = wide(tokens_ref[...])
        scale = lax.rsqrt(jnp.mean(values * values, axis=-1, keepdims=True) + epsilon)
        for mask in range(1, planes):
            other = gain_box.at[jnp.bitwise_xor(here, mask)]
            arrived(other, gain_send.at[mask], gain_recv.at[mask])
        for i in range(planes):
            columns = slice(i * depth, (i + 1) * depth)
            normed[:, columns] = low(
                wide(tokens_ref[:, columns]) * scale * gain_box[i, 0:1, :]
            )
        gains_all[...] = gain_box[...]
        rows_task = line_gather_task(normed, normed_all, *line)
        next(rows_task)
        next(rows_task)
        for task in tasks:
            next(task)
        for task in tasks:
            next(task)
        run_tasks(rows_task, *tasks)
        for copy in sends:
            copy.wait_send()

    shapes = [
        jax.ShapeDtypeStruct((planes,) + gains.shape, jnp.float32),
        jax.ShapeDtypeStruct((count, rows, width), jnp.bfloat16),
    ] + [jax.ShapeDtypeStruct((planes * m.shape[0], m.shape[1]), m.dtype) for m in matrices]
    scratch = [
        pltpu.VMEM((rows, width), jnp.bfloat16),
        pltpu.VMEM((planes,) + gains.shape, jnp.float32),
        pltpu.SemaphoreType.DMA((planes,)),
        pltpu.SemaphoreType.DMA((planes,)),
        pltpu.SemaphoreType.DMA(()),
    ]
    scratch += line_semaphores()
    for _ in matrices:
        scratch += gather_semaphores()
    results = pl.pallas_call(
        kernel,
        out_shape=shapes,
        in_specs=[INSIDE] * (2 + number),
        out_specs=[INSIDE, ANY] + [ANY] * number,
        scratch_shapes=scratch,
        compiler_params=kernel_params(1),
        cost_estimate=pl.CostEstimate(
            flops=60_000_000, bytes_accessed=150_000_000, transcendentals=0
        ),
        name="opening",
    )(tokens, gains, *matrices)
    return results[0], results[1], results[2:]


def head_mask(head, heads, rope):
    lanes = lax.broadcasted_iota(jnp.int32, (1, rope), 1)
    return jnp.where(lax.rem(lanes, rope // 2) // (ROPE // 2) == head, 1.0, 0.0)


def middle_sum(query_nope, query_rope, keys, tiled, up, out, source, gain, experts, grads):
    count, rows = query_nope.shape[:2]
    key_count, rope = keys.shape[1], query_rope.shape[2]
    heads = query_nope.shape[2] // NOPE
    width = source.shape[1]
    planes, contexts = lax.axis_size(PLANE), lax.axis_size(CONTEXT_AXIS)
    routed = len(experts)
    score_scale = (NOPE + ROPE) ** (-0.5)

    def kernel(*refs):
        nope_ref, rope_ref, keys_ref, tiled_ref, up_ref, out_ref, source_ref, gain_ref = refs[:8]
        expert_refs = refs[8 : 8 + routed]
        grads_ref = refs[8 + routed]
        outputs = refs[9 + routed :]
        middle_ref, hidden_all, grads_all, mixed, probs, expanded = outputs[:6]
        targets = outputs[6 : 6 + routed]
        scratch = list(outputs[6 + routed :])
        grads_line = [scratch.pop() for _ in range(3)][::-1]
        partial_ref = scratch.pop(0)
        inbox, hidden, reduce_send, reduce_recv, own, line_send, line_recv = scratch[:7]
        stages = scratch[7 : 7 + routed]
        semaphores = scratch[7 + routed :]
        meet((1, 2, 4, 6), True)
        reduce_stages, reduce_finish = line_reduce_steps(
            partial_ref, inbox, reduce_send, reduce_recv
        )
        begin, forward, finish = line_gather_steps(hidden_all, line_send, line_recv, rows)
        part = rows // LINE_PARTS

        def ready(span, c):
            values = middle_ref[span]
            scale = lax.rsqrt(jnp.mean(values * values, axis=-1, keepdims=True) + epsilon)
            hidden[span] = low(values * scale * gain_ref[...])
            begin(c, hidden.at[span])

        def line_task():
            middle_ref[...] = wide(source_ref[...])
            yield from reduce_stages(middle_ref, ready)
            local = pltpu.make_async_copy(hidden, hidden_all.at[lax.axis_index(EXPERT_AXIS)], own)
            local.start()
            for distance in range(1, count):
                for c in range(LINE_PARTS):
                    forward(c, distance)
                yield 1
            local.wait()
            finish(lambda c: hidden.at[pl.ds(c * part, part)])
            reduce_finish()

        tasks = [
            expert_fetch_task(
                expert_refs[i], targets[i], stages[i], *semaphores[3 * i : 3 * i + 3]
            )
            for i in range(routed)
        ]
        for task in tasks:
            next(task)
        grads_task = line_gather_task(grads_ref, grads_all, *grads_line)
        next(grads_task)
        for task in tasks:
            next(task)
        here = lax.axis_index(CONTEXT_AXIS)
        row = lax.broadcasted_iota(jnp.int32, (rows, key_count), 0)
        place = jnp.where(
            row < PROMPT_DEV,
            here * PROMPT_DEV + row,
            contexts * PROMPT_DEV + row - PROMPT_DEV,
        )
        allowed = lax.broadcasted_iota(jnp.int32, (rows, key_count), 1) <= place

        def attend(g, carry):
            expanded[g] = low(product(keys_ref[g, :, :LATENT], up_ref[...]))
            for h in range(heads):
                start = h * (NOPE + VDIM)
                scores = product_right(
                    nope_ref[g, :, h * NOPE : (h + 1) * NOPE],
                    expanded[g, :, start : start + NOPE],
                ) + product_right(
                    rope_ref[g] * low(head_mask(h, heads, rope)), tiled_ref[g]
                )
                scores = jnp.where(allowed, scores * score_scale, -1e30)
                powers = jnp.exp(scores - jnp.max(scores, axis=-1, keepdims=True))
                weights = low(powers / jnp.sum(powers, axis=-1, keepdims=True))
                probs[g, h] = weights
                mixed[g, :, h * VDIM : (h + 1) * VDIM] = low(
                    product(weights, expanded[g, :, start + NOPE : start + NOPE + VDIM])
                )
            partial_ref[g] = low(product_right(mixed[g], out_ref[...]))
            return carry

        lax.fori_loop(0, count, attend, 0)
        run_tasks(line_task())
        run_tasks(grads_task, *tasks)

    shapes = [
        jax.ShapeDtypeStruct((rows, width), jnp.float32),
        jax.ShapeDtypeStruct((count, rows, width), jnp.bfloat16),
        jax.ShapeDtypeStruct((count, rows, width), jnp.bfloat16),
        jax.ShapeDtypeStruct((count, rows, heads * VDIM), jnp.bfloat16),
        jax.ShapeDtypeStruct((count, heads, rows, key_count), jnp.bfloat16),
        jax.ShapeDtypeStruct((count, key_count, up.shape[1]), jnp.bfloat16),
    ] + [jax.ShapeDtypeStruct((planes * e.shape[1], e.shape[2]), e.dtype) for e in experts]
    scratch = [
        pltpu.VMEM((count, rows, width), jnp.bfloat16),
        pltpu.VMEM((count + 1, rows, width), jnp.bfloat16),
        pltpu.VMEM((rows, width), jnp.bfloat16),
    ]
    scratch += line_semaphores() + [pltpu.SemaphoreType.DMA(())] + line_semaphores()
    scratch += [pltpu.VMEM(e.shape[1:], e.dtype) for e in experts]
    for _ in range(routed):
        scratch += gather_semaphores()
    scratch += [pltpu.SemaphoreType.DMA(())] + line_semaphores()
    results = pl.pallas_call(
        kernel,
        out_shape=shapes,
        in_specs=[INSIDE] * 8 + [ANY] * routed + [INSIDE],
        out_specs=[INSIDE, ANY, ANY] + [INSIDE] * 3 + [ANY] * routed,
        scratch_shapes=scratch,
        compiler_params=kernel_params(2),
        cost_estimate=pl.CostEstimate(
            flops=60_000_000, bytes_accessed=300_000_000, transcendentals=0
        ),
        name="middle_sum",
    )(query_nope, query_rope, keys, tiled, up, out, source, gain, *experts, grads)
    return results[:6], results[6:]


def add_rows(target, first, second):
    def tile(i, carry):
        span = pl.ds(pl.multiple_of(i * 16, 16), 16)
        target[span] = (wide(first[span]) + wide(second[span])).astype(target.dtype)
        return carry

    lax.fori_loop(0, target.shape[0] // 16, tile, 0)


def expert_return_task(source, result, mine, came, load, send, recv):
    rows = mine.shape[1]
    here = plane_here()
    expert_own = here // 2

    def slot(mask):
        return source.at[pl.ds(pl.multiple_of(jnp.bitwise_xor(here, mask) * rows, 16), rows)]

    def go(number, source_ref, target_ref, mask):
        copy = remote(source_ref, target_ref, send.at[number], recv.at[number], plane_device(mask))
        copy.start()
        return copy

    copies, loads = [], {}

    def cross(k):
        copies.append(go(k, slot(2 * k + 1), came.at[k], 1))
        loads[k] = pltpu.make_async_copy(slot(2 * k), mine.at[k], load.at[k])
        loads[k].start()

    cross(3)
    yield 1
    for k, following in ((3, 1), (1, 2), (2, 0), (0, None)):
        if following is not None:
            cross(following)
        arrived(came.at[k], send.at[k], recv.at[k])
        loads[k].wait()
        add_rows(mine.at[k], mine.at[k], came.at[k])
        if k:
            copies.append(go(4 + k, mine.at[k], result.at[expert_own], 2 * k))
        else:
            local = pltpu.make_async_copy(mine.at[0], result.at[expert_own], load.at[0])
            local.start()
        yield 1
    for k in (3, 1, 2):
        arrived(
            result.at[jnp.bitwise_xor(expert_own, k)], send.at[4 + k], recv.at[4 + k]
        )
    local.wait()
    for copy in copies:
        copy.wait_send()


def expert_return_scratch(rows, columns):
    return [
        pltpu.VMEM((4, rows, columns), jnp.bfloat16),
        pltpu.VMEM((4, rows, columns), jnp.bfloat16),
        pltpu.SemaphoreType.DMA((4,)),
        pltpu.SemaphoreType.DMA((8,)),
        pltpu.SemaphoreType.DMA((8,)),
    ]


def plane_scatter_task(source, result, mine, came, box, last, load, send, recv):
    rows = mine.shape[1]
    half = rows // 2
    here = plane_here()
    upper, lower = pl.ds(0, half), pl.ds(half, half)

    def slot(mask):
        return source.at[pl.ds(pl.multiple_of(jnp.bitwise_xor(here, mask) * rows, 16), rows)]

    def go(number, source_ref, target_ref, mask):
        copy = remote(source_ref, target_ref, send.at[number], recv.at[number], plane_device(mask))
        copy.start()
        return copy

    def got(number, ref):
        arrived(ref, send.at[number], recv.at[number])

    copies, loads = [], {}

    def cross(k):
        copies.append(go(k, slot(2 * k + 1), came.at[k], 1))
        loads[k] = pltpu.make_async_copy(slot(2 * k), mine.at[k], load.at[k])
        loads[k].start()

    cross(3)
    yield 1
    for k, following in ((3, 1), (1, 2), (2, 0)):
        cross(following)
        got(k, came.at[k])
        loads[k].wait()
        add_rows(mine.at[k], mine.at[k], came.at[k])
        if k == 3:
            copies.append(go(4, mine.at[3, upper], box.at[0], 2))
            copies.append(go(5, mine.at[3, lower], box.at[1], 4))
        elif k == 1:
            copies.append(go(6, mine.at[1, upper], last.at[0, upper], 2))
        else:
            copies.append(go(7, mine.at[2, lower], last.at[1, lower], 4))
        yield 1
    got(4, box.at[0])
    add_rows(mine.at[2, upper], mine.at[2, upper], box.at[0])
    copies.append(go(8, mine.at[2, upper], last.at[1, upper], 4))
    yield 1
    got(5, box.at[1])
    add_rows(mine.at[1, lower], mine.at[1, lower], box.at[1])
    copies.append(go(9, mine.at[1, lower], last.at[0, lower], 2))
    yield 1
    got(0, came.at[0])
    loads[0].wait()
    add_rows(result, mine.at[0], came.at[0])
    got(6, last.at[0, upper])
    got(7, last.at[1, lower])
    yield 1
    got(9, last.at[0, lower])
    add_rows(result, result, last.at[0])
    got(8, last.at[1, upper])
    add_rows(result, result, last.at[1])
    for copy in copies:
        copy.wait_send()


def plane_scatter_scratch(rows, columns):
    return [
        pltpu.VMEM((4, rows, columns), jnp.bfloat16),
        pltpu.VMEM((4, rows, columns), jnp.bfloat16),
        pltpu.VMEM((2, rows // 2, columns), jnp.bfloat16),
        pltpu.VMEM((2, rows, columns), jnp.bfloat16),
        pltpu.SemaphoreType.DMA((4,)),
        pltpu.SemaphoreType.DMA((10,)),
        pltpu.SemaphoreType.DMA((10,)),
    ]


def norm_back(values, gain, grad):
    scale = lax.rsqrt(jnp.mean(values * values, axis=-1, keepdims=True) + epsilon)
    scaled = gain * grad
    mean = jnp.mean(values * scaled, axis=-1, keepdims=True)
    part = jnp.sum(values * scale * grad, axis=0, keepdims=True)
    return scale * scaled - values * (scale * scale * scale * mean), part


def branch_sum(partial, middle, gain, grad_out, experts, local_experts, later):
    count, rows, width = partial.shape
    planes = lax.axis_size(PLANE)
    routed, waiting = len(experts), len(later)

    def kernel(*refs):
        partial_ref, middle_ref, gain_ref, grad_ref = refs[:4]
        expert_refs = refs[4 : 4 + routed]
        outputs = refs[4 + routed + waiting :]
        grad_middle, grad_gain, branch_all = outputs[:3]
        results = outputs[3 : 3 + routed]
        scratch = list(outputs[3 + routed + waiting :])
        inbox, branch, reduce_send, reduce_recv, own, line_send, line_recv = scratch[:7]
        rest = scratch[7:]
        meet((1, 2, 4, 6), True)
        reduce_stages, reduce_finish = line_reduce_steps(
            partial_ref, inbox, reduce_send, reduce_recv
        )
        begin, forward, finish = line_gather_steps(branch_all, line_send, line_recv, rows)
        part = rows // LINE_PARTS

        def ready(span, c):
            back, gain_part = norm_back(middle_ref[span], gain_ref[...], grad_middle[span])
            grad_gain[...] = gain_part if c == 0 else grad_gain[...] + gain_part
            back = wide(grad_ref[span]) + back
            grad_middle[span] = back
            branch[span] = low(back)
            begin(c, branch.at[span])

        def line_task():
            grad_middle[...] = jnp.zeros((rows, width), jnp.float32)
            yield from reduce_stages(grad_middle, ready)
            local = pltpu.make_async_copy(branch, branch_all.at[lax.axis_index(EXPERT_AXIS)], own)
            local.start()
            for distance in range(1, count):
                for c in range(LINE_PARTS):
                    forward(c, distance)
                yield 1
            local.wait()
            finish(lambda c: branch.at[pl.ds(c * part, part)])
            reduce_finish()

        task_kind = plane_scatter_task if local_experts == 1 else expert_return_task
        size = len(rest) // routed
        tasks = [
            task_kind(
                expert_refs[i], results[i], *rest[size * i : size * (i + 1)]
            )
            for i in range(routed)
        ]
        line = line_task()
        for stage in range(5):
            for task in tasks:
                next(task)
            if stage:
                next(line)
        run_tasks(line)
        run_tasks(*tasks)

    shapes = [
        jax.ShapeDtypeStruct((rows, width), jnp.float32),
        jax.ShapeDtypeStruct((1, width), jnp.float32),
        jax.ShapeDtypeStruct((count, rows, width), jnp.bfloat16),
    ]
    scratch = [
        pltpu.VMEM((count + 1, rows, width), jnp.bfloat16),
        pltpu.VMEM((rows, width), jnp.bfloat16),
    ]
    scratch += line_semaphores() + [pltpu.SemaphoreType.DMA(())] + line_semaphores()
    for expert in experts:
        shard, columns = expert.shape[0] // planes, expert.shape[1]
        if local_experts == 1:
            shapes.append(jax.ShapeDtypeStruct((shard, columns), jnp.float32))
            scratch += plane_scatter_scratch(shard, columns)
        else:
            shapes.append(jax.ShapeDtypeStruct((local_experts, shard, columns), jnp.bfloat16))
            scratch += expert_return_scratch(shard, columns)
    shapes += [jax.ShapeDtypeStruct(x.shape, x.dtype) for x in later]
    results = pl.pallas_call(
        kernel,
        out_shape=shapes,
        in_specs=[INSIDE] * 4 + [ANY] * (routed + waiting),
        out_specs=[INSIDE, INSIDE, ANY]
        + [INSIDE if local_experts == 1 else ANY] * routed
        + [ANY] * waiting,
        input_output_aliases={4 + routed + i: 3 + routed + i for i in range(waiting)},
        scratch_shapes=scratch,
        compiler_params=kernel_params(3),
        cost_estimate=pl.CostEstimate(
            flops=60_000_000, bytes_accessed=300_000_000, transcendentals=0
        ),
        name="branch_sum",
    )(partial, middle, gain, grad_out, *experts, *later)
    grads = [
        wide(r).reshape((local_experts,) + r.shape[-2:]) for r in results[3 : 3 + routed]
    ]
    return results[0], results[1][0], results[2], grads, results[3 + routed :]


def meet_all():
    planes, count = lax.axis_size(PLANE), lax.axis_size(EXPERT_AXIS)
    for mask in range(1, planes):
        signal(plane_device(mask))
    for mask in range(1, count):
        signal({EXPERT_AXIS: jnp.bitwise_xor(lax.axis_index(EXPERT_AXIS), mask)})
    pl.semaphore_wait(pltpu.get_barrier_semaphore(), planes + count - 2)


def closing(partial, ready_before, source, gain, grad_middle, gain_grads, matrices, spread):
    count, rows, width = partial.shape
    planes = lax.axis_size(PLANE)
    number = len(matrices)
    depth = gain_grads.shape[2]
    shard, columns = matrices[0].shape[0] // planes, matrices[0].shape[1]
    thin = shard // count

    def kernel(*refs):
        partial_ref, _, source_ref, gain_ref, middle_ref, gains_ref = refs[:6]
        sources = refs[6 : 6 + number]
        grad_tokens, gains_out, thin_out = refs[6 + number : 9 + number]
        results = refs[9 + number : 9 + 2 * number]
        scratch = list(refs[9 + 2 * number :])
        inbox, reduce_send, reduce_recv, gain_row = scratch[:4]
        gain_part, gain_box, gain_send, gain_recv = scratch[4:8]
        gain_held, gain_far, far_send, far_recv, thin_box, thin_send, thin_recv = scratch[8:15]
        rest = scratch[15:]
        meet_all()
        place = lax.axis_index(EXPERT_AXIS)
        here = plane_here()
        reduce_stages, reduce_finish = line_reduce_steps(
            partial_ref, inbox, reduce_send, reduce_recv
        )

        def ready(span, c):
            back, row = norm_back(wide(source_ref[span]), gain_ref[...], grad_tokens[span])
            gain_row[...] = row if c == 0 else gain_row[...] + row
            grad_tokens[span] = middle_ref[span] + back

        def line_task():
            grad_tokens[...] = jnp.zeros((rows, width), jnp.float32)
            yield from reduce_stages(grad_tokens, ready)
            gain_part[...] = gains_ref[...]
            for i in range(planes):
                gain_part[i, 0:1, :] = gain_row[:, i * depth : (i + 1) * depth]
            copies = []
            for mask in range(1, planes):
                copy = remote(
                    gain_part.at[jnp.bitwise_xor(here, mask)],
                    gain_box.at[mask],
                    gain_send.at[mask],
                    gain_recv.at[mask],
                    plane_device(mask),
                )
                copy.start()
                copies.append(copy)
            gain_total = gain_part[here]
            yield 1
            for mask in range(1, planes):
                arrived(gain_box.at[mask], gain_send.at[mask], gain_recv.at[mask])
                gain_total = gain_total + gain_box[mask]
            gain_held[...] = gain_total
            for mask in range(1, count):
                copy = remote(
                    gain_held,
                    gain_far.at[mask],
                    far_send.at[mask],
                    far_recv.at[mask],
                    {EXPERT_AXIS: jnp.bitwise_xor(place, mask)},
                )
                copy.start()
                copies.append(copy)
            yield 1
            for mask in range(1, count):
                arrived(gain_far.at[mask], far_send.at[mask], far_recv.at[mask])
                gain_total = gain_total + gain_far[mask]
            gains_out[...] = gain_total
            for copy in copies:
                copy.wait_send()
            reduce_finish()

        def first_task(task):
            yield from task
            copies = []

            def piece(mask):
                start = pl.multiple_of(jnp.bitwise_xor(place, mask) * thin, 8 if thin % 8 == 0 else thin)
                return results[0].at[pl.ds(start, thin), pl.ds(spread, columns - spread)]

            for mask in range(1, count):
                copy = remote(
                    piece(mask),
                    thin_box.at[mask],
                    thin_send.at[mask],
                    thin_recv.at[mask],
                    {EXPERT_AXIS: jnp.bitwise_xor(place, mask)},
                )
                copy.start()
                copies.append(copy)
            yield 1
            total = piece(0)[...]
            for mask in range(1, count):
                arrived(thin_box.at[mask], thin_send.at[mask], thin_recv.at[mask])
                total = total + thin_box[mask]
            thin_out[...] = total
            for copy in copies:
                copy.wait_send()

        size = len(rest) // number
        tasks = [
            plane_scatter_task(sources[i], results[i], *rest[size * i : size * (i + 1)])
            for i in range(number)
        ]
        tasks[0] = first_task(tasks[0])
        line = line_task()
        for stage in range(6):
            for task in tasks:
                next(task)
            if stage:
                next(line)
        run_tasks(line, *tasks)

    shapes = [
        jax.ShapeDtypeStruct((rows, width), jnp.float32),
        jax.ShapeDtypeStruct(gain_grads.shape[1:], jnp.float32),
        jax.ShapeDtypeStruct((thin, columns - spread), jnp.float32),
    ] + [jax.ShapeDtypeStruct((m.shape[0] // planes, m.shape[1]), jnp.float32) for m in matrices]
    scratch = [pltpu.VMEM((count + 1, rows, width), jnp.bfloat16)]
    scratch += line_semaphores()
    scratch += [
        pltpu.VMEM((1, width), jnp.float32),
        pltpu.VMEM(gain_grads.shape, jnp.float32),
        pltpu.VMEM(gain_grads.shape, jnp.float32),
        pltpu.SemaphoreType.DMA((planes,)),
        pltpu.SemaphoreType.DMA((planes,)),
        pltpu.VMEM(gain_grads.shape[1:], jnp.float32),
        pltpu.VMEM((count,) + gain_grads.shape[1:], jnp.float32),
        pltpu.SemaphoreType.DMA((count,)),
        pltpu.SemaphoreType.DMA((count,)),
        pltpu.VMEM((count, thin, columns - spread), jnp.float32),
        pltpu.SemaphoreType.DMA((count,)),
        pltpu.SemaphoreType.DMA((count,)),
    ]
    for m in matrices:
        scratch += plane_scatter_scratch(m.shape[0] // planes, m.shape[1])
    results = pl.pallas_call(
        kernel,
        out_shape=shapes,
        in_specs=[INSIDE, ANY] + [INSIDE] * 4 + [ANY] * number,
        out_specs=[INSIDE] * (3 + number),
        scratch_shapes=scratch,
        compiler_params=kernel_params(4),
        cost_estimate=pl.CostEstimate(
            flops=60_000_000, bytes_accessed=200_000_000, transcendentals=0
        ),
        name="closing",
    )(partial, ready_before, source, gain, grad_middle, gain_grads, *matrices)
    return results[:3], results[3:]


def silu_back(gate, up, grad):
    sigmoid_part = 1.0 / (1.0 + jnp.exp(-gate))
    silu_part = gate * sigmoid_part
    slope = sigmoid_part * (1.0 + gate * (1.0 - sigmoid_part))
    return silu_part * up, grad * up * slope, grad * silu_part


def row_copies(source, target, send, recv, copies):
    return [
        remote(source(k), target(k), send.at[k], recv.at[k], plane_device(k * copies))
        for k in (3, 1, 2)
    ]


def shared_and_rows(hidden, grads, weights, hidden_slots, grad_slots, gates, copies):
    tokens, width = hidden.shape
    columns = weights.shape[1] // 3
    pieces, slots = hidden_slots.shape[:2]
    exchanged = copies > 0
    tall = max(t for t in (256, 128, tokens) if tokens % t == 0)
    wide_part = 256

    def kernel(*refs):
        hidden_any, grads_any, weights_any, rows_any, grad_rows_any, gates_ref = refs[:6]
        act_out, back_out, weight_grads = refs[6:9]
        outputs = refs[9:12]
        scratch = refs[12:] if exchanged else refs[9:]
        hid, grd, wts, both, load = scratch[:5]
        loads = [
            pltpu.make_async_copy(hidden_any, hid, load.at[0]),
            pltpu.make_async_copy(weights_any, wts, load.at[1]),
            pltpu.make_async_copy(grads_any, grd, load.at[2]),
        ]
        moves = []
        if exchanged:
            semaphores = scratch[5:]
            meet([k * copies for k in (1, 2, 3)], False)
            for i, source in enumerate((gates_ref, rows_any, grad_rows_any)):
                moves += row_copies(
                    lambda k, source=source: source.at[k],
                    lambda k, i=i: outputs[i].at[k - 1],
                    semaphores[2 * i],
                    semaphores[2 * i + 1],
                    copies,
                )
            for move in moves:
                move.start()
        for copy in loads:
            copy.start()
        for copy in loads:
            copy.wait()

        def rows_tile(i, carry):
            span = pl.ds(pl.multiple_of(i * tall, 16), tall)
            gate = product(hid[span], wts[:, :columns])
            up = product(hid[span], wts[:, columns : 2 * columns])
            grad = product(grd[span], wts[:, 2 * columns :])
            act, dgate, dup = silu_back(gate, up, grad)
            act_out[span] = low(act)
            both[span, :columns] = low(dgate)
            both[span, columns:] = low(dup)
            back_out[span] = product_right(both[span], wts[:, : 2 * columns])
            return carry

        lax.fori_loop(0, tokens // tall, rows_tile, 0)

        def weights_tile(i, carry):
            span = pl.ds(pl.multiple_of(i * wide_part, wide_part), wide_part)
            weight_grads[span, : 2 * columns] = low(product_left(hid[:, span], both[...]))
            weight_grads[span, 2 * columns :] = low(product_left(grd[:, span], act_out[...]))
            return carry

        lax.fori_loop(0, width // wide_part, weights_tile, 0)
        for move in moves:
            move.wait()

    shapes = [
        jax.ShapeDtypeStruct((tokens, columns), jnp.bfloat16),
        jax.ShapeDtypeStruct((tokens, width), jnp.float32),
        jax.ShapeDtypeStruct(weights.shape, jnp.bfloat16),
    ]
    out_specs = [INSIDE] * 3
    scratch = [
        pltpu.VMEM(hidden.shape, jnp.bfloat16),
        pltpu.VMEM(grads.shape, jnp.bfloat16),
        pltpu.VMEM(weights.shape, jnp.bfloat16),
        pltpu.VMEM((tokens, 2 * columns), jnp.bfloat16),
        pltpu.SemaphoreType.DMA((3,)),
    ]
    if exchanged:
        shapes += [jax.ShapeDtypeStruct((3,) + x.shape[1:], x.dtype) for x in (gates, hidden_slots, grad_slots)]
        out_specs += [INSIDE, ANY, ANY]
        scratch += [pltpu.SemaphoreType.DMA((4,))] * 6
    results = pl.pallas_call(
        kernel,
        out_shape=shapes,
        in_specs=[ANY] * 5 + [INSIDE],
        out_specs=out_specs,
        scratch_shapes=scratch,
        compiler_params=kernel_params(5) if exchanged else pltpu.CompilerParams(vmem_limit_bytes=60 << 20),
        cost_estimate=pl.CostEstimate(
            flops=12 * tokens * width * columns, bytes_accessed=120_000_000, transcendentals=0
        ),
        name="shared_and_rows",
    )(hidden, grads, weights, hidden_slots, grad_slots, gates)
    return results[:3], results[3:]


def routed_expert(hidden_slots, grad_slots, hidden_far, grad_far, gates, weights, copies):
    slots, width = hidden_slots.shape[1:]
    gate_full, up_full, down_full = weights
    units = gate_full.shape[1]
    exchanged = copies > 0

    def kernel(*refs):
        far = 2 if exchanged else 0
        hidden_any, grad_any = refs[:2]
        hidden_far_any, grad_far_any = refs[2:4] if exchanged else (None, None)
        gates_ref, wg_any, wu_any, wd_any = refs[2 + far : 6 + far]
        pair_back, result_back, scale_back, dwg, dwu, dwd = refs[6 + far : 12 + far]
        scratch = refs[12 + far :]
        wg, wu, wd, hid, grd, act, dgate, dup, pair, result, scale = scratch[:11]
        tile_up, tile_down, load, own, store = scratch[11:16]
        semaphores = scratch[16:]

        def piece(ref, ref_far, k):
            return ref.at[k] if k == 0 or not exchanged else ref_far.at[k - 1]

        if exchanged:
            meet([k * copies for k in (1, 2, 3)], False)
        loads = {}

        def fetch(number, source, target):
            loads[number] = pltpu.make_async_copy(source, target, load.at[number])
            loads[number].start()

        fetch(0, wg_any, wg)
        for k in (3, 2, 1, 0):
            fetch(3 + k, piece(hidden_any, hidden_far_any, k), hid.at[pl.ds(k * slots, slots)])
        fetch(1, wu_any, wu)
        fetch(2, wd_any, wd)
        for k in (3, 2, 1, 0):
            fetch(7 + k, piece(grad_any, grad_far_any, k), grd.at[pl.ds(k * slots, slots)])
        def back(k, which):
            source, target = ((pair, pair_back), (result, result_back), (scale, scale_back))[which]
            return remote(
                source.at[k],
                target.at[k],
                semaphores[2 * which].at[k],
                semaphores[2 * which + 1].at[k],
                plane_device(k * copies),
            )

        def deliver(k, which):
            if exchanged:
                pl.when(k > 0)(lambda: back(k, which).start())

        def first(i, carry):
            k = 3 - i
            span = pl.ds(pl.multiple_of(k * slots, 16), slots)

            def ready(*numbers):
                @pl.when(i == 0)
                def _():
                    for number in numbers:
                        loads[number].wait()

            ready(0, 6, 5, 4, 3)
            gate = product(hid[span], wg[...])
            ready(1)
            up = product(hid[span], wu[...])
            ready(2, 10, 9, 8, 7)
            grad = product_right(grd[span], wd[...])
            gates_here = gates_ref[span]
            act_part, dgate_part, dup_part = silu_back(gate, up, grad)
            scale[k] = jnp.broadcast_to(
                jnp.sum(act_part * grad, axis=-1, keepdims=True), scale.shape[1:]
            )
            act[span] = low(act_part * gates_here)
            dgate[span] = low(dgate_part * gates_here)
            dup[span] = low(dup_part * gates_here)
            pair[k] = low(product_right(dgate[span], wg[...]) + product_right(dup[span], wu[...]))
            deliver(k, 0)
            deliver(k, 2)
            result[k] = low(product(act[span], wd[...]))
            deliver(k, 1)
            return carry

        lax.fori_loop(0, 4, first, 0)
        kept = []
        for which, (source, target) in enumerate(
            ((pair, pair_back), (result, result_back), (scale, scale_back))
        ):
            for k in range(1 if exchanged else 4):
                copy = pltpu.make_async_copy(source.at[k], target.at[k], own.at[which, k])
                copy.start()
                kept.append(copy)

        def tiles(count, rows, buffer, target, compute):
            def put(i, slot):
                start = pl.multiple_of(i * rows, 16)
                return pltpu.make_async_copy(
                    buffer.at[slot], target.at[pl.ds(start, rows)], store.at[slot]
                )

            def tile(i, carry):
                slot = lax.rem(i, 2)
                pl.when(i >= 2)(lambda: put(i - 2, slot).wait())
                buffer[slot] = compute(pl.ds(pl.multiple_of(i * rows, rows), rows))
                put(i, slot).start()
                return carry

            lax.fori_loop(0, count, tile, 0)
            for i in (count - 2, count - 1):
                put(i, i % 2).wait()

        tiles(width // 256, 256, tile_up, dwg, lambda s: low(product_left(hid[:, s], dgate[...])))
        tiles(width // 256, 256, tile_up, dwu, lambda s: low(product_left(hid[:, s], dup[...])))
        tiles(units // 128, 128, tile_down, dwd, lambda s: low(product_left(act[:, s], grd[...])))
        for copy in kept:
            copy.wait()
        if exchanged:
            for which in (0, 2, 1):
                for k in (3, 2, 1):
                    back(k, which).wait()

    shapes = [
        jax.ShapeDtypeStruct((4, slots, width), jnp.bfloat16),
        jax.ShapeDtypeStruct((4, slots, width), jnp.bfloat16),
        jax.ShapeDtypeStruct((4, slots, 128), jnp.float32),
    ] + [jax.ShapeDtypeStruct(w.shape, jnp.bfloat16) for w in weights]
    rows = 4 * slots
    scratch = [pltpu.VMEM(w.shape, jnp.bfloat16) for w in weights]
    scratch += [pltpu.VMEM((rows, width), jnp.bfloat16)] * 2
    scratch += [pltpu.VMEM((rows, units), jnp.bfloat16)] * 3
    scratch += [pltpu.VMEM((4, slots, width), jnp.bfloat16)] * 2
    scratch += [pltpu.VMEM((4, slots, 128), jnp.float32)]
    scratch += [
        pltpu.VMEM((2, 256, units), jnp.bfloat16),
        pltpu.VMEM((2, 128, width), jnp.bfloat16),
        pltpu.SemaphoreType.DMA((11,)),
        pltpu.SemaphoreType.DMA((3, 4)),
        pltpu.SemaphoreType.DMA((2,)),
    ]
    if exchanged:
        scratch += [pltpu.SemaphoreType.DMA((4,))] * 6
    operands = [hidden_slots, grad_slots] + ([hidden_far, grad_far] if exchanged else [])
    results = pl.pallas_call(
        kernel,
        out_shape=shapes,
        in_specs=[ANY] * len(operands) + [INSIDE] + [ANY] * 3,
        out_specs=[ANY] * 6,
        scratch_shapes=scratch,
        compiler_params=pltpu.CompilerParams(
            collective_id=6, has_side_effects=True, vmem_limit_bytes=60 << 20
        )
        if exchanged
        else pltpu.CompilerParams(vmem_limit_bytes=60 << 20),
        cost_estimate=pl.CostEstimate(
            flops=18 * rows * units * width, bytes_accessed=200_000_000, transcendentals=0
        ),
        name="routed_expert",
    )(*operands, gates, *weights)
    return results


def attention_back(branch, out, probs, expanded, query_nope, query_rope, keys, tiled, up):
    groups, rows, width = branch.shape
    heads, key_count = probs.shape[1], probs.shape[3]
    rope = query_rope.shape[2]
    score_scale = (NOPE + ROPE) ** (-0.5)

    def kernel(*refs):
        branch_ref, out_ref, probs_ref, exp_ref, nope_ref, rope_ref, keys_ref, tiled_ref, up_ref = (
            refs[:9]
        )
        dnope, drope, dlatent, dkey_rope, dup, dexp = refs[9:]
        dmixed = low(product(branch_ref[...], out_ref[...]))
        drope_sum = jnp.zeros((rows, rope), jnp.float32)
        dkey_sum = jnp.zeros((key_count, rope), jnp.float32)
        for h in range(heads):
            nope_span = slice(h * NOPE, (h + 1) * NOPE)
            key_span = slice(h * (NOPE + VDIM), h * (NOPE + VDIM) + NOPE)
            value_span = slice(h * (NOPE + VDIM) + NOPE, (h + 1) * (NOPE + VDIM))
            mask = head_mask(h, heads, rope)
            weights = probs_ref[h]
            part = dmixed[:, h * VDIM : (h + 1) * VDIM]
            dprobs = product_right(part, exp_ref[:, value_span])
            wide_weights = wide(weights)
            delta = jnp.sum(wide_weights * dprobs, axis=-1, keepdims=True)
            dscore = low(wide_weights * (dprobs - delta) * score_scale)
            dexp[:, key_span] = low(product_left(dscore, nope_ref[:, nope_span]))
            dexp[:, value_span] = low(product_left(weights, part))
            dnope[:, nope_span] = low(product(dscore, exp_ref[:, key_span]))
            drope_sum = drope_sum + product(dscore, tiled_ref[...]) * mask
            dkey_sum = dkey_sum + product_left(dscore, rope_ref[...] * low(mask))
        drope[...] = drope_sum
        dkey_rope[...] = dkey_sum
        dlatent[...] = product_right(dexp[...], up_ref[...])
        grad_up = product_left(keys_ref[:, :LATENT], dexp[...])

        @pl.when(pl.program_id(0) == 0)
        def _():
            dup[...] = grad_up

        @pl.when(pl.program_id(0) > 0)
        def _():
            dup[...] = dup[...] + grad_up

    def group(array):
        shape = array.shape
        return pl.BlockSpec(
            (None,) + tuple(shape[1:]), lambda g, n=len(shape) - 1: (g,) + (0,) * n
        )

    def whole(array):
        return pl.BlockSpec(array.shape, lambda g: (0, 0))

    shapes = [
        jax.ShapeDtypeStruct((groups, rows, heads * NOPE), jnp.bfloat16),
        jax.ShapeDtypeStruct((groups, rows, rope), jnp.float32),
        jax.ShapeDtypeStruct((groups, key_count, LATENT), jnp.float32),
        jax.ShapeDtypeStruct((groups, key_count, rope), jnp.float32),
        jax.ShapeDtypeStruct(up.shape, jnp.float32),
    ]
    operands = [branch, out, probs, expanded, query_nope, query_rope, keys, tiled, up]
    return pl.pallas_call(
        kernel,
        grid=(groups,),
        out_shape=shapes,
        in_specs=[whole(x) if x is out or x is up else group(x) for x in operands],
        out_specs=[group(x) for x in shapes[:4]] + [whole(up)],
        scratch_shapes=[pltpu.VMEM((key_count, heads * (NOPE + VDIM)), jnp.bfloat16)],
        compiler_params=pltpu.CompilerParams(vmem_limit_bytes=40 << 20),
        cost_estimate=pl.CostEstimate(
            flops=20_000_000_000, bytes_accessed=30_000_000, transcendentals=0
        ),
        name="attention_back",
    )(*operands)


def body(
    tokens,
    routes,
    grad_out,
    attn_gain,
    query_weight,
    latent_down,
    latent_gain,
    latent_up,
    out_weight,
    ffn_gain,
    router_weight,
    shared_gate,
    shared_up,
    shared_down,
    expert_gate,
    expert_up,
    expert_down,
):
    contexts = lax.axis_size(CONTEXT_AXIS)
    context_index = lax.axis_index(CONTEXT_AXIS)
    groups_local = lax.axis_size(EXPERT_AXIS)
    expert_index = lax.axis_index(EXPERT_AXIS)
    plane_count = lax.axis_size(PLANE)
    plane_index = lax.axis_index(PLANE)
    local_experts = expert_gate.shape[0]
    experts_all = router_weight.shape[1]
    copies = plane_count // local_experts
    expert_own = plane_index // copies
    query_cols = query_weight.shape[1]
    heads_local = query_cols // (NOPE + ROPE)
    down_cols = LATENT + ROPE
    shard_rows = query_weight.shape[0]
    latent_rows = latent_up.shape[0]
    prompt_len = PROMPT_DEV * contexts
    capacity = (TOK_DEV * TOPK * 9 + 8 * experts_all - 1) // (8 * experts_all)
    slots = groups_local * capacity
    slots = -(-slots // 16) * 16 if local_experts > 1 else -(-slots // 64) * 64
    token_count = groups_local * TOK_DEV
    score_scale = (NOPE + ROPE) ** (-0.5)

    half_rope = ROPE // 2
    rope_cols = heads_local * half_rope
    nope_cols = heads_local * NOPE

    def query_split(columns):
        each = columns.reshape(columns.shape[0], heads_local, NOPE + ROPE)
        parts = (each[..., :NOPE], each[..., NOPE : NOPE + half_rope], each[..., NOPE + half_rope :])
        return [part.reshape(columns.shape[0], -1) for part in parts]

    def query_join(columns):
        rows = columns.shape[0]
        parts = (
            columns[:, :nope_cols],
            columns[:, nope_cols : nope_cols + rope_cols],
            columns[:, nope_cols + rope_cols :],
        )
        each = [part.reshape(rows, heads_local, -1) for part in parts]
        return jnp.concatenate(each, axis=-1).reshape(rows, query_cols)

    used_cols = query_cols + down_cols
    extra_cols = experts_all + 3
    pad_cols = -(used_cols + extra_cols) % 128
    gains = jnp.stack(
        [
            wide(attn_gain),
            wide(ffn_gain),
            jnp.pad(wide(latent_gain), (0, shard_rows - latent_gain.shape[0])),
        ]
        + [jnp.zeros((shard_rows,), jnp.float32)] * 5
    )
    first_local = jnp.concatenate(
        [
            *query_split(query_weight),
            latent_down,
            router_weight,
            jnp.zeros((shard_rows, 3 + pad_cols), jnp.bfloat16),
        ],
        axis=1,
    )
    shared_cols = shared_gate.shape[1]
    shared_pad = -(-shared_cols // 128) * 128

    def padded(weight):
        return jnp.pad(weight, ((0, 0), (0, shared_pad - shared_cols)))

    shared_own = jnp.concatenate(
        [padded(shared_gate), padded(shared_up), padded(shared_down.T)], axis=1
    )
    shared_whole = lax.all_gather(shared_own, PLANE, axis=0, tiled=True)
    gains_all, normed_all, (first_full, up_local, out_local) = opening(
        tokens[0], gains, [first_local, latent_up, out_weight.T]
    )
    full_router = first_full[:, used_cols : used_cols + experts_all]
    full_attn_gain = gains_all[:, 0].reshape(D)
    full_ffn_gain = gains_all[:, 1].reshape(D)
    full_latent_gain = gains_all[:, 2, : latent_gain.shape[0]].reshape(LATENT)

    within = jnp.arange(TOK_DEV, dtype=jnp.int32)
    query_places = jnp.where(
        within < PROMPT_DEV, context_index * PROMPT_DEV + within, prompt_len + within - PROMPT_DEV
    )
    cosine, sine_part = rotary_tables(query_places.astype(jnp.float32), ROPE // 2)
    source = wide(tokens[0])

    def pack_latent(comp_rows, latent_scale):
        return jnp.concatenate(
            [
                norm_rows(comp_rows[..., :LATENT], latent_scale),
                rotate(comp_rows[..., LATENT:], cosine[None], sine_part[None]),
            ],
            axis=-1,
        )

    routes_all = axis_gather(routes[0], EXPERT_AXIS)
    first_product = product(normed_all, first_full)
    compressed = first_product[..., query_cols:used_cols]
    packed = low(pack_latent(compressed, wide(full_latent_gain)))
    key_count = prompt_len + CONT_LEN
    keys = jnp.zeros((groups_local, contexts + 1, PROMPT_DEV, down_cols), jnp.bfloat16)
    prompt_own = packed[:, :PROMPT_DEV]
    for mask in range(contexts):
        came = swap(prompt_own, CONTEXT_AXIS, mask) if mask else prompt_own
        keys = lax.dynamic_update_slice(
            keys, came[:, None], (0, jnp.bitwise_xor(context_index, mask), 0, 0)
        )
    keys = lax.dynamic_update_slice(
        keys, packed[:, None, PROMPT_DEV:], (0, contexts, 0, 0)
    ).reshape(groups_local, key_count, down_cols)
    query_nope = low(first_product[..., :nope_cols])
    cosine_heads = jnp.tile(cosine, (1, heads_local))[None]
    sine_heads = jnp.tile(sine_part, (1, heads_local))[None]
    lower = first_product[..., nope_cols : nope_cols + rope_cols]
    upper = first_product[..., nope_cols + rope_cols : query_cols]
    query_rope = low(
        jnp.concatenate(
            [
                lower * cosine_heads - upper * sine_heads,
                upper * cosine_heads + lower * sine_heads,
            ],
            axis=-1,
        )
    )
    tiled_rope = jnp.concatenate(
        [keys[..., LATENT : LATENT + half_rope]] * heads_local
        + [keys[..., LATENT + half_rope :]] * heads_local,
        axis=-1,
    )
    slot_experts = expert_index * local_experts + (
        expert_own ^ jnp.arange(local_experts, dtype=jnp.int32)
    )
    expert_cols = jnp.arange(experts_all, dtype=jnp.int32)[:, None] == slot_experts[None, :]
    chosen_slots = jnp.any(routes_all[..., None] == slot_experts, axis=2)
    before = (within[:, None] > within[None, :]).astype(jnp.bfloat16)
    rank = jnp.einsum(
        "ts,gsl->gtl",
        before,
        chosen_slots.astype(jnp.bfloat16),
        preferred_element_type=jnp.float32,
    ).astype(jnp.int32)
    slot_of = jnp.where(
        chosen_slots,
        rank + capacity * jnp.arange(groups_local, dtype=jnp.int32)[:, None, None],
        -1,
    ).reshape(token_count, local_experts)
    picked = (
        slot_of.T[:, None, :] == jnp.arange(slots, dtype=jnp.int32)[None, :, None]
    )
    picked_low = picked.astype(jnp.bfloat16).reshape(local_experts * slots, token_count)
    piece_slots = slots * local_experts // 4
    (middle, hidden_all, grad_all, mixed_all, probs, expanded), fetched = middle_sum(
        query_nope,
        query_rope,
        keys,
        tiled_rope,
        up_local,
        out_local,
        tokens[0],
        full_ffn_gain[None],
        [expert_gate, expert_up, expert_down],
        grad_out[0],
    )
    gate_full, up_full, down_full = fetched
    hidden_flat = hidden_all.reshape(token_count, D)

    grad_flat = grad_all.reshape(token_count, D)
    hidden_slots = low(product(picked_low, hidden_flat)).reshape(4, piece_slots, D)
    grad_slots = low(product(picked_low, grad_flat)).reshape(4, piece_slots, D)
    logits = product(hidden_flat, full_router)
    expert_probs = jax.nn.softmax(logits, axis=-1)
    gate_tokens = jnp.sum(jnp.where(expert_cols[None], expert_probs[:, :, None], 0.0), axis=1)
    gate_slots = jnp.sum(jnp.where(picked, gate_tokens.T[:, None, :], 0.0), axis=-1)
    gate_slots = gate_slots.reshape(4, piece_slots)
    gates_padded = jnp.broadcast_to(
        jnp.pad(gate_slots, ((0, 0), (0, -piece_slots % 128)))[:, None], (4, 8, -(-piece_slots // 128) * 128)
    )
    row_hops = copies if local_experts > 1 else 0
    (act_shared, shared_hidden, shared_grads), far = shared_and_rows(
        hidden_flat, grad_flat, shared_whole, hidden_slots, grad_slots, gates_padded, row_hops
    )
    gates_far, hidden_far, grad_far = far if far else (None, None, None)
    if far:
        gate_slots = jnp.concatenate([gate_slots[:1], gates_far[:, 0, :piece_slots]], axis=0)
    pair_back, result, scale_back, *expert_partials = routed_expert(
        hidden_slots,
        grad_slots,
        hidden_far,
        grad_far,
        gate_slots.reshape(-1, 1),
        [gate_full, up_full, down_full],
        row_hops,
    )
    grad_gate_back = scale_back[:, :, 0].reshape(local_experts, slots)
    grad_routed = product_left(picked_low, pair_back.reshape(-1, D))
    grad_gate_tokens = jnp.sum(jnp.where(picked, grad_gate_back[:, :, None], 0.0), axis=1).T
    grad_spread = jnp.sum(
        jnp.where(expert_cols[None], grad_gate_tokens[:, None, :], 0.0), axis=-1
    )
    weighted = jnp.sum(expert_probs * grad_spread, axis=-1, keepdims=True)
    grad_logits = expert_probs * (grad_spread - weighted)
    grad_router = lax.dot_general(
        grad_logits,
        wide(hidden_flat),
        (((0,), (0,)), ((), ())),
        precision=lax.Precision.HIGHEST,
    )
    grad_from_router = lax.dot_general(
        grad_logits,
        wide(full_router),
        (((1,), (1,)), ((), ())),
        precision=lax.Precision.HIGHEST,
    )
    grad_hidden_part = low(
        shared_hidden + grad_routed + grad_from_router
    )
    grad_middle, grad_ffn_gain, branch_all, expert_grads, (result, shared_grads) = branch_sum(
        grad_hidden_part.reshape(groups_local, TOK_DEV, D),
        middle,
        full_ffn_gain[None],
        grad_out[0],
        expert_partials,
        local_experts,
        [result.reshape(-1, D), shared_grads],
    )
    shared_grads = wide(lax.psum_scatter(shared_grads, PLANE, scatter_dimension=0, tiled=True))
    routed_term = product_left(picked_low, result)
    branch_out = low(
        product_right(act_shared, shared_whole[:, 2 * shared_pad :]) + routed_term
    )
    grad_out_weight = low(
        product_left(
            branch_all.reshape(token_count, D), mixed_all.reshape(token_count, heads_local * VDIM)
        )
    )
    grad_nope, grad_rope, grad_latent, grad_key_rope, grad_latent_up = attention_back(
        branch_all,
        out_local,
        probs,
        expanded,
        query_nope,
        query_rope,
        keys,
        tiled_rope,
        up_local,
    )
    lower, upper = grad_rope[..., :rope_cols], grad_rope[..., rope_cols:]
    grad_query_raw = jnp.concatenate(
        [
            grad_nope,
            low(lower * cosine_heads + upper * sine_heads),
            low(upper * cosine_heads - lower * sine_heads),
        ],
        axis=-1,
    )
    grad_key_rope = jnp.sum(
        grad_key_rope.reshape(groups_local, key_count, 2, heads_local, half_rope), axis=3
    ).reshape(groups_local, key_count, ROPE)
    grad_keys = jnp.concatenate([grad_latent, grad_key_rope], axis=-1)
    grad_keys = grad_keys.reshape(groups_local, contexts + 1, PROMPT_DEV, down_cols)

    def keys_of(mask):
        return lax.dynamic_index_in_dim(
            grad_keys, jnp.bitwise_xor(context_index, mask), 1, keepdims=False
        )

    prompt_sum = keys_of(0)
    for mask in range(1, contexts):
        prompt_sum = prompt_sum + wide(swap(low(keys_of(mask)), CONTEXT_AXIS, mask))
    grad_packed = jnp.concatenate([prompt_sum, grad_keys[:, contexts]], axis=1)
    _, pack_back = jax.vjp(pack_latent, compressed, wide(full_latent_gain))
    grad_compressed, grad_latent_gain = pack_back(grad_packed)
    grad_first = jnp.concatenate(
        [
            grad_query_raw,
            low(grad_compressed),
            jnp.zeros((groups_local, TOK_DEV, first_full.shape[1] - used_cols), jnp.bfloat16),
        ],
        axis=-1,
    )
    grad_normed_part = low(against_rows(grad_first, first_full))

    first_back = product_left(
        normed_all.reshape(token_count, D), grad_first.reshape(token_count, first_full.shape[1])
    )
    gain_rows = jnp.concatenate(
        [
            jnp.zeros((plane_count, 1, shard_rows), jnp.float32),
            grad_ffn_gain.reshape(plane_count, 1, shard_rows),
            jnp.pad(
                grad_latent_gain.reshape(plane_count, 1, latent_rows),
                ((0, 0), (0, 0), (0, shard_rows - latent_rows)),
            ),
            grad_router.reshape(experts_all, plane_count, shard_rows).transpose(1, 0, 2),
            jnp.zeros((plane_count, -(3 + experts_all) % 8, shard_rows), jnp.float32),
        ],
        axis=1,
    )
    block_out = low(
        middle + axis_scatter(branch_out.reshape(groups_local, TOK_DEV, D), EXPERT_AXIS)
    )
    (grad_tokens, gain_sum, down_own), sums = closing(
        grad_normed_part,
        block_out,
        tokens[0],
        full_attn_gain[None],
        grad_middle,
        gain_rows,
        [low(first_back), low(grad_latent_up), grad_out_weight],
        query_cols // 128 * 128,
    )
    first_sum, up_sum, out_sum = sums
    small_rows = shard_rows // groups_local
    small_own = lax.dynamic_slice_in_dim(gain_sum, expert_index * small_rows, small_rows, 1)
    latent_small = latent_rows // groups_local
    latent_own = lax.dynamic_slice_in_dim(gain_sum[2], expert_index * latent_small, latent_small, 0)
    down_start = query_cols % 128
    return (
        block_out[None],
        grad_tokens[None],
        small_own[0],
        query_join(first_sum[:, :query_cols]),
        down_own[:, down_start : down_start + down_cols],
        latent_own,
        up_sum,
        out_sum.T,
        small_own[1],
        small_own[3 : 3 + experts_all].T,
        shared_grads[:, :shared_cols],
        shared_grads[:, shared_pad : shared_pad + shared_cols],
        shared_grads[:, 2 * shared_pad : 2 * shared_pad + shared_cols].T,
        *expert_grads,
    )


def solution(mesh):
    in_specs = (
        P((DP_AXIS, EXPERT_AXIS), CONTEXT_AXIS, None),
        P((DP_AXIS, EXPERT_AXIS), CONTEXT_AXIS, None),
        P((DP_AXIS, EXPERT_AXIS), CONTEXT_AXIS, None),
        P((DP_AXIS, CONTEXT_AXIS)),
        P((DP_AXIS, CONTEXT_AXIS), EXPERT_AXIS),
        P((DP_AXIS, CONTEXT_AXIS), None),
        P((DP_AXIS, CONTEXT_AXIS)),
        P((DP_AXIS, CONTEXT_AXIS), EXPERT_AXIS),
        P(EXPERT_AXIS, (DP_AXIS, CONTEXT_AXIS)),
        P((DP_AXIS, CONTEXT_AXIS)),
        P((DP_AXIS, CONTEXT_AXIS), None),
        P((DP_AXIS, CONTEXT_AXIS), EXPERT_AXIS),
        P((DP_AXIS, CONTEXT_AXIS), EXPERT_AXIS),
        P(EXPERT_AXIS, (DP_AXIS, CONTEXT_AXIS)),
        P(EXPERT_AXIS, (DP_AXIS, CONTEXT_AXIS), None),
        P(EXPERT_AXIS, (DP_AXIS, CONTEXT_AXIS), None),
        P(EXPERT_AXIS, (DP_AXIS, CONTEXT_AXIS), None),
    )
    out_specs = (
        P((DP_AXIS, EXPERT_AXIS), CONTEXT_AXIS, None),
        P((DP_AXIS, EXPERT_AXIS), CONTEXT_AXIS, None),
        P((DP_AXIS, CONTEXT_AXIS, EXPERT_AXIS)),
        P((DP_AXIS, CONTEXT_AXIS), EXPERT_AXIS),
        P((DP_AXIS, CONTEXT_AXIS, EXPERT_AXIS), None),
        P((DP_AXIS, CONTEXT_AXIS, EXPERT_AXIS)),
        P((DP_AXIS, CONTEXT_AXIS), EXPERT_AXIS),
        P(EXPERT_AXIS, (DP_AXIS, CONTEXT_AXIS)),
        P((DP_AXIS, CONTEXT_AXIS, EXPERT_AXIS)),
        P((DP_AXIS, CONTEXT_AXIS, EXPERT_AXIS), None),
        P((DP_AXIS, CONTEXT_AXIS), EXPERT_AXIS),
        P((DP_AXIS, CONTEXT_AXIS), EXPERT_AXIS),
        P(EXPERT_AXIS, (DP_AXIS, CONTEXT_AXIS)),
        P(EXPERT_AXIS, (DP_AXIS, CONTEXT_AXIS), None),
        P(EXPERT_AXIS, (DP_AXIS, CONTEXT_AXIS), None),
        P(EXPERT_AXIS, (DP_AXIS, CONTEXT_AXIS), None),
    )
    return jax.shard_map(body, mesh=mesh, in_specs=in_specs, out_specs=out_specs, check_vma=False)
```

```python
import jax
import jax.numpy as jnp
from jax import lax
from jax.experimental import pallas as pl
from jax.experimental.pallas import tpu as pltpu
from jax.experimental.layout import Layout, with_layout_constraint
from jax.sharding import PartitionSpec as P

D = 2048
NOPE = 128
ROPE = 64
VDIM = 128
LATENT = 512
TOPK = 6
PROMPT_DEV = 64
CONT_LEN = 64
TOK_DEV = 128


epsilon = 1e-06


def norm_rows(values, scale_gain):
    return (
        values * lax.rsqrt(jnp.mean(values * values, axis=-1, keepdims=True) + epsilon) * scale_gain
    )


def rotary_tables(places, half_size):
    frequency = 10000.0 ** (-jnp.arange(half_size, dtype=jnp.float32) / half_size)
    angles = places[:, None] * frequency[None, :]
    return (jnp.cos(angles), jnp.sin(angles))


def rotate(values, cosine, sine_part):
    half_size = values.shape[-1] // 2
    lower_half = values[..., :half_size]
    upper_half = values[..., half_size:]
    return jnp.concatenate(
        [
            lower_half * cosine - upper_half * sine_part,
            upper_half * cosine + lower_half * sine_part,
        ],
        axis=-1,
    )


def product(left_side, right_side):
    return jnp.dot(left_side, right_side, preferred_element_type=jnp.float32)


def product_left(left_side, right_side):
    return lax.dot_general(
        left_side, right_side, (((0,), (0,)), ((), ())), preferred_element_type=jnp.float32
    )


def product_right(left_side, right_side):
    return lax.dot_general(
        left_side, right_side, (((1,), (1,)), ((), ())), preferred_element_type=jnp.float32
    )


def against_rows(left_side, right_side):
    return lax.dot_general(
        left_side,
        right_side,
        (((left_side.ndim - 1,), (1,)), ((), ())),
        preferred_element_type=jnp.float32,
    )


DP_AXIS, CONTEXT_AXIS, EXPERT_AXIS = "dp", "context", "expert"
PLANE = (DP_AXIS, CONTEXT_AXIS)


def swap(values, axis, mask):
    count = lax.axis_size(axis)
    return lax.ppermute(values, axis, [(i, i ^ mask) for i in range(count)])


def place_pieces(pieces, index, count):
    first = pieces[0]
    whole = jnp.zeros((count,) + first.shape, first.dtype)
    for mask, piece in pieces.items():
        whole = lax.dynamic_update_slice(whole, piece[None], (index ^ mask,) + (0,) * first.ndim)
    return with_layout_constraint(whole, Layout(tuple(range(whole.ndim))))


def low(values):
    return values.astype(jnp.bfloat16)


def wide(values):
    return values.astype(jnp.float32)


def axis_gather(values, axis):
    count = lax.axis_size(axis)
    pieces = {mask: swap(values, axis, mask) if mask else values for mask in range(count)}
    return place_pieces(pieces, lax.axis_index(axis), count)


def axis_scatter(blocks, axis):
    count = lax.axis_size(axis)
    index = lax.axis_index(axis)

    def part(mask):
        return lax.dynamic_index_in_dim(blocks, index ^ mask, 0, keepdims=False)

    total = wide(part(0))
    for mask in range(1, count):
        total = total + wide(swap(low(part(mask)), axis, mask))
    return total


MESH_ID = pl.DeviceIdType.MESH
ANY = pl.BlockSpec(memory_space=pl.ANY)
INSIDE = pl.BlockSpec(memory_space=pltpu.VMEM)


def plane_here():
    return lax.axis_index(DP_AXIS) * lax.axis_size(CONTEXT_AXIS) + lax.axis_index(CONTEXT_AXIS)


def plane_device(mask):
    contexts = lax.axis_size(CONTEXT_AXIS)
    other = jnp.bitwise_xor(plane_here(), mask)
    return {DP_AXIS: other // contexts, CONTEXT_AXIS: lax.rem(other, contexts)}


def line_device(offset):
    return {EXPERT_AXIS: lax.axis_index(EXPERT_AXIS) + offset}


def signal(device):
    pl.semaphore_signal(
        pltpu.get_barrier_semaphore(), inc=1, device_id=device, device_id_type=MESH_ID
    )


def meet(masks, line):
    count = len(masks)
    for mask in masks:
        signal(plane_device(mask))
    if line:
        place, last = lax.axis_index(EXPERT_AXIS), lax.axis_size(EXPERT_AXIS) - 1
        pl.when(place > 0)(lambda: signal(line_device(-1)))
        pl.when(place < last)(lambda: signal(line_device(1)))
        count = count + jnp.where(place > 0, 1, 0) + jnp.where(place < last, 1, 0)
    pl.semaphore_wait(pltpu.get_barrier_semaphore(), count)


def remote(source, target, send, recv, device):
    return pltpu.make_async_remote_copy(
        src_ref=source,
        dst_ref=target,
        send_sem=send,
        recv_sem=recv,
        device_id=device,
        device_id_type=MESH_ID,
    )


def arrived(target, send, recv):
    remote(target, target, send, recv, plane_device(1)).wait_recv()


def run_tasks(*tasks):
    active = list(tasks)
    while active:
        for task in list(active):
            if next(task, None) is None:
                active.remove(task)


def plane_gather_task(source, target, own, send, recv):
    rows = source.shape[0]
    half = rows // 2
    here = plane_here()

    def slot(mask, first=0, count=rows):
        start = pl.multiple_of(jnp.bitwise_xor(here, mask) * rows + first, 16)
        return target.at[pl.ds(start, count)]

    def go(number, source_ref, target_ref, mask):
        copy = remote(source_ref, target_ref, send.at[number], recv.at[number], plane_device(mask))
        copy.start()
        return copy

    def got(number, ref):
        arrived(ref, send.at[number], recv.at[number])

    local = pltpu.make_async_copy(source, slot(0), own)
    copies = [go(0, source, slot(0), 2), go(1, source, slot(0), 4)]
    yield 1
    copies.append(go(4, source, slot(0), 1))
    local.start()
    yield 1
    got(0, slot(2))
    copies.append(go(2, slot(2, 0, half), slot(2, 0, half), 4))
    copies.append(go(5, slot(2), slot(2), 1))
    yield 1
    got(1, slot(4))
    copies.append(go(3, slot(4, half, half), slot(4, half, half), 2))
    copies.append(go(6, slot(4), slot(4), 1))
    yield 1
    got(2, slot(6, 0, half))
    copies.append(go(7, slot(6, 0, half), slot(6, 0, half), 1))
    yield 1
    got(3, slot(6, half, half))
    copies.append(go(8, slot(6, half, half), slot(6, half, half), 1))
    yield 1
    got(4, slot(1))
    got(5, slot(3))
    got(6, slot(5))
    got(7, slot(7, 0, half))
    got(8, slot(7, half, half))
    local.wait()
    for copy in copies:
        copy.wait_send()


def expert_fetch_task(source, target, stage, own, send, recv):
    if source.shape[0] == 1:
        load = pltpu.make_async_copy(source.at[0], stage, own)
        load.start()
        load.wait()
        yield from plane_gather_task(stage, target, own, send, recv)
        return
    rows = source.shape[1]
    here = plane_here()
    expert_own = here // 2

    def slot(mask):
        start = pl.multiple_of(jnp.bitwise_xor(here, mask) * rows, 16)
        return target.at[pl.ds(start, rows)]

    def go(number, source_ref, target_ref, mask):
        copy = remote(source_ref, target_ref, send.at[number], recv.at[number], plane_device(mask))
        copy.start()
        return copy

    def got(number, ref):
        arrived(ref, send.at[number], recv.at[number])

    copies = []
    for k in (3, 1, 2):
        copies.append(go(k, source.at[jnp.bitwise_xor(expert_own, k)], slot(0), 2 * k))
    load = pltpu.make_async_copy(source.at[expert_own], stage, own)
    load.start()
    yield 1
    load.wait()
    local = pltpu.make_async_copy(stage, slot(0), own)
    local.start()
    copies.append(go(0, stage, slot(0), 1))
    for k in (1, 2, 3):
        yield 1
        got(k, slot(2 * k))
        copies.append(go(4 + k, slot(2 * k), slot(2 * k), 1))
    yield 1
    got(0, slot(1))
    for k in (1, 2, 3):
        got(4 + k, slot(2 * k + 1))
    local.wait()
    for copy in copies:
        copy.wait_send()


LINE_PARTS = 4


def line_gather_steps(target, send, recv, rows):
    place, count = lax.axis_index(EXPERT_AXIS), lax.axis_size(EXPERT_AXIS)
    part = rows // LINE_PARTS

    def piece(block, c):
        return target.at[block, pl.ds(c * part, part)]

    def copy(way, distance, c, source=None):
        block = place - way * distance
        ref = piece(block, c)
        return remote(
            ref if source is None else source,
            ref,
            send.at[(way + 1) // 2, distance, c],
            recv.at[(way + 1) // 2, distance, c],
            line_device(way),
        )

    def has_next(way):
        return place < count - 1 if way == 1 else place > 0

    def has_block(way, distance):
        return place - distance >= 0 if way == 1 else place + distance < count

    def begin(c, source):
        for way in (1, -1):
            pl.when(has_next(way))(lambda way=way: copy(way, 0, c, source).start())

    def forward(c, distance):
        for way in (1, -1):

            @pl.when(has_block(way, distance))
            def _(way=way):
                ref = piece(place - way * distance, c)
                arrived(
                    ref,
                    send.at[(way + 1) // 2, distance - 1, c],
                    recv.at[(way + 1) // 2, distance - 1, c],
                )
                if distance < count - 1:
                    pl.when(has_next(way))(lambda: copy(way, distance, c).start())

    def finish(source):
        for c in range(LINE_PARTS):
            for way in (1, -1):
                for distance in range(count - 1):

                    @pl.when(jnp.logical_and(has_next(way), has_block(way, distance)))
                    def _(way=way, distance=distance, c=c):
                        copy(way, distance, c, source(c) if distance == 0 else None).wait_send()

    return begin, forward, finish


def line_gather_task(source, target, own, send, recv):
    rows = source.shape[0]
    part = rows // LINE_PARTS
    count = lax.axis_size(EXPERT_AXIS)
    begin, forward, finish = line_gather_steps(target, send, recv, rows)
    local = pltpu.make_async_copy(source, target.at[lax.axis_index(EXPERT_AXIS)], own)
    for c in range(LINE_PARTS):
        begin(c, source.at[pl.ds(c * part, part)])
    local.start()
    yield 1
    for distance in range(1, count):
        for c in range(LINE_PARTS):
            forward(c, distance)
        yield 1
    local.wait()
    finish(lambda c: source.at[pl.ds(c * part, part)])


def line_semaphores():
    count = lax.axis_size(EXPERT_AXIS)
    return [pltpu.SemaphoreType.DMA((2, count, LINE_PARTS))] * 2


def line_reduce_steps(partial, inbox, send, recv):
    place, count = lax.axis_index(EXPERT_AXIS), lax.axis_size(EXPERT_AXIS)
    rows = partial.shape[1]
    part = rows // LINE_PARTS

    def span(c):
        return pl.ds(c * part, part)

    def box(way, distance, c):
        return inbox.at[distance if way == 1 else count - distance, span(c)]

    def copy(way, distance, c, source):
        side = (way + 1) // 2
        return remote(
            source,
            box(way, distance - 1, c),
            send.at[side, distance, c],
            recv.at[side, distance - 1, c],
            line_device(way),
        )

    def wait_inbox(way, distance, c):
        side = (way + 1) // 2
        arrived(box(way, distance, c), send.at[side, distance, c], recv.at[side, distance, c])

    def has_source(way):
        return place > 0 if way == 1 else place < count - 1

    def has_target(way, distance):
        return place + distance < count if way == 1 else place - distance >= 0

    def step(c, distance):
        for way in (1, -1):
            mine = partial.at[place + way * distance, span(c)]

            def pass_on(way=way, mine=mine):
                came = box(way, distance, c)
                wait_inbox(way, distance, c)
                came[...] = low(wide(mine[...]) + wide(came[...]))
                copy(way, distance, c, came).start()

            def send_first(way=way, mine=mine):
                copy(way, distance, c, mine).start()

            valid = has_target(way, distance)
            if distance < count - 1:
                pl.when(jnp.logical_and(valid, has_source(way)))(pass_on)
                pl.when(jnp.logical_and(valid, jnp.logical_not(has_source(way))))(send_first)
            else:
                pl.when(valid)(send_first)

    def total(c, result):
        result[span(c)] = result[span(c)] + wide(partial[place, span(c)])
        for way in (1, -1):

            @pl.when(has_source(way))
            def _(way=way):
                wait_inbox(way, 0, c)
                result[span(c)] = result[span(c)] + wide(box(way, 0, c)[...])

    def stages(result, done):
        for t in range(LINE_PARTS + count - 1):
            for c in range(LINE_PARTS):
                distance = count - 1 - (t - c)
                if 1 <= distance <= count - 1:
                    step(c, distance)
                elif distance == 0:
                    total(c, result)
                    done(span(c), c)
            yield 1

    def finish():
        for c in range(LINE_PARTS):
            for way in (1, -1):
                for distance in range(1, count):
                    pl.when(has_target(way, distance))(
                        lambda way=way, distance=distance, c=c: copy(
                            way, distance, c, partial.at[place + way * distance, span(c)]
                        ).wait_send()
                    )

    return stages, finish


def gather_semaphores():
    return [
        pltpu.SemaphoreType.DMA(()),
        pltpu.SemaphoreType.DMA((9,)),
        pltpu.SemaphoreType.DMA((9,)),
    ]


def kernel_params(number):
    return pltpu.CompilerParams(
        collective_id=number,
        has_side_effects=True,
        vmem_limit_bytes=(52 if lax.axis_size(EXPERT_AXIS) <= 4 else 60) << 20,
    )


def opening(tokens, gains, matrices):
    count = lax.axis_size(EXPERT_AXIS)
    rows, width = tokens.shape
    number = len(matrices)
    planes = lax.axis_size(PLANE)
    depth = gains.shape[1]

    def kernel(*refs):
        tokens_ref, gains_ref = refs[:2]
        sources = refs[2 : 2 + number]
        gains_all, normed_all = refs[2 + number : 4 + number]
        targets = refs[4 + number : 4 + 2 * number]
        scratch = list(refs[4 + 2 * number :])
        normed, gain_box, gain_send, gain_recv = scratch[:4]
        line = scratch[4:7]
        semaphores = scratch[7:]
        meet(range(1, planes), True)
        here = plane_here()
        sends = []
        for mask in range(1, planes):
            copy = remote(
                gains_ref,
                gain_box.at[here],
                gain_send.at[mask],
                gain_recv.at[mask],
                plane_device(mask),
            )
            copy.start()
            sends.append(copy)
        tasks = [
            plane_gather_task(sources[i], targets[i], *semaphores[3 * i : 3 * i + 3])
            for i in range(number)
        ]
        for task in tasks:
            next(task)
        for task in tasks:
            next(task)
        gain_box[here] = gains_ref[...]
        values = wide(tokens_ref[...])
        scale = lax.rsqrt(jnp.mean(values * values, axis=-1, keepdims=True) + epsilon)
        for mask in range(1, planes):
            other = gain_box.at[jnp.bitwise_xor(here, mask)]
            arrived(other, gain_send.at[mask], gain_recv.at[mask])
        for i in range(planes):
            columns = slice(i * depth, (i + 1) * depth)
            normed[:, columns] = low(
                wide(tokens_ref[:, columns]) * scale * gain_box[i, 0:1, :]
            )
        gains_all[...] = gain_box[...]
        rows_task = line_gather_task(normed, normed_all, *line)
        next(rows_task)
        next(rows_task)
        for task in tasks:
            next(task)
        for task in tasks:
            next(task)
        run_tasks(rows_task, *tasks)
        for copy in sends:
            copy.wait_send()

    shapes = [
        jax.ShapeDtypeStruct((planes,) + gains.shape, jnp.float32),
        jax.ShapeDtypeStruct((count, rows, width), jnp.bfloat16),
    ] + [jax.ShapeDtypeStruct((planes * m.shape[0], m.shape[1]), m.dtype) for m in matrices]
    scratch = [
        pltpu.VMEM((rows, width), jnp.bfloat16),
        pltpu.VMEM((planes,) + gains.shape, jnp.float32),
        pltpu.SemaphoreType.DMA((planes,)),
        pltpu.SemaphoreType.DMA((planes,)),
        pltpu.SemaphoreType.DMA(()),
    ]
    scratch += line_semaphores()
    for _ in matrices:
        scratch += gather_semaphores()
    results = pl.pallas_call(
        kernel,
        out_shape=shapes,
        in_specs=[INSIDE] * (2 + number),
        out_specs=[INSIDE, ANY] + [ANY] * number,
        scratch_shapes=scratch,
        compiler_params=kernel_params(1),
        cost_estimate=pl.CostEstimate(
            flops=60_000_000, bytes_accessed=150_000_000, transcendentals=0
        ),
        name="opening",
    )(tokens, gains, *matrices)
    return results[0], results[1], results[2:]


def head_mask(head, heads, rope):
    lanes = lax.broadcasted_iota(jnp.int32, (1, rope), 1)
    return jnp.where(lax.rem(lanes, rope // 2) // (ROPE // 2) == head, 1.0, 0.0)


def middle_sum(query_nope, query_rope, keys, tiled, up, out, source, gain, experts, grads):
    count, rows = query_nope.shape[:2]
    key_count, rope = keys.shape[1], query_rope.shape[2]
    heads = query_nope.shape[2] // NOPE
    width = source.shape[1]
    planes, contexts = lax.axis_size(PLANE), lax.axis_size(CONTEXT_AXIS)
    routed = len(experts)
    score_scale = (NOPE + ROPE) ** (-0.5)

    def kernel(*refs):
        nope_ref, rope_ref, keys_ref, tiled_ref, up_ref, out_ref, source_ref, gain_ref = refs[:8]
        expert_refs = refs[8 : 8 + routed]
        grads_ref = refs[8 + routed]
        outputs = refs[9 + routed :]
        middle_ref, hidden_all, grads_all, mixed, probs, expanded = outputs[:6]
        targets = outputs[6 : 6 + routed]
        scratch = list(outputs[6 + routed :])
        grads_line = [scratch.pop() for _ in range(3)][::-1]
        partial_ref = scratch.pop(0)
        inbox, hidden, reduce_send, reduce_recv, own, line_send, line_recv = scratch[:7]
        stages = scratch[7 : 7 + routed]
        semaphores = scratch[7 + routed :]
        meet((1, 2, 4, 6), True)
        reduce_stages, reduce_finish = line_reduce_steps(
            partial_ref, inbox, reduce_send, reduce_recv
        )
        begin, forward, finish = line_gather_steps(hidden_all, line_send, line_recv, rows)
        part = rows // LINE_PARTS

        def ready(span, c):
            values = middle_ref[span]
            scale = lax.rsqrt(jnp.mean(values * values, axis=-1, keepdims=True) + epsilon)
            hidden[span] = low(values * scale * gain_ref[...])
            begin(c, hidden.at[span])

        def line_task():
            middle_ref[...] = wide(source_ref[...])
            yield from reduce_stages(middle_ref, ready)
            local = pltpu.make_async_copy(hidden, hidden_all.at[lax.axis_index(EXPERT_AXIS)], own)
            local.start()
            for distance in range(1, count):
                for c in range(LINE_PARTS):
                    forward(c, distance)
                yield 1
            local.wait()
            finish(lambda c: hidden.at[pl.ds(c * part, part)])
            reduce_finish()

        tasks = [
            expert_fetch_task(
                expert_refs[i], targets[i], stages[i], *semaphores[3 * i : 3 * i + 3]
            )
            for i in range(routed)
        ]
        for task in tasks:
            next(task)
        grads_task = line_gather_task(grads_ref, grads_all, *grads_line)
        next(grads_task)
        for task in tasks:
            next(task)
        here = lax.axis_index(CONTEXT_AXIS)
        row = lax.broadcasted_iota(jnp.int32, (rows, key_count), 0)
        place = jnp.where(
            row < PROMPT_DEV,
            here * PROMPT_DEV + row,
            contexts * PROMPT_DEV + row - PROMPT_DEV,
        )
        allowed = lax.broadcasted_iota(jnp.int32, (rows, key_count), 1) <= place

        def attend(g, carry):
            expanded[g] = low(product(keys_ref[g, :, :LATENT], up_ref[...]))
            for h in range(heads):
                start = h * (NOPE + VDIM)
                scores = product_right(
                    nope_ref[g, :, h * NOPE : (h + 1) * NOPE],
                    expanded[g, :, start : start + NOPE],
                ) + product_right(
                    rope_ref[g] * low(head_mask(h, heads, rope)), tiled_ref[g]
                )
                scores = jnp.where(allowed, scores * score_scale, -1e30)
                powers = jnp.exp(scores - jnp.max(scores, axis=-1, keepdims=True))
                weights = low(powers / jnp.sum(powers, axis=-1, keepdims=True))
                probs[g, h] = weights
                mixed[g, :, h * VDIM : (h + 1) * VDIM] = low(
                    product(weights, expanded[g, :, start + NOPE : start + NOPE + VDIM])
                )
            partial_ref[g] = low(product_right(mixed[g], out_ref[...]))
            return carry

        lax.fori_loop(0, count, attend, 0)
        run_tasks(line_task())
        run_tasks(grads_task, *tasks)

    shapes = [
        jax.ShapeDtypeStruct((rows, width), jnp.float32),
        jax.ShapeDtypeStruct((count, rows, width), jnp.bfloat16),
        jax.ShapeDtypeStruct((count, rows, width), jnp.bfloat16),
        jax.ShapeDtypeStruct((count, rows, heads * VDIM), jnp.bfloat16),
        jax.ShapeDtypeStruct((count, heads, rows, key_count), jnp.bfloat16),
        jax.ShapeDtypeStruct((count, key_count, up.shape[1]), jnp.bfloat16),
    ] + [jax.ShapeDtypeStruct((planes * e.shape[1], e.shape[2]), e.dtype) for e in experts]
    scratch = [
        pltpu.VMEM((count, rows, width), jnp.bfloat16),
        pltpu.VMEM((count + 1, rows, width), jnp.bfloat16),
        pltpu.VMEM((rows, width), jnp.bfloat16),
    ]
    scratch += line_semaphores() + [pltpu.SemaphoreType.DMA(())] + line_semaphores()
    scratch += [pltpu.VMEM(e.shape[1:], e.dtype) for e in experts]
    for _ in range(routed):
        scratch += gather_semaphores()
    scratch += [pltpu.SemaphoreType.DMA(())] + line_semaphores()
    results = pl.pallas_call(
        kernel,
        out_shape=shapes,
        in_specs=[INSIDE] * 8 + [ANY] * routed + [INSIDE],
        out_specs=[INSIDE, ANY, ANY] + [INSIDE] * 3 + [ANY] * routed,
        scratch_shapes=scratch,
        compiler_params=kernel_params(2),
        cost_estimate=pl.CostEstimate(
            flops=60_000_000, bytes_accessed=300_000_000, transcendentals=0
        ),
        name="middle_sum",
    )(query_nope, query_rope, keys, tiled, up, out, source, gain, *experts, grads)
    return results[:6], results[6:]


def add_rows(target, first, second):
    def tile(i, carry):
        span = pl.ds(pl.multiple_of(i * 16, 16), 16)
        target[span] = (wide(first[span]) + wide(second[span])).astype(target.dtype)
        return carry

    lax.fori_loop(0, target.shape[0] // 16, tile, 0)


def expert_return_task(source, result, mine, came, load, send, recv):
    rows = mine.shape[1]
    here = plane_here()
    expert_own = here // 2

    def slot(mask):
        return source.at[pl.ds(pl.multiple_of(jnp.bitwise_xor(here, mask) * rows, 16), rows)]

    def go(number, source_ref, target_ref, mask):
        copy = remote(source_ref, target_ref, send.at[number], recv.at[number], plane_device(mask))
        copy.start()
        return copy

    copies, loads = [], {}

    def cross(k):
        copies.append(go(k, slot(2 * k + 1), came.at[k], 1))
        loads[k] = pltpu.make_async_copy(slot(2 * k), mine.at[k], load.at[k])
        loads[k].start()

    cross(3)
    yield 1
    for k, following in ((3, 1), (1, 2), (2, 0), (0, None)):
        if following is not None:
            cross(following)
        arrived(came.at[k], send.at[k], recv.at[k])
        loads[k].wait()
        add_rows(mine.at[k], mine.at[k], came.at[k])
        if k:
            copies.append(go(4 + k, mine.at[k], result.at[expert_own], 2 * k))
        else:
            local = pltpu.make_async_copy(mine.at[0], result.at[expert_own], load.at[0])
            local.start()
        yield 1
    for k in (3, 1, 2):
        arrived(
            result.at[jnp.bitwise_xor(expert_own, k)], send.at[4 + k], recv.at[4 + k]
        )
    local.wait()
    for copy in copies:
        copy.wait_send()


def expert_return_scratch(rows, columns):
    return [
        pltpu.VMEM((4, rows, columns), jnp.bfloat16),
        pltpu.VMEM((4, rows, columns), jnp.bfloat16),
        pltpu.SemaphoreType.DMA((4,)),
        pltpu.SemaphoreType.DMA((8,)),
        pltpu.SemaphoreType.DMA((8,)),
    ]


def plane_scatter_task(source, result, mine, came, box, last, load, send, recv):
    rows = mine.shape[1]
    half = rows // 2
    here = plane_here()
    upper, lower = pl.ds(0, half), pl.ds(half, half)

    def slot(mask):
        return source.at[pl.ds(pl.multiple_of(jnp.bitwise_xor(here, mask) * rows, 16), rows)]

    def go(number, source_ref, target_ref, mask):
        copy = remote(source_ref, target_ref, send.at[number], recv.at[number], plane_device(mask))
        copy.start()
        return copy

    def got(number, ref):
        arrived(ref, send.at[number], recv.at[number])

    copies, loads = [], {}

    def cross(k):
        copies.append(go(k, slot(2 * k + 1), came.at[k], 1))
        loads[k] = pltpu.make_async_copy(slot(2 * k), mine.at[k], load.at[k])
        loads[k].start()

    cross(3)
    yield 1
    for k, following in ((3, 1), (1, 2), (2, 0)):
        cross(following)
        got(k, came.at[k])
        loads[k].wait()
        add_rows(mine.at[k], mine.at[k], came.at[k])
        if k == 3:
            copies.append(go(4, mine.at[3, upper], box.at[0], 2))
            copies.append(go(5, mine.at[3, lower], box.at[1], 4))
        elif k == 1:
            copies.append(go(6, mine.at[1, upper], last.at[0, upper], 2))
        else:
            copies.append(go(7, mine.at[2, lower], last.at[1, lower], 4))
        yield 1
    got(4, box.at[0])
    add_rows(mine.at[2, upper], mine.at[2, upper], box.at[0])
    copies.append(go(8, mine.at[2, upper], last.at[1, upper], 4))
    yield 1
    got(5, box.at[1])
    add_rows(mine.at[1, lower], mine.at[1, lower], box.at[1])
    copies.append(go(9, mine.at[1, lower], last.at[0, lower], 2))
    yield 1
    got(0, came.at[0])
    loads[0].wait()
    add_rows(result, mine.at[0], came.at[0])
    got(6, last.at[0, upper])
    got(7, last.at[1, lower])
    yield 1
    got(9, last.at[0, lower])
    add_rows(result, result, last.at[0])
    got(8, last.at[1, upper])
    add_rows(result, result, last.at[1])
    for copy in copies:
        copy.wait_send()


def plane_scatter_scratch(rows, columns):
    return [
        pltpu.VMEM((4, rows, columns), jnp.bfloat16),
        pltpu.VMEM((4, rows, columns), jnp.bfloat16),
        pltpu.VMEM((2, rows // 2, columns), jnp.bfloat16),
        pltpu.VMEM((2, rows, columns), jnp.bfloat16),
        pltpu.SemaphoreType.DMA((4,)),
        pltpu.SemaphoreType.DMA((10,)),
        pltpu.SemaphoreType.DMA((10,)),
    ]


def norm_back(values, gain, grad):
    scale = lax.rsqrt(jnp.mean(values * values, axis=-1, keepdims=True) + epsilon)
    scaled = gain * grad
    mean = jnp.mean(values * scaled, axis=-1, keepdims=True)
    part = jnp.sum(values * scale * grad, axis=0, keepdims=True)
    return scale * scaled - values * (scale * scale * scale * mean), part


def branch_sum(partial, middle, gain, grad_out, experts, local_experts, later):
    count, rows, width = partial.shape
    planes = lax.axis_size(PLANE)
    routed, waiting = len(experts), len(later)

    def kernel(*refs):
        partial_ref, middle_ref, gain_ref, grad_ref = refs[:4]
        expert_refs = refs[4 : 4 + routed]
        outputs = refs[4 + routed + waiting :]
        grad_middle, grad_gain, branch_all = outputs[:3]
        results = outputs[3 : 3 + routed]
        scratch = list(outputs[3 + routed + waiting :])
        inbox, branch, reduce_send, reduce_recv, own, line_send, line_recv = scratch[:7]
        rest = scratch[7:]
        meet((1, 2, 4, 6), True)
        reduce_stages, reduce_finish = line_reduce_steps(
            partial_ref, inbox, reduce_send, reduce_recv
        )
        begin, forward, finish = line_gather_steps(branch_all, line_send, line_recv, rows)
        part = rows // LINE_PARTS

        def ready(span, c):
            back, gain_part = norm_back(middle_ref[span], gain_ref[...], grad_middle[span])
            grad_gain[...] = gain_part if c == 0 else grad_gain[...] + gain_part
            back = wide(grad_ref[span]) + back
            grad_middle[span] = back
            branch[span] = low(back)
            begin(c, branch.at[span])

        def line_task():
            grad_middle[...] = jnp.zeros((rows, width), jnp.float32)
            yield from reduce_stages(grad_middle, ready)
            local = pltpu.make_async_copy(branch, branch_all.at[lax.axis_index(EXPERT_AXIS)], own)
            local.start()
            for distance in range(1, count):
                for c in range(LINE_PARTS):
                    forward(c, distance)
                yield 1
            local.wait()
            finish(lambda c: branch.at[pl.ds(c * part, part)])
            reduce_finish()

        task_kind = plane_scatter_task if local_experts == 1 else expert_return_task
        size = len(rest) // routed
        tasks = [
            task_kind(
                expert_refs[i], results[i], *rest[size * i : size * (i + 1)]
            )
            for i in range(routed)
        ]
        line = line_task()
        for stage in range(5):
            for task in tasks:
                next(task)
            if stage:
                next(line)
        run_tasks(line)
        run_tasks(*tasks)

    shapes = [
        jax.ShapeDtypeStruct((rows, width), jnp.float32),
        jax.ShapeDtypeStruct((1, width), jnp.float32),
        jax.ShapeDtypeStruct((count, rows, width), jnp.bfloat16),
    ]
    scratch = [
        pltpu.VMEM((count + 1, rows, width), jnp.bfloat16),
        pltpu.VMEM((rows, width), jnp.bfloat16),
    ]
    scratch += line_semaphores() + [pltpu.SemaphoreType.DMA(())] + line_semaphores()
    for expert in experts:
        shard, columns = expert.shape[0] // planes, expert.shape[1]
        if local_experts == 1:
            shapes.append(jax.ShapeDtypeStruct((shard, columns), jnp.float32))
            scratch += plane_scatter_scratch(shard, columns)
        else:
            shapes.append(jax.ShapeDtypeStruct((local_experts, shard, columns), jnp.bfloat16))
            scratch += expert_return_scratch(shard, columns)
    shapes += [jax.ShapeDtypeStruct(x.shape, x.dtype) for x in later]
    results = pl.pallas_call(
        kernel,
        out_shape=shapes,
        in_specs=[INSIDE] * 4 + [ANY] * (routed + waiting),
        out_specs=[INSIDE, INSIDE, ANY]
        + [INSIDE if local_experts == 1 else ANY] * routed
        + [ANY] * waiting,
        input_output_aliases={4 + routed + i: 3 + routed + i for i in range(waiting)},
        scratch_shapes=scratch,
        compiler_params=kernel_params(3),
        cost_estimate=pl.CostEstimate(
            flops=60_000_000, bytes_accessed=300_000_000, transcendentals=0
        ),
        name="branch_sum",
    )(partial, middle, gain, grad_out, *experts, *later)
    grads = [
        wide(r).reshape((local_experts,) + r.shape[-2:]) for r in results[3 : 3 + routed]
    ]
    return results[0], results[1][0], results[2], grads, results[3 + routed :]


def meet_all():
    planes, count = lax.axis_size(PLANE), lax.axis_size(EXPERT_AXIS)
    for mask in range(1, planes):
        signal(plane_device(mask))
    for mask in range(1, count):
        signal({EXPERT_AXIS: jnp.bitwise_xor(lax.axis_index(EXPERT_AXIS), mask)})
    pl.semaphore_wait(pltpu.get_barrier_semaphore(), planes + count - 2)


def closing(grad_first, first_full, normed, ready_before, source, gain, grad_middle, gain_grads, matrices, spread):
    rows, width = source.shape
    count = lax.axis_size(EXPERT_AXIS)
    planes = lax.axis_size(PLANE)
    number = len(matrices) + 1
    sizes = [first_full.shape] + [m.shape for m in matrices]
    depth = gain_grads.shape[2]
    shard, columns = first_full.shape[0] // planes, first_full.shape[1]
    thin = shard // count

    def kernel(*refs):
        first_ref, full_ref, normed_ref, _, source_ref, gain_ref, middle_ref, gains_ref = refs[:8]
        sources = list(refs[8 : 7 + number])
        grad_tokens, gains_out, thin_out = refs[7 + number : 10 + number]
        results = refs[10 + number : 10 + 2 * number]
        scratch = list(refs[10 + 2 * number :])
        partial_ref, back_ref = scratch.pop(), scratch.pop()
        sources = [back_ref] + sources
        inbox, reduce_send, reduce_recv, gain_row = scratch[:4]
        gain_part, gain_box, gain_send, gain_recv = scratch[4:8]
        gain_held, gain_far, far_send, far_recv, thin_box, thin_send, thin_recv = scratch[8:15]
        rest = scratch[15:]
        meet_all()
        place = lax.axis_index(EXPERT_AXIS)
        here = plane_here()
        reduce_stages, reduce_finish = line_reduce_steps(
            partial_ref, inbox, reduce_send, reduce_recv
        )

        def ready(span, c):
            back, row = norm_back(wide(source_ref[span]), gain_ref[...], grad_tokens[span])
            gain_row[...] = row if c == 0 else gain_row[...] + row
            grad_tokens[span] = middle_ref[span] + back

        def line_task():
            grad_tokens[...] = jnp.zeros((rows, width), jnp.float32)
            yield from reduce_stages(grad_tokens, ready)
            gain_part[...] = gains_ref[...]
            for i in range(planes):
                gain_part[i, 0:1, :] = gain_row[:, i * depth : (i + 1) * depth]
            copies = []
            for mask in range(1, planes):
                copy = remote(
                    gain_part.at[jnp.bitwise_xor(here, mask)],
                    gain_box.at[mask],
                    gain_send.at[mask],
                    gain_recv.at[mask],
                    plane_device(mask),
                )
                copy.start()
                copies.append(copy)
            gain_total = gain_part[here]
            yield 1
            for mask in range(1, planes):
                arrived(gain_box.at[mask], gain_send.at[mask], gain_recv.at[mask])
                gain_total = gain_total + gain_box[mask]
            gain_held[...] = gain_total
            for mask in range(1, count):
                copy = remote(
                    gain_held,
                    gain_far.at[mask],
                    far_send.at[mask],
                    far_recv.at[mask],
                    {EXPERT_AXIS: jnp.bitwise_xor(place, mask)},
                )
                copy.start()
                copies.append(copy)
            yield 1
            for mask in range(1, count):
                arrived(gain_far.at[mask], far_send.at[mask], far_recv.at[mask])
                gain_total = gain_total + gain_far[mask]
            gains_out[...] = gain_total
            for copy in copies:
                copy.wait_send()
            reduce_finish()

        def first_task(task):
            yield from task
            copies = []

            def piece(mask):
                start = pl.multiple_of(jnp.bitwise_xor(place, mask) * thin, 8 if thin % 8 == 0 else thin)
                return results[0].at[pl.ds(start, thin), pl.ds(spread, columns - spread)]

            for mask in range(1, count):
                copy = remote(
                    piece(mask),
                    thin_box.at[mask],
                    thin_send.at[mask],
                    thin_recv.at[mask],
                    {EXPERT_AXIS: jnp.bitwise_xor(place, mask)},
                )
                copy.start()
                copies.append(copy)
            yield 1
            total = piece(0)[...]
            for mask in range(1, count):
                arrived(thin_box.at[mask], thin_send.at[mask], thin_recv.at[mask])
                total = total + thin_box[mask]
            thin_out[...] = total
            for copy in copies:
                copy.wait_send()

        size = len(rest) // number
        tasks = [
            plane_scatter_task(sources[i], results[i], *rest[size * i : size * (i + 1)])
            for i in range(number)
        ]
        tasks[0] = first_task(tasks[0])
        for task in tasks[1:]:
            next(task)

        def back_tile(i, carry):
            span = pl.ds(pl.multiple_of(i * 256, 256), 256)
            back_ref[span] = low(product_left(normed_ref[:, span], first_ref[...]))
            return carry

        lax.fori_loop(0, width // 256, back_tile, 0)
        for task in tasks:
            next(task)

        def partial_tile(i, carry):
            span = pl.ds(pl.multiple_of(i * 2 * rows, 2 * rows), 2 * rows)
            tile = low(product_right(first_ref[span], full_ref[...]))
            partial_ref[2 * i] = tile[:rows]
            partial_ref[2 * i + 1] = tile[rows:]
            return carry

        lax.fori_loop(0, count // 2, partial_tile, 0)
        line = line_task()
        for stage in range(5):
            for task in tasks if stage < 4 else tasks[:1]:
                next(task)
            next(line)
        run_tasks(line, *tasks)

    shapes = [
        jax.ShapeDtypeStruct((rows, width), jnp.float32),
        jax.ShapeDtypeStruct(gain_grads.shape[1:], jnp.float32),
        jax.ShapeDtypeStruct((thin, columns - spread), jnp.float32),
    ] + [jax.ShapeDtypeStruct((m[0] // planes, m[1]), jnp.float32) for m in sizes]
    scratch = [pltpu.VMEM((count + 1, rows, width), jnp.bfloat16)]
    scratch += line_semaphores()
    scratch += [
        pltpu.VMEM((1, width), jnp.float32),
        pltpu.VMEM(gain_grads.shape, jnp.float32),
        pltpu.VMEM(gain_grads.shape, jnp.float32),
        pltpu.SemaphoreType.DMA((planes,)),
        pltpu.SemaphoreType.DMA((planes,)),
        pltpu.VMEM(gain_grads.shape[1:], jnp.float32),
        pltpu.VMEM((count,) + gain_grads.shape[1:], jnp.float32),
        pltpu.SemaphoreType.DMA((count,)),
        pltpu.SemaphoreType.DMA((count,)),
        pltpu.VMEM((count, thin, columns - spread), jnp.float32),
        pltpu.SemaphoreType.DMA((count,)),
        pltpu.SemaphoreType.DMA((count,)),
    ]
    for m in sizes:
        scratch += plane_scatter_scratch(m[0] // planes, m[1])
    scratch += [
        pltpu.VMEM(first_full.shape, jnp.bfloat16),
        pltpu.VMEM((count, rows, width), jnp.bfloat16),
    ]
    results = pl.pallas_call(
        kernel,
        out_shape=shapes,
        in_specs=[INSIDE] * 3 + [ANY] + [INSIDE] * 4 + [ANY] * len(matrices),
        out_specs=[INSIDE] * (3 + number),
        scratch_shapes=scratch,
        compiler_params=kernel_params(4),
        cost_estimate=pl.CostEstimate(
            flops=60_000_000, bytes_accessed=200_000_000, transcendentals=0
        ),
        name="closing",
    )(grad_first, first_full, normed, ready_before, source, gain, grad_middle, gain_grads, *matrices)
    return results[:3], results[3:]


def silu_back(gate, up, grad):
    sigmoid_part = 1.0 / (1.0 + jnp.exp(-gate))
    silu_part = gate * sigmoid_part
    slope = sigmoid_part * (1.0 + gate * (1.0 - sigmoid_part))
    return silu_part * up, grad * up * slope, grad * silu_part


def row_copies(source, target, send, recv, copies):
    return [
        remote(source(k), target(k), send.at[k], recv.at[k], plane_device(k * copies))
        for k in (3, 1, 2)
    ]


def shared_and_rows(hidden, grads, weights, hidden_slots, grad_slots, gates, copies):
    tokens, width = hidden.shape
    columns = weights.shape[1] // 3
    pieces, slots = hidden_slots.shape[:2]
    exchanged = copies > 0
    tall = max(t for t in (256, 128, tokens) if tokens % t == 0)
    wide_part = 256

    def kernel(*refs):
        hidden_any, grads_any, weights_any, rows_any, grad_rows_any, gates_ref = refs[:6]
        act_out, back_out, weight_grads = refs[6:9]
        outputs = refs[9:12]
        scratch = refs[12:] if exchanged else refs[9:]
        hid, grd, wts, both, load = scratch[:5]
        loads = [
            pltpu.make_async_copy(hidden_any, hid, load.at[0]),
            pltpu.make_async_copy(weights_any, wts, load.at[1]),
            pltpu.make_async_copy(grads_any, grd, load.at[2]),
        ]
        moves = []
        if exchanged:
            semaphores = scratch[5:]
            meet([k * copies for k in (1, 2, 3)], False)
            for i, source in enumerate((gates_ref, rows_any, grad_rows_any)):
                moves += row_copies(
                    lambda k, source=source: source.at[k],
                    lambda k, i=i: outputs[i].at[k - 1],
                    semaphores[2 * i],
                    semaphores[2 * i + 1],
                    copies,
                )
            for move in moves:
                move.start()
        for copy in loads:
            copy.start()
        for copy in loads:
            copy.wait()

        def rows_tile(i, carry):
            span = pl.ds(pl.multiple_of(i * tall, 16), tall)
            gate = product(hid[span], wts[:, :columns])
            up = product(hid[span], wts[:, columns : 2 * columns])
            grad = product(grd[span], wts[:, 2 * columns :])
            act, dgate, dup = silu_back(gate, up, grad)
            act_out[span] = low(act)
            both[span, :columns] = low(dgate)
            both[span, columns:] = low(dup)
            back_out[span] = product_right(both[span], wts[:, : 2 * columns])
            return carry

        lax.fori_loop(0, tokens // tall, rows_tile, 0)

        def weights_tile(i, carry):
            span = pl.ds(pl.multiple_of(i * wide_part, wide_part), wide_part)
            weight_grads[span, : 2 * columns] = low(product_left(hid[:, span], both[...]))
            weight_grads[span, 2 * columns :] = low(product_left(grd[:, span], act_out[...]))
            return carry

        lax.fori_loop(0, width // wide_part, weights_tile, 0)
        for move in moves:
            move.wait()

    shapes = [
        jax.ShapeDtypeStruct((tokens, columns), jnp.bfloat16),
        jax.ShapeDtypeStruct((tokens, width), jnp.float32),
        jax.ShapeDtypeStruct(weights.shape, jnp.bfloat16),
    ]
    out_specs = [INSIDE] * 3
    scratch = [
        pltpu.VMEM(hidden.shape, jnp.bfloat16),
        pltpu.VMEM(grads.shape, jnp.bfloat16),
        pltpu.VMEM(weights.shape, jnp.bfloat16),
        pltpu.VMEM((tokens, 2 * columns), jnp.bfloat16),
        pltpu.SemaphoreType.DMA((3,)),
    ]
    if exchanged:
        shapes += [jax.ShapeDtypeStruct((3,) + x.shape[1:], x.dtype) for x in (gates, hidden_slots, grad_slots)]
        out_specs += [INSIDE, ANY, ANY]
        scratch += [pltpu.SemaphoreType.DMA((4,))] * 6
    results = pl.pallas_call(
        kernel,
        out_shape=shapes,
        in_specs=[ANY] * 5 + [INSIDE],
        out_specs=out_specs,
        scratch_shapes=scratch,
        compiler_params=kernel_params(5) if exchanged else pltpu.CompilerParams(vmem_limit_bytes=60 << 20),
        cost_estimate=pl.CostEstimate(
            flops=12 * tokens * width * columns, bytes_accessed=120_000_000, transcendentals=0
        ),
        name="shared_and_rows",
    )(hidden, grads, weights, hidden_slots, grad_slots, gates)
    return results[:3], results[3:]


def routed_expert(hidden_slots, grad_slots, hidden_far, grad_far, gates, weights, copies):
    slots, width = hidden_slots.shape[1:]
    gate_full, up_full, down_full = weights
    units = gate_full.shape[1]
    exchanged = copies > 0

    def kernel(*refs):
        far = 2 if exchanged else 0
        hidden_any, grad_any = refs[:2]
        hidden_far_any, grad_far_any = refs[2:4] if exchanged else (None, None)
        gates_ref, wg_any, wu_any, wd_any = refs[2 + far : 6 + far]
        pair_back, result_back, scale_back, dwg, dwu, dwd = refs[6 + far : 12 + far]
        scratch = refs[12 + far :]
        wg, wu, wd, hid, grd, act, dgate, dup, pair, result, scale = scratch[:11]
        tile_up, tile_down, load, own, store = scratch[11:16]
        semaphores = scratch[16:]

        def piece(ref, ref_far, k):
            return ref.at[k] if k == 0 or not exchanged else ref_far.at[k - 1]

        if exchanged:
            meet([k * copies for k in (1, 2, 3)], False)
        loads = {}

        def fetch(number, source, target):
            loads[number] = pltpu.make_async_copy(source, target, load.at[number])
            loads[number].start()

        fetch(0, wg_any, wg)
        for k in (3, 2, 1, 0):
            fetch(3 + k, piece(hidden_any, hidden_far_any, k), hid.at[pl.ds(k * slots, slots)])
        fetch(1, wu_any, wu)
        fetch(2, wd_any, wd)
        for k in (3, 2, 1, 0):
            fetch(7 + k, piece(grad_any, grad_far_any, k), grd.at[pl.ds(k * slots, slots)])
        def back(k, which):
            source, target = ((pair, pair_back), (result, result_back), (scale, scale_back))[which]
            return remote(
                source.at[k],
                target.at[k],
                semaphores[2 * which].at[k],
                semaphores[2 * which + 1].at[k],
                plane_device(k * copies),
            )

        def deliver(k, which):
            if exchanged:
                pl.when(k > 0)(lambda: back(k, which).start())

        def first(i, carry):
            k = 3 - i
            span = pl.ds(pl.multiple_of(k * slots, 16), slots)

            def ready(*numbers):
                @pl.when(i == 0)
                def _():
                    for number in numbers:
                        loads[number].wait()

            ready(0, 6, 5, 4, 3)
            gate = product(hid[span], wg[...])
            ready(1)
            up = product(hid[span], wu[...])
            ready(2, 10, 9, 8, 7)
            grad = product_right(grd[span], wd[...])
            gates_here = gates_ref[span]
            act_part, dgate_part, dup_part = silu_back(gate, up, grad)
            scale[k] = jnp.broadcast_to(
                jnp.sum(act_part * grad, axis=-1, keepdims=True), scale.shape[1:]
            )
            act[span] = low(act_part * gates_here)
            dgate[span] = low(dgate_part * gates_here)
            dup[span] = low(dup_part * gates_here)
            pair[k] = low(product_right(dgate[span], wg[...]) + product_right(dup[span], wu[...]))
            deliver(k, 0)
            deliver(k, 2)
            result[k] = low(product(act[span], wd[...]))
            deliver(k, 1)
            return carry

        lax.fori_loop(0, 4, first, 0)
        kept = []
        for which, (source, target) in enumerate(
            ((pair, pair_back), (result, result_back), (scale, scale_back))
        ):
            for k in range(1 if exchanged else 4):
                copy = pltpu.make_async_copy(source.at[k], target.at[k], own.at[which, k])
                copy.start()
                kept.append(copy)

        def tiles(count, rows, buffer, target, compute):
            def put(i, slot):
                start = pl.multiple_of(i * rows, 16)
                return pltpu.make_async_copy(
                    buffer.at[slot], target.at[pl.ds(start, rows)], store.at[slot]
                )

            def tile(i, carry):
                slot = lax.rem(i, 2)
                pl.when(i >= 2)(lambda: put(i - 2, slot).wait())
                buffer[slot] = compute(pl.ds(pl.multiple_of(i * rows, rows), rows))
                put(i, slot).start()
                return carry

            lax.fori_loop(0, count, tile, 0)
            for i in (count - 2, count - 1):
                put(i, i % 2).wait()

        tiles(width // 256, 256, tile_up, dwg, lambda s: low(product_left(hid[:, s], dgate[...])))
        tiles(width // 256, 256, tile_up, dwu, lambda s: low(product_left(hid[:, s], dup[...])))
        tiles(units // 128, 128, tile_down, dwd, lambda s: low(product_left(act[:, s], grd[...])))
        for copy in kept:
            copy.wait()
        if exchanged:
            for which in (0, 2, 1):
                for k in (3, 2, 1):
                    back(k, which).wait()

    shapes = [
        jax.ShapeDtypeStruct((4, slots, width), jnp.bfloat16),
        jax.ShapeDtypeStruct((4, slots, width), jnp.bfloat16),
        jax.ShapeDtypeStruct((4, slots, 128), jnp.float32),
    ] + [jax.ShapeDtypeStruct(w.shape, jnp.bfloat16) for w in weights]
    rows = 4 * slots
    scratch = [pltpu.VMEM(w.shape, jnp.bfloat16) for w in weights]
    scratch += [pltpu.VMEM((rows, width), jnp.bfloat16)] * 2
    scratch += [pltpu.VMEM((rows, units), jnp.bfloat16)] * 3
    scratch += [pltpu.VMEM((4, slots, width), jnp.bfloat16)] * 2
    scratch += [pltpu.VMEM((4, slots, 128), jnp.float32)]
    scratch += [
        pltpu.VMEM((2, 256, units), jnp.bfloat16),
        pltpu.VMEM((2, 128, width), jnp.bfloat16),
        pltpu.SemaphoreType.DMA((11,)),
        pltpu.SemaphoreType.DMA((3, 4)),
        pltpu.SemaphoreType.DMA((2,)),
    ]
    if exchanged:
        scratch += [pltpu.SemaphoreType.DMA((4,))] * 6
    operands = [hidden_slots, grad_slots] + ([hidden_far, grad_far] if exchanged else [])
    results = pl.pallas_call(
        kernel,
        out_shape=shapes,
        in_specs=[ANY] * len(operands) + [INSIDE] + [ANY] * 3,
        out_specs=[ANY] * 6,
        scratch_shapes=scratch,
        compiler_params=pltpu.CompilerParams(
            collective_id=6, has_side_effects=True, vmem_limit_bytes=60 << 20
        )
        if exchanged
        else pltpu.CompilerParams(vmem_limit_bytes=60 << 20),
        cost_estimate=pl.CostEstimate(
            flops=18 * rows * units * width, bytes_accessed=200_000_000, transcendentals=0
        ),
        name="routed_expert",
    )(*operands, gates, *weights)
    return results


def attention_back(branch, out, probs, expanded, query_nope, query_rope, keys, tiled, up):
    groups, rows, width = branch.shape
    heads, key_count = probs.shape[1], probs.shape[3]
    rope = query_rope.shape[2]
    score_scale = (NOPE + ROPE) ** (-0.5)

    def kernel(*refs):
        branch_ref, out_ref, probs_ref, exp_ref, nope_ref, rope_ref, keys_ref, tiled_ref, up_ref = (
            refs[:9]
        )
        dnope, drope, dkeys, dup, dexp = refs[9:]
        dmixed = low(product(branch_ref[...], out_ref[...]))
        drope_sum = jnp.zeros((rows, rope), jnp.float32)
        dkey_sum = jnp.zeros((key_count, rope), jnp.float32)
        for h in range(heads):
            nope_span = slice(h * NOPE, (h + 1) * NOPE)
            key_span = slice(h * (NOPE + VDIM), h * (NOPE + VDIM) + NOPE)
            value_span = slice(h * (NOPE + VDIM) + NOPE, (h + 1) * (NOPE + VDIM))
            mask = head_mask(h, heads, rope)
            weights = probs_ref[h]
            part = dmixed[:, h * VDIM : (h + 1) * VDIM]
            dprobs = product_right(part, exp_ref[:, value_span])
            wide_weights = wide(weights)
            delta = jnp.sum(wide_weights * dprobs, axis=-1, keepdims=True)
            dscore = low(wide_weights * (dprobs - delta) * score_scale)
            dexp[:, key_span] = low(product_left(dscore, nope_ref[:, nope_span]))
            dexp[:, value_span] = low(product_left(weights, part))
            dnope[:, nope_span] = low(product(dscore, exp_ref[:, key_span]))
            drope_sum = drope_sum + product(dscore, tiled_ref[...]) * mask
            dkey_sum = dkey_sum + product_left(dscore, rope_ref[...] * low(mask))
        drope[...] = drope_sum
        lane = lax.broadcasted_iota(jnp.int32, (rope, ROPE), 0)
        column = lax.broadcasted_iota(jnp.int32, (rope, ROPE), 1)
        half = ROPE // 2
        target = lane // (rope // 2) * half + lax.rem(lane, half)
        fold = low(jnp.where(target == column, 1.0, 0.0))
        dkeys[:, :LATENT] = product_right(dexp[...], up_ref[...])
        dkeys[:, LATENT:] = product(low(dkey_sum), fold)
        grad_up = product_left(keys_ref[:, :LATENT], dexp[...])

        @pl.when(pl.program_id(0) == 0)
        def _():
            dup[...] = grad_up

        @pl.when(pl.program_id(0) > 0)
        def _():
            dup[...] = dup[...] + grad_up

    def group(array):
        shape = array.shape
        return pl.BlockSpec(
            (None,) + tuple(shape[1:]), lambda g, n=len(shape) - 1: (g,) + (0,) * n
        )

    def whole(array):
        return pl.BlockSpec(array.shape, lambda g: (0, 0))

    shapes = [
        jax.ShapeDtypeStruct((groups, rows, heads * NOPE), jnp.bfloat16),
        jax.ShapeDtypeStruct((groups, rows, rope), jnp.float32),
        jax.ShapeDtypeStruct((groups, key_count, LATENT + ROPE), jnp.float32),
        jax.ShapeDtypeStruct(up.shape, jnp.float32),
    ]
    operands = [branch, out, probs, expanded, query_nope, query_rope, keys, tiled, up]
    return pl.pallas_call(
        kernel,
        grid=(groups,),
        out_shape=shapes,
        in_specs=[whole(x) if x is out or x is up else group(x) for x in operands],
        out_specs=[group(x) for x in shapes[:3]] + [whole(up)],
        scratch_shapes=[pltpu.VMEM((key_count, heads * (NOPE + VDIM)), jnp.bfloat16)],
        compiler_params=pltpu.CompilerParams(vmem_limit_bytes=40 << 20),
        cost_estimate=pl.CostEstimate(
            flops=20_000_000_000, bytes_accessed=30_000_000, transcendentals=0
        ),
        name="attention_back",
    )(*operands)


def body(
    tokens,
    routes,
    grad_out,
    attn_gain,
    query_weight,
    latent_down,
    latent_gain,
    latent_up,
    out_weight,
    ffn_gain,
    router_weight,
    shared_gate,
    shared_up,
    shared_down,
    expert_gate,
    expert_up,
    expert_down,
):
    contexts = lax.axis_size(CONTEXT_AXIS)
    context_index = lax.axis_index(CONTEXT_AXIS)
    groups_local = lax.axis_size(EXPERT_AXIS)
    expert_index = lax.axis_index(EXPERT_AXIS)
    plane_count = lax.axis_size(PLANE)
    plane_index = lax.axis_index(PLANE)
    local_experts = expert_gate.shape[0]
    experts_all = router_weight.shape[1]
    copies = plane_count // local_experts
    expert_own = plane_index // copies
    query_cols = query_weight.shape[1]
    heads_local = query_cols // (NOPE + ROPE)
    down_cols = LATENT + ROPE
    shard_rows = query_weight.shape[0]
    latent_rows = latent_up.shape[0]
    prompt_len = PROMPT_DEV * contexts
    capacity = (TOK_DEV * TOPK * 9 + 8 * experts_all - 1) // (8 * experts_all)
    slots = groups_local * capacity
    slots = -(-slots // 16) * 16 if local_experts > 1 else -(-slots // 64) * 64
    token_count = groups_local * TOK_DEV
    score_scale = (NOPE + ROPE) ** (-0.5)

    half_rope = ROPE // 2
    rope_cols = heads_local * half_rope
    nope_cols = heads_local * NOPE

    def query_split(columns):
        each = columns.reshape(columns.shape[0], heads_local, NOPE + ROPE)
        parts = (each[..., :NOPE], each[..., NOPE : NOPE + half_rope], each[..., NOPE + half_rope :])
        return [part.reshape(columns.shape[0], -1) for part in parts]

    def query_join(columns):
        rows = columns.shape[0]
        parts = (
            columns[:, :nope_cols],
            columns[:, nope_cols : nope_cols + rope_cols],
            columns[:, nope_cols + rope_cols :],
        )
        each = [part.reshape(rows, heads_local, -1) for part in parts]
        return jnp.concatenate(each, axis=-1).reshape(rows, query_cols)

    used_cols = query_cols + down_cols
    extra_cols = experts_all + 3
    pad_cols = -(used_cols + extra_cols) % 128
    gains = jnp.stack(
        [
            wide(attn_gain),
            wide(ffn_gain),
            jnp.pad(wide(latent_gain), (0, shard_rows - latent_gain.shape[0])),
        ]
        + [jnp.zeros((shard_rows,), jnp.float32)] * 5
    )
    first_local = jnp.concatenate(
        [
            *query_split(query_weight),
            latent_down,
            router_weight,
            jnp.zeros((shard_rows, 3 + pad_cols), jnp.bfloat16),
        ],
        axis=1,
    )
    shared_cols = shared_gate.shape[1]
    shared_pad = -(-shared_cols // 128) * 128

    def padded(weight):
        return jnp.pad(weight, ((0, 0), (0, shared_pad - shared_cols)))

    shared_own = jnp.concatenate(
        [padded(shared_gate), padded(shared_up), padded(shared_down.T)], axis=1
    )
    shared_whole = lax.all_gather(shared_own, PLANE, axis=0, tiled=True)
    gains_all, normed_all, (first_full, up_local, out_local) = opening(
        tokens[0], gains, [first_local, latent_up, out_weight.T]
    )
    full_router = first_full[:, used_cols : used_cols + experts_all]
    full_attn_gain = gains_all[:, 0].reshape(D)
    full_ffn_gain = gains_all[:, 1].reshape(D)
    full_latent_gain = gains_all[:, 2, : latent_gain.shape[0]].reshape(LATENT)

    within = jnp.arange(TOK_DEV, dtype=jnp.int32)
    query_places = jnp.where(
        within < PROMPT_DEV, context_index * PROMPT_DEV + within, prompt_len + within - PROMPT_DEV
    )
    cosine, sine_part = rotary_tables(query_places.astype(jnp.float32), ROPE // 2)
    source = wide(tokens[0])

    def pack_latent(comp_rows, latent_scale):
        return jnp.concatenate(
            [
                norm_rows(comp_rows[..., :LATENT], latent_scale),
                rotate(comp_rows[..., LATENT:], cosine[None], sine_part[None]),
            ],
            axis=-1,
        )

    routes_all = axis_gather(routes[0], EXPERT_AXIS)
    first_product = product(normed_all, first_full)
    compressed = first_product[..., query_cols:used_cols]
    packed = low(pack_latent(compressed, wide(full_latent_gain)))
    key_count = prompt_len + CONT_LEN
    keys = jnp.zeros((groups_local, contexts + 1, PROMPT_DEV, down_cols), jnp.bfloat16)
    prompt_own = packed[:, :PROMPT_DEV]
    for mask in range(contexts):
        came = swap(prompt_own, CONTEXT_AXIS, mask) if mask else prompt_own
        keys = lax.dynamic_update_slice(
            keys, came[:, None], (0, jnp.bitwise_xor(context_index, mask), 0, 0)
        )
    keys = lax.dynamic_update_slice(
        keys, packed[:, None, PROMPT_DEV:], (0, contexts, 0, 0)
    ).reshape(groups_local, key_count, down_cols)
    query_nope = low(first_product[..., :nope_cols])
    cosine_heads = jnp.tile(cosine, (1, heads_local))[None]
    sine_heads = jnp.tile(sine_part, (1, heads_local))[None]
    lower = first_product[..., nope_cols : nope_cols + rope_cols]
    upper = first_product[..., nope_cols + rope_cols : query_cols]
    query_rope = low(
        jnp.concatenate(
            [
                lower * cosine_heads - upper * sine_heads,
                upper * cosine_heads + lower * sine_heads,
            ],
            axis=-1,
        )
    )
    tiled_rope = jnp.concatenate(
        [keys[..., LATENT : LATENT + half_rope]] * heads_local
        + [keys[..., LATENT + half_rope :]] * heads_local,
        axis=-1,
    )
    slot_experts = expert_index * local_experts + (
        expert_own ^ jnp.arange(local_experts, dtype=jnp.int32)
    )
    expert_cols = jnp.arange(experts_all, dtype=jnp.int32)[:, None] == slot_experts[None, :]
    chosen_slots = jnp.any(routes_all[..., None] == slot_experts, axis=2)
    before = (within[:, None] > within[None, :]).astype(jnp.bfloat16)
    rank = jnp.einsum(
        "ts,gsl->gtl",
        before,
        chosen_slots.astype(jnp.bfloat16),
        preferred_element_type=jnp.float32,
    ).astype(jnp.int32)
    slot_of = jnp.where(
        chosen_slots,
        rank + capacity * jnp.arange(groups_local, dtype=jnp.int32)[:, None, None],
        -1,
    ).reshape(token_count, local_experts)
    picked = (
        slot_of.T[:, None, :] == jnp.arange(slots, dtype=jnp.int32)[None, :, None]
    )
    picked_low = picked.astype(jnp.bfloat16).reshape(local_experts * slots, token_count)
    piece_slots = slots * local_experts // 4
    (middle, hidden_all, grad_all, mixed_all, probs, expanded), fetched = middle_sum(
        query_nope,
        query_rope,
        keys,
        tiled_rope,
        up_local,
        out_local,
        tokens[0],
        full_ffn_gain[None],
        [expert_gate, expert_up, expert_down],
        grad_out[0],
    )
    gate_full, up_full, down_full = fetched
    hidden_flat = hidden_all.reshape(token_count, D)

    grad_flat = grad_all.reshape(token_count, D)
    hidden_slots = low(product(picked_low, hidden_flat)).reshape(4, piece_slots, D)
    grad_slots = low(product(picked_low, grad_flat)).reshape(4, piece_slots, D)
    logits = product(hidden_flat, full_router)
    expert_probs = jax.nn.softmax(logits, axis=-1)
    gate_tokens = jnp.sum(jnp.where(expert_cols[None], expert_probs[:, :, None], 0.0), axis=1)
    gate_slots = jnp.sum(jnp.where(picked, gate_tokens.T[:, None, :], 0.0), axis=-1)
    gate_slots = gate_slots.reshape(4, piece_slots)
    gates_padded = jnp.broadcast_to(
        jnp.pad(gate_slots, ((0, 0), (0, -piece_slots % 128)))[:, None], (4, 8, -(-piece_slots // 128) * 128)
    )
    row_hops = copies if local_experts > 1 else 0
    (act_shared, shared_hidden, shared_grads), far = shared_and_rows(
        hidden_flat, grad_flat, shared_whole, hidden_slots, grad_slots, gates_padded, row_hops
    )
    gates_far, hidden_far, grad_far = far if far else (None, None, None)
    if far:
        gate_slots = jnp.concatenate([gate_slots[:1], gates_far[:, 0, :piece_slots]], axis=0)
    pair_back, result, scale_back, *expert_partials = routed_expert(
        hidden_slots,
        grad_slots,
        hidden_far,
        grad_far,
        gate_slots.reshape(-1, 1),
        [gate_full, up_full, down_full],
        row_hops,
    )
    grad_gate_back = scale_back[:, :, 0].reshape(local_experts, slots)
    grad_routed = product_left(picked_low, pair_back.reshape(-1, D))
    grad_gate_tokens = jnp.sum(jnp.where(picked, grad_gate_back[:, :, None], 0.0), axis=1).T
    grad_spread = jnp.sum(
        jnp.where(expert_cols[None], grad_gate_tokens[:, None, :], 0.0), axis=-1
    )
    weighted = jnp.sum(expert_probs * grad_spread, axis=-1, keepdims=True)
    grad_logits = expert_probs * (grad_spread - weighted)
    grad_router = lax.dot_general(
        grad_logits,
        wide(hidden_flat),
        (((0,), (0,)), ((), ())),
        precision=lax.Precision.HIGHEST,
    )
    grad_from_router = lax.dot_general(
        grad_logits,
        wide(full_router),
        (((1,), (1,)), ((), ())),
        precision=lax.Precision.HIGHEST,
    )
    grad_hidden_part = low(
        shared_hidden + grad_routed + grad_from_router
    )
    grad_middle, grad_ffn_gain, branch_all, expert_grads, (result, shared_grads) = branch_sum(
        grad_hidden_part.reshape(groups_local, TOK_DEV, D),
        middle,
        full_ffn_gain[None],
        grad_out[0],
        expert_partials,
        local_experts,
        [result.reshape(-1, D), shared_grads],
    )
    shared_grads = wide(lax.psum_scatter(shared_grads, PLANE, scatter_dimension=0, tiled=True))
    routed_term = product_left(picked_low, result)
    branch_out = low(
        product_right(act_shared, shared_whole[:, 2 * shared_pad :]) + routed_term
    )
    grad_out_weight = low(
        product_left(
            branch_all.reshape(token_count, D), mixed_all.reshape(token_count, heads_local * VDIM)
        )
    )
    grad_nope, grad_rope, grad_keys, grad_latent_up = attention_back(
        branch_all,
        out_local,
        probs,
        expanded,
        query_nope,
        query_rope,
        keys,
        tiled_rope,
        up_local,
    )
    lower, upper = grad_rope[..., :rope_cols], grad_rope[..., rope_cols:]
    grad_query_raw = jnp.concatenate(
        [
            grad_nope,
            low(lower * cosine_heads + upper * sine_heads),
            low(upper * cosine_heads - lower * sine_heads),
        ],
        axis=-1,
    )
    grad_keys = grad_keys.reshape(groups_local, contexts + 1, PROMPT_DEV, down_cols)

    def keys_of(mask):
        return lax.dynamic_index_in_dim(
            grad_keys, jnp.bitwise_xor(context_index, mask), 1, keepdims=False
        )

    prompt_sum = keys_of(0)
    for mask in range(1, contexts):
        prompt_sum = prompt_sum + wide(swap(low(keys_of(mask)), CONTEXT_AXIS, mask))
    grad_packed = jnp.concatenate([prompt_sum, grad_keys[:, contexts]], axis=1)
    _, pack_back = jax.vjp(pack_latent, compressed, wide(full_latent_gain))
    grad_compressed, grad_latent_gain = pack_back(grad_packed)
    grad_first = jnp.concatenate(
        [
            grad_query_raw,
            low(grad_compressed),
            jnp.zeros((groups_local, TOK_DEV, first_full.shape[1] - used_cols), jnp.bfloat16),
        ],
        axis=-1,
    )
    gain_rows = jnp.concatenate(
        [
            jnp.zeros((plane_count, 1, shard_rows), jnp.float32),
            grad_ffn_gain.reshape(plane_count, 1, shard_rows),
            jnp.pad(
                grad_latent_gain.reshape(plane_count, 1, latent_rows),
                ((0, 0), (0, 0), (0, shard_rows - latent_rows)),
            ),
            grad_router.reshape(experts_all, plane_count, shard_rows).transpose(1, 0, 2),
            jnp.zeros((plane_count, -(3 + experts_all) % 8, shard_rows), jnp.float32),
        ],
        axis=1,
    )
    block_out = low(
        middle + axis_scatter(branch_out.reshape(groups_local, TOK_DEV, D), EXPERT_AXIS)
    )
    (grad_tokens, gain_sum, down_own), sums = closing(
        grad_first.reshape(token_count, -1),
        first_full,
        normed_all.reshape(token_count, D),
        block_out,
        tokens[0],
        full_attn_gain[None],
        grad_middle,
        gain_rows,
        [low(grad_latent_up), grad_out_weight],
        query_cols // 128 * 128,
    )
    first_sum, up_sum, out_sum = sums
    small_rows = shard_rows // groups_local
    small_own = lax.dynamic_slice_in_dim(gain_sum, expert_index * small_rows, small_rows, 1)
    latent_small = latent_rows // groups_local
    latent_own = lax.dynamic_slice_in_dim(gain_sum[2], expert_index * latent_small, latent_small, 0)
    down_start = query_cols % 128
    return (
        block_out[None],
        grad_tokens[None],
        small_own[0],
        query_join(first_sum[:, :query_cols]),
        down_own[:, down_start : down_start + down_cols],
        latent_own,
        up_sum,
        out_sum.T,
        small_own[1],
        small_own[3 : 3 + experts_all].T,
        shared_grads[:, :shared_cols],
        shared_grads[:, shared_pad : shared_pad + shared_cols],
        shared_grads[:, 2 * shared_pad : 2 * shared_pad + shared_cols].T,
        *expert_grads,
    )


def solution(mesh):
    in_specs = (
        P((DP_AXIS, EXPERT_AXIS), CONTEXT_AXIS, None),
        P((DP_AXIS, EXPERT_AXIS), CONTEXT_AXIS, None),
        P((DP_AXIS, EXPERT_AXIS), CONTEXT_AXIS, None),
        P((DP_AXIS, CONTEXT_AXIS)),
        P((DP_AXIS, CONTEXT_AXIS), EXPERT_AXIS),
        P((DP_AXIS, CONTEXT_AXIS), None),
        P((DP_AXIS, CONTEXT_AXIS)),
        P((DP_AXIS, CONTEXT_AXIS), EXPERT_AXIS),
        P(EXPERT_AXIS, (DP_AXIS, CONTEXT_AXIS)),
        P((DP_AXIS, CONTEXT_AXIS)),
        P((DP_AXIS, CONTEXT_AXIS), None),
        P((DP_AXIS, CONTEXT_AXIS), EXPERT_AXIS),
        P((DP_AXIS, CONTEXT_AXIS), EXPERT_AXIS),
        P(EXPERT_AXIS, (DP_AXIS, CONTEXT_AXIS)),
        P(EXPERT_AXIS, (DP_AXIS, CONTEXT_AXIS), None),
        P(EXPERT_AXIS, (DP_AXIS, CONTEXT_AXIS), None),
        P(EXPERT_AXIS, (DP_AXIS, CONTEXT_AXIS), None),
    )
    out_specs = (
        P((DP_AXIS, EXPERT_AXIS), CONTEXT_AXIS, None),
        P((DP_AXIS, EXPERT_AXIS), CONTEXT_AXIS, None),
        P((DP_AXIS, CONTEXT_AXIS, EXPERT_AXIS)),
        P((DP_AXIS, CONTEXT_AXIS), EXPERT_AXIS),
        P((DP_AXIS, CONTEXT_AXIS, EXPERT_AXIS), None),
        P((DP_AXIS, CONTEXT_AXIS, EXPERT_AXIS)),
        P((DP_AXIS, CONTEXT_AXIS), EXPERT_AXIS),
        P(EXPERT_AXIS, (DP_AXIS, CONTEXT_AXIS)),
        P((DP_AXIS, CONTEXT_AXIS, EXPERT_AXIS)),
        P((DP_AXIS, CONTEXT_AXIS, EXPERT_AXIS), None),
        P((DP_AXIS, CONTEXT_AXIS), EXPERT_AXIS),
        P((DP_AXIS, CONTEXT_AXIS), EXPERT_AXIS),
        P(EXPERT_AXIS, (DP_AXIS, CONTEXT_AXIS)),
        P(EXPERT_AXIS, (DP_AXIS, CONTEXT_AXIS), None),
        P(EXPERT_AXIS, (DP_AXIS, CONTEXT_AXIS), None),
        P(EXPERT_AXIS, (DP_AXIS, CONTEXT_AXIS), None),
    )
    return jax.shard_map(body, mesh=mesh, in_specs=in_specs, out_specs=out_specs, check_vma=False)
```

```python
import jax
import jax.numpy as jnp
from jax import lax
from jax.experimental import pallas as pl
from jax.experimental.pallas import tpu as pltpu
from jax.experimental.layout import Layout, with_layout_constraint
from jax.sharding import PartitionSpec as P

D = 2048
NOPE = 128
ROPE = 64
VDIM = 128
LATENT = 512
TOPK = 6
PROMPT_DEV = 64
CONT_LEN = 64
TOK_DEV = 128


epsilon = 1e-06


def norm_rows(values, scale_gain):
    return (
        values * lax.rsqrt(jnp.mean(values * values, axis=-1, keepdims=True) + epsilon) * scale_gain
    )


def rotary_tables(places, half_size):
    frequency = 10000.0 ** (-jnp.arange(half_size, dtype=jnp.float32) / half_size)
    angles = places[:, None] * frequency[None, :]
    return (jnp.cos(angles), jnp.sin(angles))


def rotate(values, cosine, sine_part):
    half_size = values.shape[-1] // 2
    lower_half = values[..., :half_size]
    upper_half = values[..., half_size:]
    return jnp.concatenate(
        [
            lower_half * cosine - upper_half * sine_part,
            upper_half * cosine + lower_half * sine_part,
        ],
        axis=-1,
    )


def product(left_side, right_side):
    return jnp.dot(left_side, right_side, preferred_element_type=jnp.float32)


def product_left(left_side, right_side):
    return lax.dot_general(
        left_side, right_side, (((0,), (0,)), ((), ())), preferred_element_type=jnp.float32
    )


def product_right(left_side, right_side):
    return lax.dot_general(
        left_side, right_side, (((1,), (1,)), ((), ())), preferred_element_type=jnp.float32
    )


def against_rows(left_side, right_side):
    return lax.dot_general(
        left_side,
        right_side,
        (((left_side.ndim - 1,), (1,)), ((), ())),
        preferred_element_type=jnp.float32,
    )


DP_AXIS, CONTEXT_AXIS, EXPERT_AXIS = "dp", "context", "expert"
PLANE = (DP_AXIS, CONTEXT_AXIS)


def swap(values, axis, mask):
    count = lax.axis_size(axis)
    return lax.ppermute(values, axis, [(i, i ^ mask) for i in range(count)])


def place_pieces(pieces, index, count):
    first = pieces[0]
    whole = jnp.zeros((count,) + first.shape, first.dtype)
    for mask, piece in pieces.items():
        whole = lax.dynamic_update_slice(whole, piece[None], (index ^ mask,) + (0,) * first.ndim)
    return with_layout_constraint(whole, Layout(tuple(range(whole.ndim))))


def low(values):
    return values.astype(jnp.bfloat16)


def wide(values):
    return values.astype(jnp.float32)


def axis_gather(values, axis):
    count = lax.axis_size(axis)
    pieces = {mask: swap(values, axis, mask) if mask else values for mask in range(count)}
    return place_pieces(pieces, lax.axis_index(axis), count)


def axis_scatter(blocks, axis):
    count = lax.axis_size(axis)
    index = lax.axis_index(axis)

    def part(mask):
        return lax.dynamic_index_in_dim(blocks, index ^ mask, 0, keepdims=False)

    total = wide(part(0))
    for mask in range(1, count):
        total = total + wide(swap(low(part(mask)), axis, mask))
    return total


MESH_ID = pl.DeviceIdType.MESH
ANY = pl.BlockSpec(memory_space=pl.ANY)
INSIDE = pl.BlockSpec(memory_space=pltpu.VMEM)


def plane_here():
    return lax.axis_index(DP_AXIS) * lax.axis_size(CONTEXT_AXIS) + lax.axis_index(CONTEXT_AXIS)


def plane_device(mask):
    contexts = lax.axis_size(CONTEXT_AXIS)
    other = jnp.bitwise_xor(plane_here(), mask)
    return {DP_AXIS: other // contexts, CONTEXT_AXIS: lax.rem(other, contexts)}


def line_device(offset):
    return {EXPERT_AXIS: lax.axis_index(EXPERT_AXIS) + offset}


def signal(device):
    pl.semaphore_signal(
        pltpu.get_barrier_semaphore(), inc=1, device_id=device, device_id_type=MESH_ID
    )


def meet(masks, line):
    count = len(masks)
    for mask in masks:
        signal(plane_device(mask))
    if line:
        place, last = lax.axis_index(EXPERT_AXIS), lax.axis_size(EXPERT_AXIS) - 1
        pl.when(place > 0)(lambda: signal(line_device(-1)))
        pl.when(place < last)(lambda: signal(line_device(1)))
        count = count + jnp.where(place > 0, 1, 0) + jnp.where(place < last, 1, 0)
    pl.semaphore_wait(pltpu.get_barrier_semaphore(), count)


def remote(source, target, send, recv, device):
    return pltpu.make_async_remote_copy(
        src_ref=source,
        dst_ref=target,
        send_sem=send,
        recv_sem=recv,
        device_id=device,
        device_id_type=MESH_ID,
    )


def arrived(target, send, recv):
    remote(target, target, send, recv, plane_device(1)).wait_recv()


def run_tasks(*tasks):
    active = list(tasks)
    while active:
        for task in list(active):
            if next(task, None) is None:
                active.remove(task)


def plane_gather_task(source, target, own, send, recv):
    rows = source.shape[0]
    half = rows // 2
    here = plane_here()

    def slot(mask, first=0, count=rows):
        start = pl.multiple_of(jnp.bitwise_xor(here, mask) * rows + first, 16)
        return target.at[pl.ds(start, count)]

    def go(number, source_ref, target_ref, mask):
        copy = remote(source_ref, target_ref, send.at[number], recv.at[number], plane_device(mask))
        copy.start()
        return copy

    def got(number, ref):
        arrived(ref, send.at[number], recv.at[number])

    local = pltpu.make_async_copy(source, slot(0), own)
    copies = [go(0, source, slot(0), 2), go(1, source, slot(0), 4)]
    yield 1
    copies.append(go(4, source, slot(0), 1))
    local.start()
    yield 1
    got(0, slot(2))
    copies.append(go(2, slot(2, 0, half), slot(2, 0, half), 4))
    copies.append(go(5, slot(2), slot(2), 1))
    yield 1
    got(1, slot(4))
    copies.append(go(3, slot(4, half, half), slot(4, half, half), 2))
    copies.append(go(6, slot(4), slot(4), 1))
    yield 1
    got(2, slot(6, 0, half))
    copies.append(go(7, slot(6, 0, half), slot(6, 0, half), 1))
    yield 1
    got(3, slot(6, half, half))
    copies.append(go(8, slot(6, half, half), slot(6, half, half), 1))
    yield 1
    got(4, slot(1))
    got(5, slot(3))
    got(6, slot(5))
    got(7, slot(7, 0, half))
    got(8, slot(7, half, half))
    local.wait()
    for copy in copies:
        copy.wait_send()


def expert_fetch_task(source, target, stage, own, send, recv):
    if source.shape[0] == 1:
        load = pltpu.make_async_copy(source.at[0], stage, own)
        load.start()
        load.wait()
        yield from plane_gather_task(stage, target, own, send, recv)
        return
    rows = source.shape[1]
    here = plane_here()
    expert_own = here // 2

    def slot(mask):
        start = pl.multiple_of(jnp.bitwise_xor(here, mask) * rows, 16)
        return target.at[pl.ds(start, rows)]

    def go(number, source_ref, target_ref, mask):
        copy = remote(source_ref, target_ref, send.at[number], recv.at[number], plane_device(mask))
        copy.start()
        return copy

    def got(number, ref):
        arrived(ref, send.at[number], recv.at[number])

    copies = []
    for k in (3, 1, 2):
        copies.append(go(k, source.at[jnp.bitwise_xor(expert_own, k)], slot(0), 2 * k))
    load = pltpu.make_async_copy(source.at[expert_own], stage, own)
    load.start()
    yield 1
    load.wait()
    local = pltpu.make_async_copy(stage, slot(0), own)
    local.start()
    copies.append(go(0, stage, slot(0), 1))
    for k in (1, 2, 3):
        yield 1
        got(k, slot(2 * k))
        copies.append(go(4 + k, slot(2 * k), slot(2 * k), 1))
    yield 1
    got(0, slot(1))
    for k in (1, 2, 3):
        got(4 + k, slot(2 * k + 1))
    local.wait()
    for copy in copies:
        copy.wait_send()


LINE_PARTS = 4


def line_gather_steps(target, send, recv, rows):
    place, count = lax.axis_index(EXPERT_AXIS), lax.axis_size(EXPERT_AXIS)
    part = rows // LINE_PARTS

    def piece(block, c):
        return target.at[block, pl.ds(c * part, part)]

    def copy(way, distance, c, source=None):
        block = place - way * distance
        ref = piece(block, c)
        return remote(
            ref if source is None else source,
            ref,
            send.at[(way + 1) // 2, distance, c],
            recv.at[(way + 1) // 2, distance, c],
            line_device(way),
        )

    def has_next(way):
        return place < count - 1 if way == 1 else place > 0

    def has_block(way, distance):
        return place - distance >= 0 if way == 1 else place + distance < count

    def begin(c, source):
        for way in (1, -1):
            pl.when(has_next(way))(lambda way=way: copy(way, 0, c, source).start())

    def forward(c, distance):
        for way in (1, -1):

            @pl.when(has_block(way, distance))
            def _(way=way):
                ref = piece(place - way * distance, c)
                arrived(
                    ref,
                    send.at[(way + 1) // 2, distance - 1, c],
                    recv.at[(way + 1) // 2, distance - 1, c],
                )
                if distance < count - 1:
                    pl.when(has_next(way))(lambda: copy(way, distance, c).start())

    def finish(source):
        for c in range(LINE_PARTS):
            for way in (1, -1):
                for distance in range(count - 1):

                    @pl.when(jnp.logical_and(has_next(way), has_block(way, distance)))
                    def _(way=way, distance=distance, c=c):
                        copy(way, distance, c, source(c) if distance == 0 else None).wait_send()

    return begin, forward, finish


def line_gather_task(source, target, own, send, recv):
    rows = source.shape[0]
    part = rows // LINE_PARTS
    count = lax.axis_size(EXPERT_AXIS)
    begin, forward, finish = line_gather_steps(target, send, recv, rows)
    local = pltpu.make_async_copy(source, target.at[lax.axis_index(EXPERT_AXIS)], own)
    for c in range(LINE_PARTS):
        begin(c, source.at[pl.ds(c * part, part)])
    local.start()
    yield 1
    for distance in range(1, count):
        for c in range(LINE_PARTS):
            forward(c, distance)
        yield 1
    local.wait()
    finish(lambda c: source.at[pl.ds(c * part, part)])


def line_semaphores():
    count = lax.axis_size(EXPERT_AXIS)
    return [pltpu.SemaphoreType.DMA((2, count, LINE_PARTS))] * 2


def line_reduce_steps(partial, inbox, send, recv):
    place, count = lax.axis_index(EXPERT_AXIS), lax.axis_size(EXPERT_AXIS)
    rows = partial.shape[1]
    part = rows // LINE_PARTS

    def span(c):
        return pl.ds(c * part, part)

    def box(way, distance, c):
        return inbox.at[distance if way == 1 else count - distance, span(c)]

    def copy(way, distance, c, source):
        side = (way + 1) // 2
        return remote(
            source,
            box(way, distance - 1, c),
            send.at[side, distance, c],
            recv.at[side, distance - 1, c],
            line_device(way),
        )

    def wait_inbox(way, distance, c):
        side = (way + 1) // 2
        arrived(box(way, distance, c), send.at[side, distance, c], recv.at[side, distance, c])

    def has_source(way):
        return place > 0 if way == 1 else place < count - 1

    def has_target(way, distance):
        return place + distance < count if way == 1 else place - distance >= 0

    def step(c, distance):
        for way in (1, -1):
            mine = partial.at[place + way * distance, span(c)]

            def pass_on(way=way, mine=mine):
                came = box(way, distance, c)
                wait_inbox(way, distance, c)
                came[...] = low(wide(mine[...]) + wide(came[...]))
                copy(way, distance, c, came).start()

            def send_first(way=way, mine=mine):
                copy(way, distance, c, mine).start()

            valid = has_target(way, distance)
            if distance < count - 1:
                pl.when(jnp.logical_and(valid, has_source(way)))(pass_on)
                pl.when(jnp.logical_and(valid, jnp.logical_not(has_source(way))))(send_first)
            else:
                pl.when(valid)(send_first)

    def total(c, result):
        result[span(c)] = result[span(c)] + wide(partial[place, span(c)])
        for way in (1, -1):

            @pl.when(has_source(way))
            def _(way=way):
                wait_inbox(way, 0, c)
                result[span(c)] = result[span(c)] + wide(box(way, 0, c)[...])

    def stages(result, done):
        for t in range(LINE_PARTS + count - 1):
            for c in range(LINE_PARTS):
                distance = count - 1 - (t - c)
                if 1 <= distance <= count - 1:
                    step(c, distance)
                elif distance == 0:
                    total(c, result)
                    done(span(c), c)
            yield 1

    def finish():
        for c in range(LINE_PARTS):
            for way in (1, -1):
                for distance in range(1, count):
                    pl.when(has_target(way, distance))(
                        lambda way=way, distance=distance, c=c: copy(
                            way, distance, c, partial.at[place + way * distance, span(c)]
                        ).wait_send()
                    )

    return stages, finish


def gather_semaphores():
    return [
        pltpu.SemaphoreType.DMA(()),
        pltpu.SemaphoreType.DMA((9,)),
        pltpu.SemaphoreType.DMA((9,)),
    ]


def kernel_params(number):
    return pltpu.CompilerParams(
        collective_id=number,
        has_side_effects=True,
        vmem_limit_bytes=(52 if lax.axis_size(EXPERT_AXIS) <= 4 else 60) << 20,
    )


def opening(tokens, gains, matrices):
    count = lax.axis_size(EXPERT_AXIS)
    rows, width = tokens.shape
    number = len(matrices)
    planes = lax.axis_size(PLANE)
    depth = gains.shape[1]

    def kernel(*refs):
        tokens_ref, gains_ref = refs[:2]
        sources = refs[2 : 2 + number]
        gains_all, normed_all = refs[2 + number : 4 + number]
        targets = refs[4 + number : 4 + 2 * number]
        scratch = list(refs[4 + 2 * number :])
        normed, gain_box, gain_send, gain_recv = scratch[:4]
        line = scratch[4:7]
        semaphores = scratch[7:]
        meet(range(1, planes), True)
        here = plane_here()
        sends = []
        for mask in range(1, planes):
            copy = remote(
                gains_ref,
                gain_box.at[here],
                gain_send.at[mask],
                gain_recv.at[mask],
                plane_device(mask),
            )
            copy.start()
            sends.append(copy)
        tasks = [
            plane_gather_task(sources[i], targets[i], *semaphores[3 * i : 3 * i + 3])
            for i in range(number)
        ]
        for task in tasks:
            next(task)
        for task in tasks:
            next(task)
        gain_box[here] = gains_ref[...]
        values = wide(tokens_ref[...])
        scale = lax.rsqrt(jnp.mean(values * values, axis=-1, keepdims=True) + epsilon)
        for mask in range(1, planes):
            other = gain_box.at[jnp.bitwise_xor(here, mask)]
            arrived(other, gain_send.at[mask], gain_recv.at[mask])
        for i in range(planes):
            columns = slice(i * depth, (i + 1) * depth)
            normed[:, columns] = low(
                wide(tokens_ref[:, columns]) * scale * gain_box[i, 0:1, :]
            )
        gains_all[...] = gain_box[...]
        rows_task = line_gather_task(normed, normed_all, *line)
        next(rows_task)
        next(rows_task)
        for task in tasks:
            next(task)
        for task in tasks:
            next(task)
        run_tasks(rows_task, *tasks)
        for copy in sends:
            copy.wait_send()

    shapes = [
        jax.ShapeDtypeStruct((planes,) + gains.shape, jnp.float32),
        jax.ShapeDtypeStruct((count, rows, width), jnp.bfloat16),
    ] + [jax.ShapeDtypeStruct((planes * m.shape[0], m.shape[1]), m.dtype) for m in matrices]
    scratch = [
        pltpu.VMEM((rows, width), jnp.bfloat16),
        pltpu.VMEM((planes,) + gains.shape, jnp.float32),
        pltpu.SemaphoreType.DMA((planes,)),
        pltpu.SemaphoreType.DMA((planes,)),
        pltpu.SemaphoreType.DMA(()),
    ]
    scratch += line_semaphores()
    for _ in matrices:
        scratch += gather_semaphores()
    results = pl.pallas_call(
        kernel,
        out_shape=shapes,
        in_specs=[INSIDE] * (2 + number),
        out_specs=[INSIDE, ANY] + [ANY] * number,
        scratch_shapes=scratch,
        compiler_params=kernel_params(1),
        cost_estimate=pl.CostEstimate(
            flops=60_000_000, bytes_accessed=150_000_000, transcendentals=0
        ),
        name="opening",
    )(tokens, gains, *matrices)
    return results[0], results[1], results[2:]


def rope_fold(rope):
    lane = lax.broadcasted_iota(jnp.int32, (rope, ROPE), 0)
    column = lax.broadcasted_iota(jnp.int32, (rope, ROPE), 1)
    half = ROPE // 2
    target = lane // (rope // 2) * half + lax.rem(lane, half)
    return low(jnp.where(target == column, 1.0, 0.0))


def head_mask(head, heads, rope):
    lanes = lax.broadcasted_iota(jnp.int32, (1, rope), 1)
    return jnp.where(lax.rem(lanes, rope // 2) // (ROPE // 2) == head, 1.0, 0.0)


def middle_sum(query_nope, query_rope, keys, up, out, source, gain, experts, grads):
    count, rows = query_nope.shape[:2]
    key_count, rope = keys.shape[1], query_rope.shape[2]
    heads = query_nope.shape[2] // NOPE
    width = source.shape[1]
    planes, contexts = lax.axis_size(PLANE), lax.axis_size(CONTEXT_AXIS)
    routed = len(experts)
    score_scale = (NOPE + ROPE) ** (-0.5)

    def kernel(*refs):
        nope_ref, rope_ref, keys_ref, up_ref, out_ref, source_ref, gain_ref = refs[:7]
        expert_refs = refs[7 : 7 + routed]
        grads_ref = refs[7 + routed]
        outputs = refs[8 + routed :]
        middle_ref, hidden_all, grads_all, mixed, probs, expanded = outputs[:6]
        targets = outputs[6 : 6 + routed]
        scratch = list(outputs[6 + routed :])
        grads_line = [scratch.pop() for _ in range(3)][::-1]
        partial_ref = scratch.pop(0)
        inbox, hidden, reduce_send, reduce_recv, own, line_send, line_recv = scratch[:7]
        stages = scratch[7 : 7 + routed]
        semaphores = scratch[7 + routed :]
        meet((1, 2, 4, 6), True)
        reduce_stages, reduce_finish = line_reduce_steps(
            partial_ref, inbox, reduce_send, reduce_recv
        )
        begin, forward, finish = line_gather_steps(hidden_all, line_send, line_recv, rows)
        part = rows // LINE_PARTS

        def ready(span, c):
            values = middle_ref[span]
            scale = lax.rsqrt(jnp.mean(values * values, axis=-1, keepdims=True) + epsilon)
            hidden[span] = low(values * scale * gain_ref[...])
            begin(c, hidden.at[span])

        def line_task():
            middle_ref[...] = wide(source_ref[...])
            yield from reduce_stages(middle_ref, ready)
            local = pltpu.make_async_copy(hidden, hidden_all.at[lax.axis_index(EXPERT_AXIS)], own)
            local.start()
            for distance in range(1, count):
                for c in range(LINE_PARTS):
                    forward(c, distance)
                yield 1
            local.wait()
            finish(lambda c: hidden.at[pl.ds(c * part, part)])
            reduce_finish()

        tasks = [
            expert_fetch_task(
                expert_refs[i], targets[i], stages[i], *semaphores[3 * i : 3 * i + 3]
            )
            for i in range(routed)
        ]
        for task in tasks:
            next(task)
        grads_task = line_gather_task(grads_ref, grads_all, *grads_line)
        next(grads_task)
        for task in tasks:
            next(task)
        here = lax.axis_index(CONTEXT_AXIS)
        row = lax.broadcasted_iota(jnp.int32, (rows, key_count), 0)
        place = jnp.where(
            row < PROMPT_DEV,
            here * PROMPT_DEV + row,
            contexts * PROMPT_DEV + row - PROMPT_DEV,
        )
        allowed = lax.broadcasted_iota(jnp.int32, (rows, key_count), 1) <= place

        def attend(g, carry):
            expanded[g] = low(product(keys_ref[g, :, :LATENT], up_ref[...]))
            tiled = low(product_right(keys_ref[g, :, LATENT:], rope_fold(rope)))
            for h in range(heads):
                start = h * (NOPE + VDIM)
                scores = product_right(
                    nope_ref[g, :, h * NOPE : (h + 1) * NOPE],
                    expanded[g, :, start : start + NOPE],
                ) + product_right(
                    rope_ref[g] * low(head_mask(h, heads, rope)), tiled
                )
                scores = jnp.where(allowed, scores * score_scale, -1e30)
                powers = jnp.exp(scores - jnp.max(scores, axis=-1, keepdims=True))
                weights = low(powers / jnp.sum(powers, axis=-1, keepdims=True))
                probs[g, h] = weights
                mixed[g, :, h * VDIM : (h + 1) * VDIM] = low(
                    product(weights, expanded[g, :, start + NOPE : start + NOPE + VDIM])
                )
            partial_ref[g] = low(product_right(mixed[g], out_ref[...]))
            return carry

        lax.fori_loop(0, count, attend, 0)
        run_tasks(line_task())
        run_tasks(grads_task, *tasks)

    shapes = [
        jax.ShapeDtypeStruct((rows, width), jnp.float32),
        jax.ShapeDtypeStruct((count, rows, width), jnp.bfloat16),
        jax.ShapeDtypeStruct((count, rows, width), jnp.bfloat16),
        jax.ShapeDtypeStruct((count, rows, heads * VDIM), jnp.bfloat16),
        jax.ShapeDtypeStruct((count, heads, rows, key_count), jnp.bfloat16),
        jax.ShapeDtypeStruct((count, key_count, up.shape[1]), jnp.bfloat16),
    ] + [jax.ShapeDtypeStruct((planes * e.shape[1], e.shape[2]), e.dtype) for e in experts]
    scratch = [
        pltpu.VMEM((count, rows, width), jnp.bfloat16),
        pltpu.VMEM((count + 1, rows, width), jnp.bfloat16),
        pltpu.VMEM((rows, width), jnp.bfloat16),
    ]
    scratch += line_semaphores() + [pltpu.SemaphoreType.DMA(())] + line_semaphores()
    scratch += [pltpu.VMEM(e.shape[1:], e.dtype) for e in experts]
    for _ in range(routed):
        scratch += gather_semaphores()
    scratch += [pltpu.SemaphoreType.DMA(())] + line_semaphores()
    results = pl.pallas_call(
        kernel,
        out_shape=shapes,
        in_specs=[INSIDE] * 7 + [ANY] * routed + [INSIDE],
        out_specs=[INSIDE, ANY, ANY] + [INSIDE] * 3 + [ANY] * routed,
        scratch_shapes=scratch,
        compiler_params=kernel_params(2),
        cost_estimate=pl.CostEstimate(
            flops=60_000_000, bytes_accessed=300_000_000, transcendentals=0
        ),
        name="middle_sum",
    )(query_nope, query_rope, keys, up, out, source, gain, *experts, grads)
    return results[:6], results[6:]


def add_rows(target, first, second):
    def tile(i, carry):
        span = pl.ds(pl.multiple_of(i * 16, 16), 16)
        target[span] = (wide(first[span]) + wide(second[span])).astype(target.dtype)
        return carry

    lax.fori_loop(0, target.shape[0] // 16, tile, 0)


def expert_return_task(source, result, mine, came, load, send, recv):
    rows = mine.shape[1]
    here = plane_here()
    expert_own = here // 2

    def slot(mask):
        return source.at[pl.ds(pl.multiple_of(jnp.bitwise_xor(here, mask) * rows, 16), rows)]

    def go(number, source_ref, target_ref, mask):
        copy = remote(source_ref, target_ref, send.at[number], recv.at[number], plane_device(mask))
        copy.start()
        return copy

    copies, loads = [], {}

    def cross(k):
        copies.append(go(k, slot(2 * k + 1), came.at[k], 1))
        loads[k] = pltpu.make_async_copy(slot(2 * k), mine.at[k], load.at[k])
        loads[k].start()

    cross(3)
    yield 1
    for k, following in ((3, 1), (1, 2), (2, 0), (0, None)):
        if following is not None:
            cross(following)
        arrived(came.at[k], send.at[k], recv.at[k])
        loads[k].wait()
        add_rows(mine.at[k], mine.at[k], came.at[k])
        if k:
            copies.append(go(4 + k, mine.at[k], result.at[expert_own], 2 * k))
        else:
            local = pltpu.make_async_copy(mine.at[0], result.at[expert_own], load.at[0])
            local.start()
        yield 1
    for k in (3, 1, 2):
        arrived(
            result.at[jnp.bitwise_xor(expert_own, k)], send.at[4 + k], recv.at[4 + k]
        )
    local.wait()
    for copy in copies:
        copy.wait_send()


def expert_return_scratch(rows, columns):
    return [
        pltpu.VMEM((4, rows, columns), jnp.bfloat16),
        pltpu.VMEM((4, rows, columns), jnp.bfloat16),
        pltpu.SemaphoreType.DMA((4,)),
        pltpu.SemaphoreType.DMA((8,)),
        pltpu.SemaphoreType.DMA((8,)),
    ]


def plane_scatter_task(source, result, mine, came, box, last, load, send, recv):
    rows = mine.shape[1]
    half = rows // 2
    here = plane_here()
    upper, lower = pl.ds(0, half), pl.ds(half, half)

    def slot(mask):
        return source.at[pl.ds(pl.multiple_of(jnp.bitwise_xor(here, mask) * rows, 16), rows)]

    def go(number, source_ref, target_ref, mask):
        copy = remote(source_ref, target_ref, send.at[number], recv.at[number], plane_device(mask))
        copy.start()
        return copy

    def got(number, ref):
        arrived(ref, send.at[number], recv.at[number])

    copies, loads = [], {}

    def cross(k):
        copies.append(go(k, slot(2 * k + 1), came.at[k], 1))
        loads[k] = pltpu.make_async_copy(slot(2 * k), mine.at[k], load.at[k])
        loads[k].start()

    cross(3)
    yield 1
    for k, following in ((3, 1), (1, 2), (2, 0)):
        cross(following)
        got(k, came.at[k])
        loads[k].wait()
        add_rows(mine.at[k], mine.at[k], came.at[k])
        if k == 3:
            copies.append(go(4, mine.at[3, upper], box.at[0], 2))
            copies.append(go(5, mine.at[3, lower], box.at[1], 4))
        elif k == 1:
            copies.append(go(6, mine.at[1, upper], last.at[0, upper], 2))
        else:
            copies.append(go(7, mine.at[2, lower], last.at[1, lower], 4))
        yield 1
    got(4, box.at[0])
    add_rows(mine.at[2, upper], mine.at[2, upper], box.at[0])
    copies.append(go(8, mine.at[2, upper], last.at[1, upper], 4))
    yield 1
    got(5, box.at[1])
    add_rows(mine.at[1, lower], mine.at[1, lower], box.at[1])
    copies.append(go(9, mine.at[1, lower], last.at[0, lower], 2))
    yield 1
    got(0, came.at[0])
    loads[0].wait()
    add_rows(result, mine.at[0], came.at[0])
    got(6, last.at[0, upper])
    got(7, last.at[1, lower])
    yield 1
    got(9, last.at[0, lower])
    add_rows(result, result, last.at[0])
    got(8, last.at[1, upper])
    add_rows(result, result, last.at[1])
    for copy in copies:
        copy.wait_send()


def plane_scatter_scratch(rows, columns):
    return [
        pltpu.VMEM((4, rows, columns), jnp.bfloat16),
        pltpu.VMEM((4, rows, columns), jnp.bfloat16),
        pltpu.VMEM((2, rows // 2, columns), jnp.bfloat16),
        pltpu.VMEM((2, rows, columns), jnp.bfloat16),
        pltpu.SemaphoreType.DMA((4,)),
        pltpu.SemaphoreType.DMA((10,)),
        pltpu.SemaphoreType.DMA((10,)),
    ]


def norm_back(values, gain, grad):
    scale = lax.rsqrt(jnp.mean(values * values, axis=-1, keepdims=True) + epsilon)
    scaled = gain * grad
    mean = jnp.mean(values * scaled, axis=-1, keepdims=True)
    part = jnp.sum(values * scale * grad, axis=0, keepdims=True)
    return scale * scaled - values * (scale * scale * scale * mean), part


def branch_sum(partial, middle, gain, grad_out, experts, local_experts, later):
    count, rows, width = partial.shape
    planes = lax.axis_size(PLANE)
    routed, waiting = len(experts), len(later)

    def kernel(*refs):
        partial_ref, middle_ref, gain_ref, grad_ref = refs[:4]
        expert_refs = refs[4 : 4 + routed]
        outputs = refs[4 + routed + waiting :]
        grad_middle, grad_gain, branch_all = outputs[:3]
        results = outputs[3 : 3 + routed]
        scratch = list(outputs[3 + routed + waiting :])
        inbox, branch, reduce_send, reduce_recv, own, line_send, line_recv = scratch[:7]
        rest = scratch[7:]
        meet((1, 2, 4, 6), True)
        reduce_stages, reduce_finish = line_reduce_steps(
            partial_ref, inbox, reduce_send, reduce_recv
        )
        begin, forward, finish = line_gather_steps(branch_all, line_send, line_recv, rows)
        part = rows // LINE_PARTS

        def ready(span, c):
            back, gain_part = norm_back(middle_ref[span], gain_ref[...], grad_middle[span])
            grad_gain[...] = gain_part if c == 0 else grad_gain[...] + gain_part
            back = wide(grad_ref[span]) + back
            grad_middle[span] = back
            branch[span] = low(back)
            begin(c, branch.at[span])

        def line_task():
            grad_middle[...] = jnp.zeros((rows, width), jnp.float32)
            yield from reduce_stages(grad_middle, ready)
            local = pltpu.make_async_copy(branch, branch_all.at[lax.axis_index(EXPERT_AXIS)], own)
            local.start()
            for distance in range(1, count):
                for c in range(LINE_PARTS):
                    forward(c, distance)
                yield 1
            local.wait()
            finish(lambda c: branch.at[pl.ds(c * part, part)])
            reduce_finish()

        task_kind = plane_scatter_task if local_experts == 1 else expert_return_task
        size = len(rest) // routed
        tasks = [
            task_kind(
                expert_refs[i], results[i], *rest[size * i : size * (i + 1)]
            )
            for i in range(routed)
        ]
        line = line_task()
        for stage in range(5):
            for task in tasks:
                next(task)
            if stage:
                next(line)
        run_tasks(line)
        run_tasks(*tasks)

    shapes = [
        jax.ShapeDtypeStruct((rows, width), jnp.float32),
        jax.ShapeDtypeStruct((1, width), jnp.float32),
        jax.ShapeDtypeStruct((count, rows, width), jnp.bfloat16),
    ]
    scratch = [
        pltpu.VMEM((count + 1, rows, width), jnp.bfloat16),
        pltpu.VMEM((rows, width), jnp.bfloat16),
    ]
    scratch += line_semaphores() + [pltpu.SemaphoreType.DMA(())] + line_semaphores()
    for expert in experts:
        shard, columns = expert.shape[0] // planes, expert.shape[1]
        if local_experts == 1:
            shapes.append(jax.ShapeDtypeStruct((shard, columns), jnp.float32))
            scratch += plane_scatter_scratch(shard, columns)
        else:
            shapes.append(jax.ShapeDtypeStruct((local_experts, shard, columns), jnp.bfloat16))
            scratch += expert_return_scratch(shard, columns)
    shapes += [jax.ShapeDtypeStruct(x.shape, x.dtype) for x in later]
    results = pl.pallas_call(
        kernel,
        out_shape=shapes,
        in_specs=[INSIDE] * 4 + [ANY] * (routed + waiting),
        out_specs=[INSIDE, INSIDE, ANY]
        + [INSIDE if local_experts == 1 else ANY] * routed
        + [ANY] * waiting,
        input_output_aliases={4 + routed + i: 3 + routed + i for i in range(waiting)},
        scratch_shapes=scratch,
        compiler_params=kernel_params(3),
        cost_estimate=pl.CostEstimate(
            flops=60_000_000, bytes_accessed=300_000_000, transcendentals=0
        ),
        name="branch_sum",
    )(partial, middle, gain, grad_out, *experts, *later)
    grads = [
        wide(r).reshape((local_experts,) + r.shape[-2:]) for r in results[3 : 3 + routed]
    ]
    return results[0], results[1][0], results[2], grads, results[3 + routed :]


def meet_all():
    planes, count = lax.axis_size(PLANE), lax.axis_size(EXPERT_AXIS)
    for mask in range(1, planes):
        signal(plane_device(mask))
    for mask in range(1, count):
        signal({EXPERT_AXIS: jnp.bitwise_xor(lax.axis_index(EXPERT_AXIS), mask)})
    pl.semaphore_wait(pltpu.get_barrier_semaphore(), planes + count - 2)


def closing(grad_first, first_full, normed, ready_before, source, gain, grad_middle, gain_grads, matrices, spread):
    rows, width = source.shape
    count = lax.axis_size(EXPERT_AXIS)
    planes = lax.axis_size(PLANE)
    number = len(matrices) + 1
    sizes = [first_full.shape] + [m.shape for m in matrices]
    depth = gain_grads.shape[2]
    shard, columns = first_full.shape[0] // planes, first_full.shape[1]
    thin = shard // count

    def kernel(*refs):
        first_ref, full_ref, normed_ref, _, source_ref, gain_ref, middle_ref, gains_ref = refs[:8]
        sources = list(refs[8 : 7 + number])
        grad_tokens, gains_out, thin_out = refs[7 + number : 10 + number]
        results = refs[10 + number : 10 + 2 * number]
        scratch = list(refs[10 + 2 * number :])
        partial_ref, back_ref = scratch.pop(), scratch.pop()
        sources = [back_ref] + sources
        inbox, reduce_send, reduce_recv, gain_row = scratch[:4]
        gain_part, gain_box, gain_send, gain_recv = scratch[4:8]
        gain_held, gain_far, far_send, far_recv, thin_box, thin_send, thin_recv = scratch[8:15]
        rest = scratch[15:]
        meet_all()
        place = lax.axis_index(EXPERT_AXIS)
        here = plane_here()
        reduce_stages, reduce_finish = line_reduce_steps(
            partial_ref, inbox, reduce_send, reduce_recv
        )

        def ready(span, c):
            back, row = norm_back(wide(source_ref[span]), gain_ref[...], grad_tokens[span])
            gain_row[...] = row if c == 0 else gain_row[...] + row
            grad_tokens[span] = middle_ref[span] + back

        def line_task():
            grad_tokens[...] = jnp.zeros((rows, width), jnp.float32)
            yield from reduce_stages(grad_tokens, ready)
            gain_part[...] = gains_ref[...]
            for i in range(planes):
                gain_part[i, 0:1, :] = gain_row[:, i * depth : (i + 1) * depth]
            copies = []
            for mask in range(1, planes):
                copy = remote(
                    gain_part.at[jnp.bitwise_xor(here, mask)],
                    gain_box.at[mask],
                    gain_send.at[mask],
                    gain_recv.at[mask],
                    plane_device(mask),
                )
                copy.start()
                copies.append(copy)
            gain_total = gain_part[here]
            yield 1
            for mask in range(1, planes):
                arrived(gain_box.at[mask], gain_send.at[mask], gain_recv.at[mask])
                gain_total = gain_total + gain_box[mask]
            gain_held[...] = gain_total
            for mask in range(1, count):
                copy = remote(
                    gain_held,
                    gain_far.at[mask],
                    far_send.at[mask],
                    far_recv.at[mask],
                    {EXPERT_AXIS: jnp.bitwise_xor(place, mask)},
                )
                copy.start()
                copies.append(copy)
            yield 1
            for mask in range(1, count):
                arrived(gain_far.at[mask], far_send.at[mask], far_recv.at[mask])
                gain_total = gain_total + gain_far[mask]
            gains_out[...] = gain_total
            for copy in copies:
                copy.wait_send()
            reduce_finish()

        def first_task(task):
            yield from task
            copies = []

            def piece(mask):
                start = pl.multiple_of(jnp.bitwise_xor(place, mask) * thin, 8 if thin % 8 == 0 else thin)
                return results[0].at[pl.ds(start, thin), pl.ds(spread, columns - spread)]

            for mask in range(1, count):
                copy = remote(
                    piece(mask),
                    thin_box.at[mask],
                    thin_send.at[mask],
                    thin_recv.at[mask],
                    {EXPERT_AXIS: jnp.bitwise_xor(place, mask)},
                )
                copy.start()
                copies.append(copy)
            yield 1
            total = piece(0)[...]
            for mask in range(1, count):
                arrived(thin_box.at[mask], thin_send.at[mask], thin_recv.at[mask])
                total = total + thin_box[mask]
            thin_out[...] = total
            for copy in copies:
                copy.wait_send()

        size = len(rest) // number
        tasks = [
            plane_scatter_task(sources[i], results[i], *rest[size * i : size * (i + 1)])
            for i in range(number)
        ]
        tasks[0] = first_task(tasks[0])
        for task in tasks[1:]:
            next(task)

        def back_tile(i, carry):
            span = pl.ds(pl.multiple_of(i * 256, 256), 256)
            back_ref[span] = low(product_left(normed_ref[:, span], first_ref[...]))
            return carry

        lax.fori_loop(0, width // 256, back_tile, 0)
        for task in tasks:
            next(task)

        def partial_tile(i, carry):
            span = pl.ds(pl.multiple_of(i * 2 * rows, 2 * rows), 2 * rows)
            tile = low(product_right(first_ref[span], full_ref[...]))
            partial_ref[2 * i] = tile[:rows]
            partial_ref[2 * i + 1] = tile[rows:]
            return carry

        lax.fori_loop(0, count // 2, partial_tile, 0)
        line = line_task()
        for stage in range(5):
            for task in tasks if stage < 4 else tasks[:1]:
                next(task)
            next(line)
        run_tasks(line, *tasks)

    shapes = [
        jax.ShapeDtypeStruct((rows, width), jnp.float32),
        jax.ShapeDtypeStruct(gain_grads.shape[1:], jnp.float32),
        jax.ShapeDtypeStruct((thin, columns - spread), jnp.float32),
    ] + [jax.ShapeDtypeStruct((m[0] // planes, m[1]), jnp.float32) for m in sizes]
    scratch = [pltpu.VMEM((count + 1, rows, width), jnp.bfloat16)]
    scratch += line_semaphores()
    scratch += [
        pltpu.VMEM((1, width), jnp.float32),
        pltpu.VMEM(gain_grads.shape, jnp.float32),
        pltpu.VMEM(gain_grads.shape, jnp.float32),
        pltpu.SemaphoreType.DMA((planes,)),
        pltpu.SemaphoreType.DMA((planes,)),
        pltpu.VMEM(gain_grads.shape[1:], jnp.float32),
        pltpu.VMEM((count,) + gain_grads.shape[1:], jnp.float32),
        pltpu.SemaphoreType.DMA((count,)),
        pltpu.SemaphoreType.DMA((count,)),
        pltpu.VMEM((count, thin, columns - spread), jnp.float32),
        pltpu.SemaphoreType.DMA((count,)),
        pltpu.SemaphoreType.DMA((count,)),
    ]
    for m in sizes:
        scratch += plane_scatter_scratch(m[0] // planes, m[1])
    scratch += [
        pltpu.VMEM(first_full.shape, jnp.bfloat16),
        pltpu.VMEM((count, rows, width), jnp.bfloat16),
    ]
    results = pl.pallas_call(
        kernel,
        out_shape=shapes,
        in_specs=[INSIDE] * 3 + [ANY] + [INSIDE] * 4 + [ANY] * len(matrices),
        out_specs=[INSIDE] * (3 + number),
        scratch_shapes=scratch,
        compiler_params=kernel_params(4),
        cost_estimate=pl.CostEstimate(
            flops=60_000_000, bytes_accessed=200_000_000, transcendentals=0
        ),
        name="closing",
    )(grad_first, first_full, normed, ready_before, source, gain, grad_middle, gain_grads, *matrices)
    return results[:3], results[3:]


def silu_back(gate, up, grad):
    sigmoid_part = 1.0 / (1.0 + jnp.exp(-gate))
    silu_part = gate * sigmoid_part
    slope = sigmoid_part * (1.0 + gate * (1.0 - sigmoid_part))
    return silu_part * up, grad * up * slope, grad * silu_part


def row_copies(source, target, send, recv, copies):
    return [
        remote(source(k), target(k), send.at[k], recv.at[k], plane_device(k * copies))
        for k in (3, 1, 2)
    ]


def shared_and_rows(hidden, grads, weights, hidden_slots, grad_slots, gates, copies):
    tokens, width = hidden.shape
    columns = weights.shape[1] // 3
    pieces, slots = hidden_slots.shape[:2]
    exchanged = copies > 0
    tall = max(t for t in (256, 128, tokens) if tokens % t == 0)
    wide_part = 256

    def kernel(*refs):
        hidden_any, grads_any, weights_any, rows_any, grad_rows_any, gates_ref = refs[:6]
        act_out, back_out, weight_grads = refs[6:9]
        outputs = refs[9:12]
        scratch = refs[12:] if exchanged else refs[9:]
        hid, grd, wts, both, load = scratch[:5]
        loads = [
            pltpu.make_async_copy(hidden_any, hid, load.at[0]),
            pltpu.make_async_copy(weights_any, wts, load.at[1]),
            pltpu.make_async_copy(grads_any, grd, load.at[2]),
        ]
        moves = []
        if exchanged:
            semaphores = scratch[5:]
            meet([k * copies for k in (1, 2, 3)], False)
            for i, source in enumerate((gates_ref, rows_any, grad_rows_any)):
                moves += row_copies(
                    lambda k, source=source: source.at[k],
                    lambda k, i=i: outputs[i].at[k - 1],
                    semaphores[2 * i],
                    semaphores[2 * i + 1],
                    copies,
                )
            for move in moves:
                move.start()
        for copy in loads:
            copy.start()
        for copy in loads:
            copy.wait()

        def rows_tile(i, carry):
            span = pl.ds(pl.multiple_of(i * tall, 16), tall)
            gate = product(hid[span], wts[:, :columns])
            up = product(hid[span], wts[:, columns : 2 * columns])
            grad = product(grd[span], wts[:, 2 * columns :])
            act, dgate, dup = silu_back(gate, up, grad)
            act_out[span] = low(act)
            both[span, :columns] = low(dgate)
            both[span, columns:] = low(dup)
            back_out[span] = product_right(both[span], wts[:, : 2 * columns])
            return carry

        lax.fori_loop(0, tokens // tall, rows_tile, 0)

        def weights_tile(i, carry):
            span = pl.ds(pl.multiple_of(i * wide_part, wide_part), wide_part)
            weight_grads[span, : 2 * columns] = low(product_left(hid[:, span], both[...]))
            weight_grads[span, 2 * columns :] = low(product_left(grd[:, span], act_out[...]))
            return carry

        lax.fori_loop(0, width // wide_part, weights_tile, 0)
        for move in moves:
            move.wait()

    shapes = [
        jax.ShapeDtypeStruct((tokens, columns), jnp.bfloat16),
        jax.ShapeDtypeStruct((tokens, width), jnp.float32),
        jax.ShapeDtypeStruct(weights.shape, jnp.bfloat16),
    ]
    out_specs = [INSIDE] * 3
    scratch = [
        pltpu.VMEM(hidden.shape, jnp.bfloat16),
        pltpu.VMEM(grads.shape, jnp.bfloat16),
        pltpu.VMEM(weights.shape, jnp.bfloat16),
        pltpu.VMEM((tokens, 2 * columns), jnp.bfloat16),
        pltpu.SemaphoreType.DMA((3,)),
    ]
    if exchanged:
        shapes += [jax.ShapeDtypeStruct((3,) + x.shape[1:], x.dtype) for x in (gates, hidden_slots, grad_slots)]
        out_specs += [INSIDE, ANY, ANY]
        scratch += [pltpu.SemaphoreType.DMA((4,))] * 6
    results = pl.pallas_call(
        kernel,
        out_shape=shapes,
        in_specs=[ANY] * 5 + [INSIDE],
        out_specs=out_specs,
        scratch_shapes=scratch,
        compiler_params=kernel_params(5) if exchanged else pltpu.CompilerParams(vmem_limit_bytes=60 << 20),
        cost_estimate=pl.CostEstimate(
            flops=12 * tokens * width * columns, bytes_accessed=120_000_000, transcendentals=0
        ),
        name="shared_and_rows",
    )(hidden, grads, weights, hidden_slots, grad_slots, gates)
    return results[:3], results[3:]


def routed_expert(hidden_slots, grad_slots, hidden_far, grad_far, gates, weights, copies):
    slots, width = hidden_slots.shape[1:]
    gate_full, up_full, down_full = weights
    units = gate_full.shape[1]
    exchanged = copies > 0

    def kernel(*refs):
        far = 2 if exchanged else 0
        hidden_any, grad_any = refs[:2]
        hidden_far_any, grad_far_any = refs[2:4] if exchanged else (None, None)
        gates_ref, wg_any, wu_any, wd_any = refs[2 + far : 6 + far]
        pair_back, result_back, scale_back, dwg, dwu, dwd = refs[6 + far : 12 + far]
        scratch = refs[12 + far :]
        wg, wu, wd, hid, grd, act, dgate, dup, pair, result, scale = scratch[:11]
        tile_up, tile_down, load, own, store = scratch[11:16]
        semaphores = scratch[16:]

        def piece(ref, ref_far, k):
            return ref.at[k] if k == 0 or not exchanged else ref_far.at[k - 1]

        if exchanged:
            meet([k * copies for k in (1, 2, 3)], False)
        loads = {}

        def fetch(number, source, target):
            loads[number] = pltpu.make_async_copy(source, target, load.at[number])
            loads[number].start()

        def fetch_rows(number, source, source_far, target, k):
            span = pl.ds(k * slots, slots)
            fetch(number + k, piece(source, source_far, k), target.at[span])

        fetch(0, wg_any, wg)
        fetch_rows(3, hidden_any, hidden_far_any, hid, 3)
        loads[0].wait()
        loads[6].wait()
        fetch(1, wu_any, wu)
        fetch(2, wd_any, wd)
        for k in (3, 2, 1, 0):
            fetch_rows(7, grad_any, grad_far_any, grd, k)
            if k < 3:
                fetch_rows(3, hidden_any, hidden_far_any, hid, k)

        def back(k, which):
            source, target = ((pair, pair_back), (result, result_back), (scale, scale_back))[which]
            return remote(
                source.at[k],
                target.at[k],
                semaphores[2 * which].at[k],
                semaphores[2 * which + 1].at[k],
                plane_device(k * copies),
            )

        def deliver(k, which):
            if exchanged:
                pl.when(k > 0)(lambda: back(k, which).start())

        def first(i, carry):
            k = 3 - i
            span = pl.ds(pl.multiple_of(k * slots, 16), slots)

            def ready(*numbers):
                @pl.when(i == 0)
                def _():
                    for number in numbers:
                        loads[number].wait()

            gate = product(hid[span], wg[...])
            ready(1)
            up = product(hid[span], wu[...])
            ready(2, 10, 9, 8, 7, 5, 4, 3)
            grad = product_right(grd[span], wd[...])
            gates_here = gates_ref[span]
            act_part, dgate_part, dup_part = silu_back(gate, up, grad)
            scale[k] = jnp.broadcast_to(
                jnp.sum(act_part * grad, axis=-1, keepdims=True), scale.shape[1:]
            )
            act[span] = low(act_part * gates_here)
            dgate[span] = low(dgate_part * gates_here)
            dup[span] = low(dup_part * gates_here)
            pair[k] = low(product_right(dgate[span], wg[...]) + product_right(dup[span], wu[...]))
            deliver(k, 0)
            deliver(k, 2)
            result[k] = low(product(act[span], wd[...]))
            deliver(k, 1)
            return carry

        lax.fori_loop(0, 4, first, 0)
        kept = []
        for which, (source, target) in enumerate(
            ((pair, pair_back), (result, result_back), (scale, scale_back))
        ):
            for k in range(1 if exchanged else 4):
                copy = pltpu.make_async_copy(source.at[k], target.at[k], own.at[which, k])
                copy.start()
                kept.append(copy)

        def tiles(count, rows, buffer, target, compute):
            def put(i, slot):
                start = pl.multiple_of(i * rows, 16)
                return pltpu.make_async_copy(
                    buffer.at[slot], target.at[pl.ds(start, rows)], store.at[slot]
                )

            def tile(i, carry):
                slot = lax.rem(i, 2)
                pl.when(i >= 2)(lambda: put(i - 2, slot).wait())
                buffer[slot] = compute(pl.ds(pl.multiple_of(i * rows, rows), rows))
                put(i, slot).start()
                return carry

            lax.fori_loop(0, count, tile, 0)
            for i in (count - 2, count - 1):
                put(i, i % 2).wait()

        tiles(width // 256, 256, tile_up, dwg, lambda s: low(product_left(hid[:, s], dgate[...])))
        tiles(width // 256, 256, tile_up, dwu, lambda s: low(product_left(hid[:, s], dup[...])))
        tiles(units // 128, 128, tile_down, dwd, lambda s: low(product_left(act[:, s], grd[...])))
        for copy in kept:
            copy.wait()
        if exchanged:
            for which in (0, 2, 1):
                for k in (3, 2, 1):
                    back(k, which).wait()

    shapes = [
        jax.ShapeDtypeStruct((4, slots, width), jnp.bfloat16),
        jax.ShapeDtypeStruct((4, slots, width), jnp.bfloat16),
        jax.ShapeDtypeStruct((4, slots, 128), jnp.float32),
    ] + [jax.ShapeDtypeStruct(w.shape, jnp.bfloat16) for w in weights]
    rows = 4 * slots
    scratch = [pltpu.VMEM(w.shape, jnp.bfloat16) for w in weights]
    scratch += [pltpu.VMEM((rows, width), jnp.bfloat16)] * 2
    scratch += [pltpu.VMEM((rows, units), jnp.bfloat16)] * 3
    scratch += [pltpu.VMEM((4, slots, width), jnp.bfloat16)] * 2
    scratch += [pltpu.VMEM((4, slots, 128), jnp.float32)]
    scratch += [
        pltpu.VMEM((2, 256, units), jnp.bfloat16),
        pltpu.VMEM((2, 128, width), jnp.bfloat16),
        pltpu.SemaphoreType.DMA((11,)),
        pltpu.SemaphoreType.DMA((3, 4)),
        pltpu.SemaphoreType.DMA((2,)),
    ]
    if exchanged:
        scratch += [pltpu.SemaphoreType.DMA((4,))] * 6
    operands = [hidden_slots, grad_slots] + ([hidden_far, grad_far] if exchanged else [])
    results = pl.pallas_call(
        kernel,
        out_shape=shapes,
        in_specs=[ANY] * len(operands) + [INSIDE] + [ANY] * 3,
        out_specs=[ANY] * 6,
        scratch_shapes=scratch,
        compiler_params=pltpu.CompilerParams(
            collective_id=6, has_side_effects=True, vmem_limit_bytes=60 << 20
        )
        if exchanged
        else pltpu.CompilerParams(vmem_limit_bytes=60 << 20),
        cost_estimate=pl.CostEstimate(
            flops=18 * rows * units * width, bytes_accessed=200_000_000, transcendentals=0
        ),
        name="routed_expert",
    )(*operands, gates, *weights)
    return results


def attention_back(branch, out, probs, expanded, query_nope, query_rope, keys, up):
    groups, rows, width = branch.shape
    heads, key_count = probs.shape[1], probs.shape[3]
    rope = query_rope.shape[2]
    score_scale = (NOPE + ROPE) ** (-0.5)

    def kernel(*refs):
        branch_ref, out_ref, probs_ref, exp_ref, nope_ref, rope_ref, keys_ref, up_ref = refs[:8]
        dnope, drope, dkeys, dup, dexp = refs[8:]
        fold = rope_fold(rope)
        tiled = low(product_right(keys_ref[:, LATENT:], fold))
        dmixed = low(product(branch_ref[...], out_ref[...]))
        drope_sum = jnp.zeros((rows, rope), jnp.float32)
        dkey_sum = jnp.zeros((key_count, rope), jnp.float32)
        for h in range(heads):
            nope_span = slice(h * NOPE, (h + 1) * NOPE)
            key_span = slice(h * (NOPE + VDIM), h * (NOPE + VDIM) + NOPE)
            value_span = slice(h * (NOPE + VDIM) + NOPE, (h + 1) * (NOPE + VDIM))
            mask = head_mask(h, heads, rope)
            weights = probs_ref[h]
            part = dmixed[:, h * VDIM : (h + 1) * VDIM]
            dprobs = product_right(part, exp_ref[:, value_span])
            wide_weights = wide(weights)
            delta = jnp.sum(wide_weights * dprobs, axis=-1, keepdims=True)
            dscore = low(wide_weights * (dprobs - delta) * score_scale)
            dexp[:, key_span] = low(product_left(dscore, nope_ref[:, nope_span]))
            dexp[:, value_span] = low(product_left(weights, part))
            dnope[:, nope_span] = low(product(dscore, exp_ref[:, key_span]))
            drope_sum = drope_sum + product(dscore, tiled) * mask
            dkey_sum = dkey_sum + product_left(dscore, rope_ref[...] * low(mask))
        drope[...] = drope_sum
        dkeys[:, :LATENT] = product_right(dexp[...], up_ref[...])
        dkeys[:, LATENT:] = product(low(dkey_sum), fold)
        grad_up = product_left(keys_ref[:, :LATENT], dexp[...])

        @pl.when(pl.program_id(0) == 0)
        def _():
            dup[...] = grad_up

        @pl.when(pl.program_id(0) > 0)
        def _():
            dup[...] = dup[...] + grad_up

    def group(array):
        shape = array.shape
        return pl.BlockSpec(
            (None,) + tuple(shape[1:]), lambda g, n=len(shape) - 1: (g,) + (0,) * n
        )

    def whole(array):
        return pl.BlockSpec(array.shape, lambda g: (0, 0))

    shapes = [
        jax.ShapeDtypeStruct((groups, rows, heads * NOPE), jnp.bfloat16),
        jax.ShapeDtypeStruct((groups, rows, rope), jnp.float32),
        jax.ShapeDtypeStruct((groups, key_count, LATENT + ROPE), jnp.float32),
        jax.ShapeDtypeStruct(up.shape, jnp.float32),
    ]
    operands = [branch, out, probs, expanded, query_nope, query_rope, keys, up]
    return pl.pallas_call(
        kernel,
        grid=(groups,),
        out_shape=shapes,
        in_specs=[whole(x) if x is out or x is up else group(x) for x in operands],
        out_specs=[group(x) for x in shapes[:3]] + [whole(up)],
        scratch_shapes=[pltpu.VMEM((key_count, heads * (NOPE + VDIM)), jnp.bfloat16)],
        compiler_params=pltpu.CompilerParams(vmem_limit_bytes=40 << 20),
        cost_estimate=pl.CostEstimate(
            flops=20_000_000_000, bytes_accessed=30_000_000, transcendentals=0
        ),
        name="attention_back",
    )(*operands)


def body(
    tokens,
    routes,
    grad_out,
    attn_gain,
    query_weight,
    latent_down,
    latent_gain,
    latent_up,
    out_weight,
    ffn_gain,
    router_weight,
    shared_gate,
    shared_up,
    shared_down,
    expert_gate,
    expert_up,
    expert_down,
):
    contexts = lax.axis_size(CONTEXT_AXIS)
    context_index = lax.axis_index(CONTEXT_AXIS)
    groups_local = lax.axis_size(EXPERT_AXIS)
    expert_index = lax.axis_index(EXPERT_AXIS)
    plane_count = lax.axis_size(PLANE)
    plane_index = lax.axis_index(PLANE)
    local_experts = expert_gate.shape[0]
    experts_all = router_weight.shape[1]
    copies = plane_count // local_experts
    expert_own = plane_index // copies
    query_cols = query_weight.shape[1]
    heads_local = query_cols // (NOPE + ROPE)
    down_cols = LATENT + ROPE
    shard_rows = query_weight.shape[0]
    latent_rows = latent_up.shape[0]
    prompt_len = PROMPT_DEV * contexts
    capacity = (TOK_DEV * TOPK * 9 + 8 * experts_all - 1) // (8 * experts_all)
    slots = groups_local * capacity
    slots = -(-slots // 16) * 16 if local_experts > 1 else -(-slots // 64) * 64
    token_count = groups_local * TOK_DEV
    score_scale = (NOPE + ROPE) ** (-0.5)

    half_rope = ROPE // 2
    rope_cols = heads_local * half_rope
    nope_cols = heads_local * NOPE

    def query_split(columns):
        each = columns.reshape(columns.shape[0], heads_local, NOPE + ROPE)
        parts = (each[..., :NOPE], each[..., NOPE : NOPE + half_rope], each[..., NOPE + half_rope :])
        return [part.reshape(columns.shape[0], -1) for part in parts]

    def query_join(columns):
        rows = columns.shape[0]
        parts = (
            columns[:, :nope_cols],
            columns[:, nope_cols : nope_cols + rope_cols],
            columns[:, nope_cols + rope_cols :],
        )
        each = [part.reshape(rows, heads_local, -1) for part in parts]
        return jnp.concatenate(each, axis=-1).reshape(rows, query_cols)

    used_cols = query_cols + down_cols
    extra_cols = experts_all + 3
    pad_cols = -(used_cols + extra_cols) % 128
    gains = jnp.stack(
        [
            wide(attn_gain),
            wide(ffn_gain),
            jnp.pad(wide(latent_gain), (0, shard_rows - latent_gain.shape[0])),
        ]
        + [jnp.zeros((shard_rows,), jnp.float32)] * 5
    )
    first_local = jnp.concatenate(
        [
            *query_split(query_weight),
            latent_down,
            router_weight,
            jnp.zeros((shard_rows, 3 + pad_cols), jnp.bfloat16),
        ],
        axis=1,
    )
    shared_cols = shared_gate.shape[1]
    shared_pad = -(-shared_cols // 128) * 128

    def padded(weight):
        return jnp.pad(weight, ((0, 0), (0, shared_pad - shared_cols)))

    shared_own = jnp.concatenate(
        [padded(shared_gate), padded(shared_up), padded(shared_down.T)], axis=1
    )
    shared_whole = lax.all_gather(shared_own, PLANE, axis=0, tiled=True)
    gains_all, normed_all, (first_full, up_local, out_local) = opening(
        tokens[0], gains, [first_local, latent_up, out_weight.T]
    )
    full_router = first_full[:, used_cols : used_cols + experts_all]
    full_attn_gain = gains_all[:, 0].reshape(D)
    full_ffn_gain = gains_all[:, 1].reshape(D)
    full_latent_gain = gains_all[:, 2, : latent_gain.shape[0]].reshape(LATENT)

    within = jnp.arange(TOK_DEV, dtype=jnp.int32)
    query_places = jnp.where(
        within < PROMPT_DEV, context_index * PROMPT_DEV + within, prompt_len + within - PROMPT_DEV
    )
    cosine, sine_part = rotary_tables(query_places.astype(jnp.float32), ROPE // 2)
    source = wide(tokens[0])

    def pack_latent(comp_rows, latent_scale):
        return jnp.concatenate(
            [
                norm_rows(comp_rows[..., :LATENT], latent_scale),
                rotate(comp_rows[..., LATENT:], cosine[None], sine_part[None]),
            ],
            axis=-1,
        )

    routes_all = axis_gather(routes[0], EXPERT_AXIS)
    first_product = product(normed_all, first_full)
    compressed = first_product[..., query_cols:used_cols]
    packed = low(pack_latent(compressed, wide(full_latent_gain)))
    key_count = prompt_len + CONT_LEN
    keys = jnp.zeros((groups_local, contexts + 1, PROMPT_DEV, down_cols), jnp.bfloat16)
    prompt_own = packed[:, :PROMPT_DEV]
    for mask in range(contexts):
        came = swap(prompt_own, CONTEXT_AXIS, mask) if mask else prompt_own
        keys = lax.dynamic_update_slice(
            keys, came[:, None], (0, jnp.bitwise_xor(context_index, mask), 0, 0)
        )
    keys = lax.dynamic_update_slice(
        keys, packed[:, None, PROMPT_DEV:], (0, contexts, 0, 0)
    ).reshape(groups_local, key_count, down_cols)
    query_nope = low(first_product[..., :nope_cols])
    cosine_heads = jnp.tile(cosine, (1, heads_local))[None]
    sine_heads = jnp.tile(sine_part, (1, heads_local))[None]
    lower = first_product[..., nope_cols : nope_cols + rope_cols]
    upper = first_product[..., nope_cols + rope_cols : query_cols]
    query_rope = low(
        jnp.concatenate(
            [
                lower * cosine_heads - upper * sine_heads,
                upper * cosine_heads + lower * sine_heads,
            ],
            axis=-1,
        )
    )
    slot_experts = expert_index * local_experts + (
        expert_own ^ jnp.arange(local_experts, dtype=jnp.int32)
    )
    expert_cols = jnp.arange(experts_all, dtype=jnp.int32)[:, None] == slot_experts[None, :]
    chosen_slots = jnp.any(routes_all[..., None] == slot_experts, axis=2)
    before = (within[:, None] > within[None, :]).astype(jnp.bfloat16)
    rank = jnp.einsum(
        "ts,gsl->gtl",
        before,
        chosen_slots.astype(jnp.bfloat16),
        preferred_element_type=jnp.float32,
    ).astype(jnp.int32)
    slot_of = jnp.where(
        chosen_slots,
        rank + capacity * jnp.arange(groups_local, dtype=jnp.int32)[:, None, None],
        -1,
    ).reshape(token_count, local_experts)
    picked = (
        slot_of.T[:, None, :] == jnp.arange(slots, dtype=jnp.int32)[None, :, None]
    )
    picked_low = picked.astype(jnp.bfloat16).reshape(local_experts * slots, token_count)
    piece_slots = slots * local_experts // 4
    (middle, hidden_all, grad_all, mixed_all, probs, expanded), fetched = middle_sum(
        query_nope,
        query_rope,
        keys,
        up_local,
        out_local,
        tokens[0],
        full_ffn_gain[None],
        [expert_gate, expert_up, expert_down],
        grad_out[0],
    )
    gate_full, up_full, down_full = fetched
    hidden_flat = hidden_all.reshape(token_count, D)

    grad_flat = grad_all.reshape(token_count, D)
    hidden_slots = low(product(picked_low, hidden_flat)).reshape(4, piece_slots, D)
    grad_slots = low(product(picked_low, grad_flat)).reshape(4, piece_slots, D)
    logits = product(hidden_flat, full_router)
    expert_probs = jax.nn.softmax(logits, axis=-1)
    gate_tokens = jnp.sum(jnp.where(expert_cols[None], expert_probs[:, :, None], 0.0), axis=1)
    gate_slots = jnp.sum(jnp.where(picked, gate_tokens.T[:, None, :], 0.0), axis=-1)
    gate_slots = gate_slots.reshape(4, piece_slots)
    gates_padded = jnp.broadcast_to(
        jnp.pad(gate_slots, ((0, 0), (0, -piece_slots % 128)))[:, None], (4, 8, -(-piece_slots // 128) * 128)
    )
    row_hops = copies if local_experts > 1 else 0
    (act_shared, shared_hidden, shared_grads), far = shared_and_rows(
        hidden_flat, grad_flat, shared_whole, hidden_slots, grad_slots, gates_padded, row_hops
    )
    gates_far, hidden_far, grad_far = far if far else (None, None, None)
    if far:
        gate_slots = jnp.concatenate([gate_slots[:1], gates_far[:, 0, :piece_slots]], axis=0)
    pair_back, result, scale_back, *expert_partials = routed_expert(
        hidden_slots,
        grad_slots,
        hidden_far,
        grad_far,
        gate_slots.reshape(-1, 1),
        [gate_full, up_full, down_full],
        row_hops,
    )
    grad_gate_back = scale_back[:, :, 0].reshape(local_experts, slots)
    grad_routed = product_left(picked_low, pair_back.reshape(-1, D))
    grad_gate_tokens = jnp.sum(jnp.where(picked, grad_gate_back[:, :, None], 0.0), axis=1).T
    grad_spread = jnp.sum(
        jnp.where(expert_cols[None], grad_gate_tokens[:, None, :], 0.0), axis=-1
    )
    weighted = jnp.sum(expert_probs * grad_spread, axis=-1, keepdims=True)
    grad_logits = expert_probs * (grad_spread - weighted)
    grad_router = lax.dot_general(
        grad_logits,
        wide(hidden_flat),
        (((0,), (0,)), ((), ())),
        precision=lax.Precision.HIGHEST,
    )
    grad_from_router = lax.dot_general(
        grad_logits,
        wide(full_router),
        (((1,), (1,)), ((), ())),
        precision=lax.Precision.HIGHEST,
    )
    grad_hidden_part = low(
        shared_hidden + grad_routed + grad_from_router
    )
    grad_middle, grad_ffn_gain, branch_all, expert_grads, (result, shared_grads) = branch_sum(
        grad_hidden_part.reshape(groups_local, TOK_DEV, D),
        middle,
        full_ffn_gain[None],
        grad_out[0],
        expert_partials,
        local_experts,
        [result.reshape(-1, D), shared_grads],
    )
    shared_grads = wide(lax.psum_scatter(shared_grads, PLANE, scatter_dimension=0, tiled=True))
    routed_term = product_left(picked_low, result)
    branch_out = low(
        product_right(act_shared, shared_whole[:, 2 * shared_pad :]) + routed_term
    )
    grad_out_weight = low(
        product_left(
            branch_all.reshape(token_count, D), mixed_all.reshape(token_count, heads_local * VDIM)
        )
    )
    grad_nope, grad_rope, grad_keys, grad_latent_up = attention_back(
        branch_all,
        out_local,
        probs,
        expanded,
        query_nope,
        query_rope,
        keys,
        up_local,
    )
    lower, upper = grad_rope[..., :rope_cols], grad_rope[..., rope_cols:]
    grad_query_raw = jnp.concatenate(
        [
            grad_nope,
            low(lower * cosine_heads + upper * sine_heads),
            low(upper * cosine_heads - lower * sine_heads),
        ],
        axis=-1,
    )
    grad_keys = grad_keys.reshape(groups_local, contexts + 1, PROMPT_DEV, down_cols)

    def keys_of(mask):
        return lax.dynamic_index_in_dim(
            grad_keys, jnp.bitwise_xor(context_index, mask), 1, keepdims=False
        )

    prompt_sum = keys_of(0)
    for mask in range(1, contexts):
        prompt_sum = prompt_sum + wide(swap(low(keys_of(mask)), CONTEXT_AXIS, mask))
    grad_packed = jnp.concatenate([prompt_sum, grad_keys[:, contexts]], axis=1)
    _, pack_back = jax.vjp(pack_latent, compressed, wide(full_latent_gain))
    grad_compressed, grad_latent_gain = pack_back(grad_packed)
    grad_first = jnp.concatenate(
        [
            grad_query_raw,
            low(grad_compressed),
            jnp.zeros((groups_local, TOK_DEV, first_full.shape[1] - used_cols), jnp.bfloat16),
        ],
        axis=-1,
    )
    gain_rows = jnp.concatenate(
        [
            jnp.zeros((plane_count, 1, shard_rows), jnp.float32),
            grad_ffn_gain.reshape(plane_count, 1, shard_rows),
            jnp.pad(
                grad_latent_gain.reshape(plane_count, 1, latent_rows),
                ((0, 0), (0, 0), (0, shard_rows - latent_rows)),
            ),
            grad_router.reshape(experts_all, plane_count, shard_rows).transpose(1, 0, 2),
            jnp.zeros((plane_count, -(3 + experts_all) % 8, shard_rows), jnp.float32),
        ],
        axis=1,
    )
    block_out = low(
        middle + axis_scatter(branch_out.reshape(groups_local, TOK_DEV, D), EXPERT_AXIS)
    )
    (grad_tokens, gain_sum, down_own), sums = closing(
        grad_first.reshape(token_count, -1),
        first_full,
        normed_all.reshape(token_count, D),
        block_out,
        tokens[0],
        full_attn_gain[None],
        grad_middle,
        gain_rows,
        [low(grad_latent_up), grad_out_weight],
        query_cols // 128 * 128,
    )
    first_sum, up_sum, out_sum = sums
    small_rows = shard_rows // groups_local
    small_own = lax.dynamic_slice_in_dim(gain_sum, expert_index * small_rows, small_rows, 1)
    latent_small = latent_rows // groups_local
    latent_own = lax.dynamic_slice_in_dim(gain_sum[2], expert_index * latent_small, latent_small, 0)
    down_start = query_cols % 128
    return (
        block_out[None],
        grad_tokens[None],
        small_own[0],
        query_join(first_sum[:, :query_cols]),
        down_own[:, down_start : down_start + down_cols],
        latent_own,
        up_sum,
        out_sum.T,
        small_own[1],
        small_own[3 : 3 + experts_all].T,
        shared_grads[:, :shared_cols],
        shared_grads[:, shared_pad : shared_pad + shared_cols],
        shared_grads[:, 2 * shared_pad : 2 * shared_pad + shared_cols].T,
        *expert_grads,
    )


def solution(mesh):
    in_specs = (
        P((DP_AXIS, EXPERT_AXIS), CONTEXT_AXIS, None),
        P((DP_AXIS, EXPERT_AXIS), CONTEXT_AXIS, None),
        P((DP_AXIS, EXPERT_AXIS), CONTEXT_AXIS, None),
        P((DP_AXIS, CONTEXT_AXIS)),
        P((DP_AXIS, CONTEXT_AXIS), EXPERT_AXIS),
        P((DP_AXIS, CONTEXT_AXIS), None),
        P((DP_AXIS, CONTEXT_AXIS)),
        P((DP_AXIS, CONTEXT_AXIS), EXPERT_AXIS),
        P(EXPERT_AXIS, (DP_AXIS, CONTEXT_AXIS)),
        P((DP_AXIS, CONTEXT_AXIS)),
        P((DP_AXIS, CONTEXT_AXIS), None),
        P((DP_AXIS, CONTEXT_AXIS), EXPERT_AXIS),
        P((DP_AXIS, CONTEXT_AXIS), EXPERT_AXIS),
        P(EXPERT_AXIS, (DP_AXIS, CONTEXT_AXIS)),
        P(EXPERT_AXIS, (DP_AXIS, CONTEXT_AXIS), None),
        P(EXPERT_AXIS, (DP_AXIS, CONTEXT_AXIS), None),
        P(EXPERT_AXIS, (DP_AXIS, CONTEXT_AXIS), None),
    )
    out_specs = (
        P((DP_AXIS, EXPERT_AXIS), CONTEXT_AXIS, None),
        P((DP_AXIS, EXPERT_AXIS), CONTEXT_AXIS, None),
        P((DP_AXIS, CONTEXT_AXIS, EXPERT_AXIS)),
        P((DP_AXIS, CONTEXT_AXIS), EXPERT_AXIS),
        P((DP_AXIS, CONTEXT_AXIS, EXPERT_AXIS), None),
        P((DP_AXIS, CONTEXT_AXIS, EXPERT_AXIS)),
        P((DP_AXIS, CONTEXT_AXIS), EXPERT_AXIS),
        P(EXPERT_AXIS, (DP_AXIS, CONTEXT_AXIS)),
        P((DP_AXIS, CONTEXT_AXIS, EXPERT_AXIS)),
        P((DP_AXIS, CONTEXT_AXIS, EXPERT_AXIS), None),
        P((DP_AXIS, CONTEXT_AXIS), EXPERT_AXIS),
        P((DP_AXIS, CONTEXT_AXIS), EXPERT_AXIS),
        P(EXPERT_AXIS, (DP_AXIS, CONTEXT_AXIS)),
        P(EXPERT_AXIS, (DP_AXIS, CONTEXT_AXIS), None),
        P(EXPERT_AXIS, (DP_AXIS, CONTEXT_AXIS), None),
        P(EXPERT_AXIS, (DP_AXIS, CONTEXT_AXIS), None),
    )
    return jax.shard_map(body, mesh=mesh, in_specs=in_specs, out_specs=out_specs, check_vma=False)
```

```python
import jax
import jax.numpy as jnp
from jax import lax
from jax.experimental import pallas as pl
from jax.experimental.pallas import tpu as pltpu
from jax.experimental.layout import Layout, with_layout_constraint
from jax.sharding import PartitionSpec as P

D = 2048
NOPE = 128
ROPE = 64
VDIM = 128
LATENT = 512
TOPK = 6
PROMPT_DEV = 64
CONT_LEN = 64
TOK_DEV = 128


epsilon = 1e-06


def norm_rows(values, scale_gain):
    return (
        values * lax.rsqrt(jnp.mean(values * values, axis=-1, keepdims=True) + epsilon) * scale_gain
    )


def rotary_tables(places, half_size):
    frequency = 10000.0 ** (-jnp.arange(half_size, dtype=jnp.float32) / half_size)
    angles = places[:, None] * frequency[None, :]
    return (jnp.cos(angles), jnp.sin(angles))


def rotate(values, cosine, sine_part):
    half_size = values.shape[-1] // 2
    lower_half = values[..., :half_size]
    upper_half = values[..., half_size:]
    return jnp.concatenate(
        [
            lower_half * cosine - upper_half * sine_part,
            upper_half * cosine + lower_half * sine_part,
        ],
        axis=-1,
    )


def product(left_side, right_side):
    return jnp.dot(left_side, right_side, preferred_element_type=jnp.float32)


def product_left(left_side, right_side):
    return lax.dot_general(
        left_side, right_side, (((0,), (0,)), ((), ())), preferred_element_type=jnp.float32
    )


def product_right(left_side, right_side):
    return lax.dot_general(
        left_side, right_side, (((1,), (1,)), ((), ())), preferred_element_type=jnp.float32
    )


def against_rows(left_side, right_side):
    return lax.dot_general(
        left_side,
        right_side,
        (((left_side.ndim - 1,), (1,)), ((), ())),
        preferred_element_type=jnp.float32,
    )


DP_AXIS, CONTEXT_AXIS, EXPERT_AXIS = "dp", "context", "expert"
PLANE = (DP_AXIS, CONTEXT_AXIS)


def swap(values, axis, mask):
    count = lax.axis_size(axis)
    return lax.ppermute(values, axis, [(i, i ^ mask) for i in range(count)])


def place_pieces(pieces, index, count):
    first = pieces[0]
    whole = jnp.zeros((count,) + first.shape, first.dtype)
    for mask, piece in pieces.items():
        whole = lax.dynamic_update_slice(whole, piece[None], (index ^ mask,) + (0,) * first.ndim)
    return with_layout_constraint(whole, Layout(tuple(range(whole.ndim))))


def low(values):
    return values.astype(jnp.bfloat16)


def wide(values):
    return values.astype(jnp.float32)


def axis_gather(values, axis):
    count = lax.axis_size(axis)
    pieces = {mask: swap(values, axis, mask) if mask else values for mask in range(count)}
    return place_pieces(pieces, lax.axis_index(axis), count)


def axis_scatter(blocks, axis):
    count = lax.axis_size(axis)
    index = lax.axis_index(axis)

    def part(mask):
        return lax.dynamic_index_in_dim(blocks, index ^ mask, 0, keepdims=False)

    total = wide(part(0))
    for mask in range(1, count):
        total = total + wide(swap(low(part(mask)), axis, mask))
    return total


MESH_ID = pl.DeviceIdType.MESH
ANY = pl.BlockSpec(memory_space=pl.ANY)
INSIDE = pl.BlockSpec(memory_space=pltpu.VMEM)


def plane_here():
    return lax.axis_index(DP_AXIS) * lax.axis_size(CONTEXT_AXIS) + lax.axis_index(CONTEXT_AXIS)


def plane_device(mask):
    contexts = lax.axis_size(CONTEXT_AXIS)
    other = jnp.bitwise_xor(plane_here(), mask)
    return {DP_AXIS: other // contexts, CONTEXT_AXIS: lax.rem(other, contexts)}


def line_device(offset):
    return {EXPERT_AXIS: lax.axis_index(EXPERT_AXIS) + offset}


def signal(device):
    pl.semaphore_signal(
        pltpu.get_barrier_semaphore(), inc=1, device_id=device, device_id_type=MESH_ID
    )


def meet(masks, line):
    count = len(masks)
    for mask in masks:
        signal(plane_device(mask))
    if line:
        place, last = lax.axis_index(EXPERT_AXIS), lax.axis_size(EXPERT_AXIS) - 1
        pl.when(place > 0)(lambda: signal(line_device(-1)))
        pl.when(place < last)(lambda: signal(line_device(1)))
        count = count + jnp.where(place > 0, 1, 0) + jnp.where(place < last, 1, 0)
    pl.semaphore_wait(pltpu.get_barrier_semaphore(), count)


def remote(source, target, send, recv, device):
    return pltpu.make_async_remote_copy(
        src_ref=source,
        dst_ref=target,
        send_sem=send,
        recv_sem=recv,
        device_id=device,
        device_id_type=MESH_ID,
    )


def arrived(target, send, recv):
    remote(target, target, send, recv, plane_device(1)).wait_recv()


def run_tasks(*tasks):
    active = list(tasks)
    while active:
        for task in list(active):
            if next(task, None) is None:
                active.remove(task)


def plane_gather_task(source, target, own, send, recv):
    rows = source.shape[0]
    half = rows // 2
    here = plane_here()

    def slot(mask, first=0, count=rows):
        start = pl.multiple_of(jnp.bitwise_xor(here, mask) * rows + first, 16)
        return target.at[pl.ds(start, count)]

    def go(number, source_ref, target_ref, mask):
        copy = remote(source_ref, target_ref, send.at[number], recv.at[number], plane_device(mask))
        copy.start()
        return copy

    def got(number, ref):
        arrived(ref, send.at[number], recv.at[number])

    local = pltpu.make_async_copy(source, slot(0), own)
    copies = [go(0, source, slot(0), 2), go(1, source, slot(0), 4)]
    yield 1
    copies.append(go(4, source, slot(0), 1))
    local.start()
    yield 1
    got(0, slot(2))
    copies.append(go(2, slot(2, 0, half), slot(2, 0, half), 4))
    copies.append(go(5, slot(2), slot(2), 1))
    yield 1
    got(1, slot(4))
    copies.append(go(3, slot(4, half, half), slot(4, half, half), 2))
    copies.append(go(6, slot(4), slot(4), 1))
    yield 1
    got(2, slot(6, 0, half))
    copies.append(go(7, slot(6, 0, half), slot(6, 0, half), 1))
    yield 1
    got(3, slot(6, half, half))
    copies.append(go(8, slot(6, half, half), slot(6, half, half), 1))
    yield 1
    got(4, slot(1))
    got(5, slot(3))
    got(6, slot(5))
    got(7, slot(7, 0, half))
    got(8, slot(7, half, half))
    local.wait()
    for copy in copies:
        copy.wait_send()


def expert_fetch_task(source, target, stage, own, send, recv):
    if source.shape[0] == 1:
        load = pltpu.make_async_copy(source.at[0], stage, own)
        load.start()
        load.wait()
        yield from plane_gather_task(stage, target, own, send, recv)
        return
    rows = source.shape[1]
    here = plane_here()
    expert_own = here // 2

    def slot(mask):
        start = pl.multiple_of(jnp.bitwise_xor(here, mask) * rows, 16)
        return target.at[pl.ds(start, rows)]

    def go(number, source_ref, target_ref, mask):
        copy = remote(source_ref, target_ref, send.at[number], recv.at[number], plane_device(mask))
        copy.start()
        return copy

    def got(number, ref):
        arrived(ref, send.at[number], recv.at[number])

    copies = []
    for k in (3, 1, 2):
        copies.append(go(k, source.at[jnp.bitwise_xor(expert_own, k)], slot(0), 2 * k))
    load = pltpu.make_async_copy(source.at[expert_own], stage, own)
    load.start()
    yield 1
    load.wait()
    local = pltpu.make_async_copy(stage, slot(0), own)
    local.start()
    copies.append(go(0, stage, slot(0), 1))
    for k in (1, 2, 3):
        yield 1
        got(k, slot(2 * k))
        copies.append(go(4 + k, slot(2 * k), slot(2 * k), 1))
    yield 1
    got(0, slot(1))
    for k in (1, 2, 3):
        got(4 + k, slot(2 * k + 1))
    local.wait()
    for copy in copies:
        copy.wait_send()


LINE_PARTS = 4


def line_gather_steps(target, send, recv, rows):
    place, count = lax.axis_index(EXPERT_AXIS), lax.axis_size(EXPERT_AXIS)
    part = rows // LINE_PARTS

    def piece(block, c):
        return target.at[block, pl.ds(c * part, part)]

    def copy(way, distance, c, source=None):
        block = place - way * distance
        ref = piece(block, c)
        return remote(
            ref if source is None else source,
            ref,
            send.at[(way + 1) // 2, distance, c],
            recv.at[(way + 1) // 2, distance, c],
            line_device(way),
        )

    def has_next(way):
        return place < count - 1 if way == 1 else place > 0

    def has_block(way, distance):
        return place - distance >= 0 if way == 1 else place + distance < count

    def begin(c, source):
        for way in (1, -1):
            pl.when(has_next(way))(lambda way=way: copy(way, 0, c, source).start())

    def forward(c, distance):
        for way in (1, -1):

            @pl.when(has_block(way, distance))
            def _(way=way):
                ref = piece(place - way * distance, c)
                arrived(
                    ref,
                    send.at[(way + 1) // 2, distance - 1, c],
                    recv.at[(way + 1) // 2, distance - 1, c],
                )
                if distance < count - 1:
                    pl.when(has_next(way))(lambda: copy(way, distance, c).start())

    def finish(source):
        for c in range(LINE_PARTS):
            for way in (1, -1):
                for distance in range(count - 1):

                    @pl.when(jnp.logical_and(has_next(way), has_block(way, distance)))
                    def _(way=way, distance=distance, c=c):
                        copy(way, distance, c, source(c) if distance == 0 else None).wait_send()

    return begin, forward, finish


def line_gather_task(source, target, own, send, recv):
    rows = source.shape[0]
    part = rows // LINE_PARTS
    count = lax.axis_size(EXPERT_AXIS)
    begin, forward, finish = line_gather_steps(target, send, recv, rows)
    local = pltpu.make_async_copy(source, target.at[lax.axis_index(EXPERT_AXIS)], own)
    for c in range(LINE_PARTS):
        begin(c, source.at[pl.ds(c * part, part)])
    local.start()
    yield 1
    for distance in range(1, count):
        for c in range(LINE_PARTS):
            forward(c, distance)
        yield 1
    local.wait()
    finish(lambda c: source.at[pl.ds(c * part, part)])


def line_semaphores():
    count = lax.axis_size(EXPERT_AXIS)
    return [pltpu.SemaphoreType.DMA((2, count, LINE_PARTS))] * 2


def line_reduce_steps(partial, inbox, send, recv):
    place, count = lax.axis_index(EXPERT_AXIS), lax.axis_size(EXPERT_AXIS)
    rows = partial.shape[1]
    part = rows // LINE_PARTS

    def span(c):
        return pl.ds(c * part, part)

    def box(way, distance, c):
        return inbox.at[distance if way == 1 else count - distance, span(c)]

    def copy(way, distance, c, source):
        side = (way + 1) // 2
        return remote(
            source,
            box(way, distance - 1, c),
            send.at[side, distance, c],
            recv.at[side, distance - 1, c],
            line_device(way),
        )

    def wait_inbox(way, distance, c):
        side = (way + 1) // 2
        arrived(box(way, distance, c), send.at[side, distance, c], recv.at[side, distance, c])

    def has_source(way):
        return place > 0 if way == 1 else place < count - 1

    def has_target(way, distance):
        return place + distance < count if way == 1 else place - distance >= 0

    def step(c, distance):
        for way in (1, -1):
            mine = partial.at[place + way * distance, span(c)]

            def pass_on(way=way, mine=mine):
                came = box(way, distance, c)
                wait_inbox(way, distance, c)
                came[...] = low(wide(mine[...]) + wide(came[...]))
                copy(way, distance, c, came).start()

            def send_first(way=way, mine=mine):
                copy(way, distance, c, mine).start()

            valid = has_target(way, distance)
            if distance < count - 1:
                pl.when(jnp.logical_and(valid, has_source(way)))(pass_on)
                pl.when(jnp.logical_and(valid, jnp.logical_not(has_source(way))))(send_first)
            else:
                pl.when(valid)(send_first)

    def total(c, result):
        result[span(c)] = result[span(c)] + wide(partial[place, span(c)])
        for way in (1, -1):

            @pl.when(has_source(way))
            def _(way=way):
                wait_inbox(way, 0, c)
                result[span(c)] = result[span(c)] + wide(box(way, 0, c)[...])

    def stages(result, done):
        for t in range(LINE_PARTS + count - 1):
            for c in range(LINE_PARTS):
                distance = count - 1 - (t - c)
                if 1 <= distance <= count - 1:
                    step(c, distance)
                elif distance == 0:
                    total(c, result)
                    done(span(c), c)
            yield 1

    def finish():
        for c in range(LINE_PARTS):
            for way in (1, -1):
                for distance in range(1, count):
                    pl.when(has_target(way, distance))(
                        lambda way=way, distance=distance, c=c: copy(
                            way, distance, c, partial.at[place + way * distance, span(c)]
                        ).wait_send()
                    )

    return stages, finish


def gather_semaphores():
    return [
        pltpu.SemaphoreType.DMA(()),
        pltpu.SemaphoreType.DMA((9,)),
        pltpu.SemaphoreType.DMA((9,)),
    ]


def kernel_params(number):
    return pltpu.CompilerParams(
        collective_id=number,
        has_side_effects=True,
        vmem_limit_bytes=(52 if lax.axis_size(EXPERT_AXIS) <= 4 else 60) << 20,
    )


def opening(tokens, gains, matrices):
    count = lax.axis_size(EXPERT_AXIS)
    rows, width = tokens.shape
    number = len(matrices)
    planes = lax.axis_size(PLANE)
    depth = gains.shape[1]

    def kernel(*refs):
        tokens_ref, gains_ref = refs[:2]
        sources = refs[2 : 2 + number]
        gains_all, normed_all = refs[2 + number : 4 + number]
        targets = refs[4 + number : 4 + 2 * number]
        scratch = list(refs[4 + 2 * number :])
        normed, gain_box, gain_send, gain_recv = scratch[:4]
        line = scratch[4:7]
        semaphores = scratch[7:]
        meet(range(1, planes), True)
        here = plane_here()
        sends = []
        for mask in range(1, planes):
            copy = remote(
                gains_ref,
                gain_box.at[here],
                gain_send.at[mask],
                gain_recv.at[mask],
                plane_device(mask),
            )
            copy.start()
            sends.append(copy)
        tasks = [
            plane_gather_task(sources[i], targets[i], *semaphores[3 * i : 3 * i + 3])
            for i in range(number)
        ]
        for task in tasks:
            next(task)
        for task in tasks:
            next(task)
        gain_box[here] = gains_ref[...]
        values = wide(tokens_ref[...])
        scale = lax.rsqrt(jnp.mean(values * values, axis=-1, keepdims=True) + epsilon)
        for mask in range(1, planes):
            other = gain_box.at[jnp.bitwise_xor(here, mask)]
            arrived(other, gain_send.at[mask], gain_recv.at[mask])
        for i in range(planes):
            columns = slice(i * depth, (i + 1) * depth)
            normed[:, columns] = low(
                wide(tokens_ref[:, columns]) * scale * gain_box[i, 0:1, :]
            )
        gains_all[...] = gain_box[...]
        rows_task = line_gather_task(normed, normed_all, *line)
        next(rows_task)
        next(rows_task)
        for task in tasks:
            next(task)
        for task in tasks:
            next(task)
        run_tasks(rows_task, *tasks)
        for copy in sends:
            copy.wait_send()

    shapes = [
        jax.ShapeDtypeStruct((planes,) + gains.shape, jnp.float32),
        jax.ShapeDtypeStruct((count, rows, width), jnp.bfloat16),
    ] + [jax.ShapeDtypeStruct((planes * m.shape[0], m.shape[1]), m.dtype) for m in matrices]
    scratch = [
        pltpu.VMEM((rows, width), jnp.bfloat16),
        pltpu.VMEM((planes,) + gains.shape, jnp.float32),
        pltpu.SemaphoreType.DMA((planes,)),
        pltpu.SemaphoreType.DMA((planes,)),
        pltpu.SemaphoreType.DMA(()),
    ]
    scratch += line_semaphores()
    for _ in matrices:
        scratch += gather_semaphores()
    results = pl.pallas_call(
        kernel,
        out_shape=shapes,
        in_specs=[INSIDE] * (2 + number),
        out_specs=[INSIDE, ANY] + [ANY] * number,
        scratch_shapes=scratch,
        compiler_params=kernel_params(1),
        cost_estimate=pl.CostEstimate(
            flops=60_000_000, bytes_accessed=150_000_000, transcendentals=0
        ),
        name="opening",
    )(tokens, gains, *matrices)
    return results[0], results[1], results[2:]


def rope_fold(rope):
    lane = lax.broadcasted_iota(jnp.int32, (rope, ROPE), 0)
    column = lax.broadcasted_iota(jnp.int32, (rope, ROPE), 1)
    half = ROPE // 2
    target = lane // (rope // 2) * half + lax.rem(lane, half)
    return low(jnp.where(target == column, 1.0, 0.0))


def head_mask(head, heads, rope):
    lanes = lax.broadcasted_iota(jnp.int32, (1, rope), 1)
    return jnp.where(lax.rem(lanes, rope // 2) // (ROPE // 2) == head, 1.0, 0.0)


def middle_sum(query_nope, query_rope, keys, up, out, source, gain, experts, grads):
    count, rows = query_nope.shape[:2]
    key_count, rope = keys.shape[1], query_rope.shape[2]
    heads = query_nope.shape[2] // NOPE
    width = source.shape[1]
    planes, contexts = lax.axis_size(PLANE), lax.axis_size(CONTEXT_AXIS)
    routed = len(experts)
    score_scale = (NOPE + ROPE) ** (-0.5)

    def kernel(*refs):
        nope_ref, rope_ref, keys_ref, up_ref, out_ref, source_ref, gain_ref = refs[:7]
        expert_refs = refs[7 : 7 + routed]
        grads_ref = refs[7 + routed]
        outputs = refs[8 + routed :]
        middle_ref, hidden_all, grads_all, mixed, probs, expanded = outputs[:6]
        targets = outputs[6 : 6 + routed]
        scratch = list(outputs[6 + routed :])
        grads_line = [scratch.pop() for _ in range(3)][::-1]
        partial_ref = scratch.pop(0)
        inbox, hidden, reduce_send, reduce_recv, own, line_send, line_recv = scratch[:7]
        stages = scratch[7 : 7 + routed]
        semaphores = scratch[7 + routed :]
        meet((1, 2, 4, 6), True)
        reduce_stages, reduce_finish = line_reduce_steps(
            partial_ref, inbox, reduce_send, reduce_recv
        )
        begin, forward, finish = line_gather_steps(hidden_all, line_send, line_recv, rows)
        part = rows // LINE_PARTS

        def ready(span, c):
            values = middle_ref[span]
            scale = lax.rsqrt(jnp.mean(values * values, axis=-1, keepdims=True) + epsilon)
            hidden[span] = low(values * scale * gain_ref[...])
            begin(c, hidden.at[span])

        def line_task():
            middle_ref[...] = wide(source_ref[...])
            yield from reduce_stages(middle_ref, ready)
            local = pltpu.make_async_copy(hidden, hidden_all.at[lax.axis_index(EXPERT_AXIS)], own)
            local.start()
            for distance in range(1, count):
                for c in range(LINE_PARTS):
                    forward(c, distance)
                yield 1
            local.wait()
            finish(lambda c: hidden.at[pl.ds(c * part, part)])
            reduce_finish()

        tasks = [
            expert_fetch_task(
                expert_refs[i], targets[i], stages[i], *semaphores[3 * i : 3 * i + 3]
            )
            for i in range(routed)
        ]
        for task in tasks:
            next(task)
        grads_task = line_gather_task(grads_ref, grads_all, *grads_line)
        next(grads_task)
        for task in tasks:
            next(task)
        here = lax.axis_index(CONTEXT_AXIS)
        row = lax.broadcasted_iota(jnp.int32, (rows, key_count), 0)
        place = jnp.where(
            row < PROMPT_DEV,
            here * PROMPT_DEV + row,
            contexts * PROMPT_DEV + row - PROMPT_DEV,
        )
        allowed = lax.broadcasted_iota(jnp.int32, (rows, key_count), 1) <= place

        def attend(g, carry):
            expanded[g] = low(product(keys_ref[g, :, :LATENT], up_ref[...]))
            tiled = low(product_right(keys_ref[g, :, LATENT:], rope_fold(rope)))
            for h in range(heads):
                start = h * (NOPE + VDIM)
                scores = product_right(
                    nope_ref[g, :, h * NOPE : (h + 1) * NOPE],
                    expanded[g, :, start : start + NOPE],
                ) + product_right(
                    rope_ref[g] * low(head_mask(h, heads, rope)), tiled
                )
                scores = jnp.where(allowed, scores * score_scale, -1e30)
                powers = jnp.exp(scores - jnp.max(scores, axis=-1, keepdims=True))
                weights = low(powers / jnp.sum(powers, axis=-1, keepdims=True))
                probs[g, h] = weights
                mixed[g, :, h * VDIM : (h + 1) * VDIM] = low(
                    product(weights, expanded[g, :, start + NOPE : start + NOPE + VDIM])
                )
            partial_ref[g] = low(product_right(mixed[g], out_ref[...]))
            return carry

        lax.fori_loop(0, count, attend, 0)
        run_tasks(line_task())
        run_tasks(grads_task, *tasks)

    shapes = [
        jax.ShapeDtypeStruct((rows, width), jnp.float32),
        jax.ShapeDtypeStruct((count, rows, width), jnp.bfloat16),
        jax.ShapeDtypeStruct((count, rows, width), jnp.bfloat16),
        jax.ShapeDtypeStruct((count, rows, heads * VDIM), jnp.bfloat16),
        jax.ShapeDtypeStruct((count, heads, rows, key_count), jnp.bfloat16),
        jax.ShapeDtypeStruct((count, key_count, up.shape[1]), jnp.bfloat16),
    ] + [jax.ShapeDtypeStruct((planes * e.shape[1], e.shape[2]), e.dtype) for e in experts]
    scratch = [
        pltpu.VMEM((count, rows, width), jnp.bfloat16),
        pltpu.VMEM((count + 1, rows, width), jnp.bfloat16),
        pltpu.VMEM((rows, width), jnp.bfloat16),
    ]
    scratch += line_semaphores() + [pltpu.SemaphoreType.DMA(())] + line_semaphores()
    scratch += [pltpu.VMEM(e.shape[1:], e.dtype) for e in experts]
    for _ in range(routed):
        scratch += gather_semaphores()
    scratch += [pltpu.SemaphoreType.DMA(())] + line_semaphores()
    results = pl.pallas_call(
        kernel,
        out_shape=shapes,
        in_specs=[INSIDE] * 7 + [ANY] * routed + [INSIDE],
        out_specs=[INSIDE, ANY, ANY] + [INSIDE] * 3 + [ANY] * routed,
        scratch_shapes=scratch,
        compiler_params=kernel_params(2),
        cost_estimate=pl.CostEstimate(
            flops=60_000_000, bytes_accessed=300_000_000, transcendentals=0
        ),
        name="middle_sum",
    )(query_nope, query_rope, keys, up, out, source, gain, *experts, grads)
    return results[:6], results[6:]


def add_rows(target, first, second):
    def tile(i, carry):
        span = pl.ds(pl.multiple_of(i * 16, 16), 16)
        target[span] = (wide(first[span]) + wide(second[span])).astype(target.dtype)
        return carry

    lax.fori_loop(0, target.shape[0] // 16, tile, 0)


def expert_return_task(source, result, mine, came, load, send, recv):
    rows = mine.shape[1]
    here = plane_here()
    expert_own = here // 2

    def slot(mask):
        return source.at[pl.ds(pl.multiple_of(jnp.bitwise_xor(here, mask) * rows, 16), rows)]

    def go(number, source_ref, target_ref, mask):
        copy = remote(source_ref, target_ref, send.at[number], recv.at[number], plane_device(mask))
        copy.start()
        return copy

    copies, loads = [], {}

    def cross(k):
        copies.append(go(k, slot(2 * k + 1), came.at[k], 1))
        loads[k] = pltpu.make_async_copy(slot(2 * k), mine.at[k], load.at[k])
        loads[k].start()

    cross(3)
    yield 1
    for k, following in ((3, 1), (1, 2), (2, 0), (0, None)):
        if following is not None:
            cross(following)
        arrived(came.at[k], send.at[k], recv.at[k])
        loads[k].wait()
        add_rows(mine.at[k], mine.at[k], came.at[k])
        if k:
            copies.append(go(4 + k, mine.at[k], result.at[expert_own], 2 * k))
        else:
            local = pltpu.make_async_copy(mine.at[0], result.at[expert_own], load.at[0])
            local.start()
        yield 1
    for k in (3, 1, 2):
        arrived(
            result.at[jnp.bitwise_xor(expert_own, k)], send.at[4 + k], recv.at[4 + k]
        )
    local.wait()
    for copy in copies:
        copy.wait_send()


def expert_return_scratch(rows, columns):
    return [
        pltpu.VMEM((4, rows, columns), jnp.bfloat16),
        pltpu.VMEM((4, rows, columns), jnp.bfloat16),
        pltpu.SemaphoreType.DMA((4,)),
        pltpu.SemaphoreType.DMA((8,)),
        pltpu.SemaphoreType.DMA((8,)),
    ]


def plane_scatter_task(source, result, mine, came, box, last, load, send, recv):
    rows = mine.shape[1]
    half = rows // 2
    here = plane_here()
    upper, lower = pl.ds(0, half), pl.ds(half, half)

    def slot(mask):
        return source.at[pl.ds(pl.multiple_of(jnp.bitwise_xor(here, mask) * rows, 16), rows)]

    def go(number, source_ref, target_ref, mask):
        copy = remote(source_ref, target_ref, send.at[number], recv.at[number], plane_device(mask))
        copy.start()
        return copy

    def got(number, ref):
        arrived(ref, send.at[number], recv.at[number])

    copies, loads = [], {}

    def cross(k):
        copies.append(go(k, slot(2 * k + 1), came.at[k], 1))
        loads[k] = pltpu.make_async_copy(slot(2 * k), mine.at[k], load.at[k])
        loads[k].start()

    cross(3)
    yield 1
    for k, following in ((3, 1), (1, 2), (2, 0)):
        cross(following)
        got(k, came.at[k])
        loads[k].wait()
        add_rows(mine.at[k], mine.at[k], came.at[k])
        if k == 3:
            copies.append(go(4, mine.at[3, upper], box.at[0], 2))
            copies.append(go(5, mine.at[3, lower], box.at[1], 4))
        elif k == 1:
            copies.append(go(6, mine.at[1, upper], last.at[0, upper], 2))
        else:
            copies.append(go(7, mine.at[2, lower], last.at[1, lower], 4))
        yield 1
    got(4, box.at[0])
    add_rows(mine.at[2, upper], mine.at[2, upper], box.at[0])
    copies.append(go(8, mine.at[2, upper], last.at[1, upper], 4))
    yield 1
    got(5, box.at[1])
    add_rows(mine.at[1, lower], mine.at[1, lower], box.at[1])
    copies.append(go(9, mine.at[1, lower], last.at[0, lower], 2))
    yield 1
    got(0, came.at[0])
    loads[0].wait()
    add_rows(result, mine.at[0], came.at[0])
    got(6, last.at[0, upper])
    got(7, last.at[1, lower])
    yield 1
    got(9, last.at[0, lower])
    add_rows(result, result, last.at[0])
    got(8, last.at[1, upper])
    add_rows(result, result, last.at[1])
    for copy in copies:
        copy.wait_send()


def plane_scatter_scratch(rows, columns):
    return [
        pltpu.VMEM((4, rows, columns), jnp.bfloat16),
        pltpu.VMEM((4, rows, columns), jnp.bfloat16),
        pltpu.VMEM((2, rows // 2, columns), jnp.bfloat16),
        pltpu.VMEM((2, rows, columns), jnp.bfloat16),
        pltpu.SemaphoreType.DMA((4,)),
        pltpu.SemaphoreType.DMA((10,)),
        pltpu.SemaphoreType.DMA((10,)),
    ]


def norm_back(values, gain, grad):
    scale = lax.rsqrt(jnp.mean(values * values, axis=-1, keepdims=True) + epsilon)
    scaled = gain * grad
    mean = jnp.mean(values * scaled, axis=-1, keepdims=True)
    part = jnp.sum(values * scale * grad, axis=0, keepdims=True)
    return scale * scaled - values * (scale * scale * scale * mean), part


def branch_sum(partial, middle, gain, grad_out, experts, local_experts, later):
    count, rows, width = partial.shape
    planes = lax.axis_size(PLANE)
    routed, waiting = len(experts), len(later)

    def kernel(*refs):
        partial_ref, middle_ref, gain_ref, grad_ref = refs[:4]
        expert_refs = refs[4 : 4 + routed]
        outputs = refs[4 + routed + waiting :]
        grad_middle, grad_gain, branch_all = outputs[:3]
        results = outputs[3 : 3 + routed]
        scratch = list(outputs[3 + routed + waiting :])
        inbox, branch, reduce_send, reduce_recv, own, line_send, line_recv = scratch[:7]
        rest = scratch[7:]
        meet((1, 2, 4, 6), True)
        reduce_stages, reduce_finish = line_reduce_steps(
            partial_ref, inbox, reduce_send, reduce_recv
        )
        begin, forward, finish = line_gather_steps(branch_all, line_send, line_recv, rows)
        part = rows // LINE_PARTS

        def ready(span, c):
            back, gain_part = norm_back(middle_ref[span], gain_ref[...], grad_middle[span])
            grad_gain[...] = gain_part if c == 0 else grad_gain[...] + gain_part
            back = wide(grad_ref[span]) + back
            grad_middle[span] = back
            branch[span] = low(back)
            begin(c, branch.at[span])

        def line_task():
            grad_middle[...] = jnp.zeros((rows, width), jnp.float32)
            yield from reduce_stages(grad_middle, ready)
            local = pltpu.make_async_copy(branch, branch_all.at[lax.axis_index(EXPERT_AXIS)], own)
            local.start()
            for distance in range(1, count):
                for c in range(LINE_PARTS):
                    forward(c, distance)
                yield 1
            local.wait()
            finish(lambda c: branch.at[pl.ds(c * part, part)])
            reduce_finish()

        task_kind = plane_scatter_task if local_experts == 1 else expert_return_task
        size = len(rest) // routed
        tasks = [
            task_kind(
                expert_refs[i], results[i], *rest[size * i : size * (i + 1)]
            )
            for i in range(routed)
        ]
        line = line_task()
        for stage in range(5):
            for task in tasks:
                next(task)
            if stage:
                next(line)
        run_tasks(line)
        run_tasks(*tasks)

    shapes = [
        jax.ShapeDtypeStruct((rows, width), jnp.float32),
        jax.ShapeDtypeStruct((1, width), jnp.float32),
        jax.ShapeDtypeStruct((count, rows, width), jnp.bfloat16),
    ]
    scratch = [
        pltpu.VMEM((count + 1, rows, width), jnp.bfloat16),
        pltpu.VMEM((rows, width), jnp.bfloat16),
    ]
    scratch += line_semaphores() + [pltpu.SemaphoreType.DMA(())] + line_semaphores()
    for expert in experts:
        shard, columns = expert.shape[0] // planes, expert.shape[1]
        if local_experts == 1:
            shapes.append(jax.ShapeDtypeStruct((shard, columns), jnp.float32))
            scratch += plane_scatter_scratch(shard, columns)
        else:
            shapes.append(jax.ShapeDtypeStruct((local_experts, shard, columns), jnp.bfloat16))
            scratch += expert_return_scratch(shard, columns)
    shapes += [jax.ShapeDtypeStruct(x.shape, x.dtype) for x in later]
    results = pl.pallas_call(
        kernel,
        out_shape=shapes,
        in_specs=[INSIDE] * 4 + [ANY] * (routed + waiting),
        out_specs=[INSIDE, INSIDE, ANY]
        + [INSIDE if local_experts == 1 else ANY] * routed
        + [ANY] * waiting,
        input_output_aliases={4 + routed + i: 3 + routed + i for i in range(waiting)},
        scratch_shapes=scratch,
        compiler_params=kernel_params(3),
        cost_estimate=pl.CostEstimate(
            flops=60_000_000, bytes_accessed=300_000_000, transcendentals=0
        ),
        name="branch_sum",
    )(partial, middle, gain, grad_out, *experts, *later)
    grads = [
        wide(r).reshape((local_experts,) + r.shape[-2:]) for r in results[3 : 3 + routed]
    ]
    return results[0], results[1][0], results[2], grads, results[3 + routed :]


def meet_all():
    planes, count = lax.axis_size(PLANE), lax.axis_size(EXPERT_AXIS)
    for mask in range(1, planes):
        signal(plane_device(mask))
    for mask in range(1, count):
        signal({EXPERT_AXIS: jnp.bitwise_xor(lax.axis_index(EXPERT_AXIS), mask)})
    pl.semaphore_wait(pltpu.get_barrier_semaphore(), planes + count - 2)


def closing(grad_first, first_full, normed, ready_before, source, gain, grad_middle, gain_grads, matrices, spread):
    rows, width = source.shape
    count = lax.axis_size(EXPERT_AXIS)
    planes = lax.axis_size(PLANE)
    number = len(matrices) + 1
    sizes = [first_full.shape] + [m.shape for m in matrices]
    depth = gain_grads.shape[2]
    shard, columns = first_full.shape[0] // planes, first_full.shape[1]
    thin = shard // count

    def kernel(*refs):
        first_ref, full_ref, normed_ref, _, source_ref, gain_ref, middle_ref, gains_ref = refs[:8]
        sources = list(refs[8 : 7 + number])
        grad_tokens, gains_out, thin_out = refs[7 + number : 10 + number]
        results = refs[10 + number : 10 + 2 * number]
        scratch = list(refs[10 + 2 * number :])
        partial_ref, back_ref = scratch.pop(), scratch.pop()
        sources = [back_ref] + sources
        inbox, reduce_send, reduce_recv, gain_row = scratch[:4]
        gain_part, gain_box, gain_send, gain_recv = scratch[4:8]
        gain_held, gain_far, far_send, far_recv, thin_box, thin_send, thin_recv = scratch[8:15]
        rest = scratch[15:]
        meet_all()
        place = lax.axis_index(EXPERT_AXIS)
        here = plane_here()
        reduce_stages, reduce_finish = line_reduce_steps(
            partial_ref, inbox, reduce_send, reduce_recv
        )

        def ready(span, c):
            back, row = norm_back(wide(source_ref[span]), gain_ref[...], grad_tokens[span])
            gain_row[...] = row if c == 0 else gain_row[...] + row
            grad_tokens[span] = middle_ref[span] + back

        def line_task():
            grad_tokens[...] = jnp.zeros((rows, width), jnp.float32)
            yield from reduce_stages(grad_tokens, ready)
            gain_part[...] = gains_ref[...]
            for i in range(planes):
                gain_part[i, 0:1, :] = gain_row[:, i * depth : (i + 1) * depth]
            copies = []
            for mask in range(1, planes):
                copy = remote(
                    gain_part.at[jnp.bitwise_xor(here, mask)],
                    gain_box.at[mask],
                    gain_send.at[mask],
                    gain_recv.at[mask],
                    plane_device(mask),
                )
                copy.start()
                copies.append(copy)
            gain_total = gain_part[here]
            yield 1
            for mask in range(1, planes):
                arrived(gain_box.at[mask], gain_send.at[mask], gain_recv.at[mask])
                gain_total = gain_total + gain_box[mask]
            gain_held[...] = gain_total
            for mask in range(1, count):
                copy = remote(
                    gain_held,
                    gain_far.at[mask],
                    far_send.at[mask],
                    far_recv.at[mask],
                    {EXPERT_AXIS: jnp.bitwise_xor(place, mask)},
                )
                copy.start()
                copies.append(copy)
            yield 1
            for mask in range(1, count):
                arrived(gain_far.at[mask], far_send.at[mask], far_recv.at[mask])
                gain_total = gain_total + gain_far[mask]
            gains_out[...] = gain_total
            for copy in copies:
                copy.wait_send()
            reduce_finish()

        def first_task(task):
            yield from task
            copies = []

            def piece(mask):
                start = pl.multiple_of(jnp.bitwise_xor(place, mask) * thin, 8 if thin % 8 == 0 else thin)
                return results[0].at[pl.ds(start, thin), pl.ds(spread, columns - spread)]

            for mask in range(1, count):
                copy = remote(
                    piece(mask),
                    thin_box.at[mask],
                    thin_send.at[mask],
                    thin_recv.at[mask],
                    {EXPERT_AXIS: jnp.bitwise_xor(place, mask)},
                )
                copy.start()
                copies.append(copy)
            yield 1
            total = piece(0)[...]
            for mask in range(1, count):
                arrived(thin_box.at[mask], thin_send.at[mask], thin_recv.at[mask])
                total = total + thin_box[mask]
            thin_out[...] = total
            for copy in copies:
                copy.wait_send()

        size = len(rest) // number
        tasks = [
            plane_scatter_task(sources[i], results[i], *rest[size * i : size * (i + 1)])
            for i in range(number)
        ]
        tasks[0] = first_task(tasks[0])
        for task in tasks[1:]:
            next(task)

        def back_tile(i, carry):
            span = pl.ds(pl.multiple_of(i * 256, 256), 256)
            back_ref[span] = low(product_left(normed_ref[:, span], first_ref[...]))
            return carry

        lax.fori_loop(0, width // 256, back_tile, 0)
        for task in tasks:
            next(task)

        def partial_tile(i, carry):
            span = pl.ds(pl.multiple_of(i * 2 * rows, 2 * rows), 2 * rows)
            tile = low(product_right(first_ref[span], full_ref[...]))
            partial_ref[2 * i] = tile[:rows]
            partial_ref[2 * i + 1] = tile[rows:]
            return carry

        lax.fori_loop(0, count // 2, partial_tile, 0)
        line = line_task()
        for stage in range(5):
            for task in tasks if stage < 4 else tasks[:1]:
                next(task)
            next(line)
        run_tasks(*tasks, line)

    shapes = [
        jax.ShapeDtypeStruct((rows, width), jnp.float32),
        jax.ShapeDtypeStruct(gain_grads.shape[1:], jnp.float32),
        jax.ShapeDtypeStruct((thin, columns - spread), jnp.float32),
    ] + [jax.ShapeDtypeStruct((m[0] // planes, m[1]), jnp.float32) for m in sizes]
    scratch = [pltpu.VMEM((count + 1, rows, width), jnp.bfloat16)]
    scratch += line_semaphores()
    scratch += [
        pltpu.VMEM((1, width), jnp.float32),
        pltpu.VMEM(gain_grads.shape, jnp.float32),
        pltpu.VMEM(gain_grads.shape, jnp.float32),
        pltpu.SemaphoreType.DMA((planes,)),
        pltpu.SemaphoreType.DMA((planes,)),
        pltpu.VMEM(gain_grads.shape[1:], jnp.float32),
        pltpu.VMEM((count,) + gain_grads.shape[1:], jnp.float32),
        pltpu.SemaphoreType.DMA((count,)),
        pltpu.SemaphoreType.DMA((count,)),
        pltpu.VMEM((count, thin, columns - spread), jnp.float32),
        pltpu.SemaphoreType.DMA((count,)),
        pltpu.SemaphoreType.DMA((count,)),
    ]
    for m in sizes:
        scratch += plane_scatter_scratch(m[0] // planes, m[1])
    scratch += [
        pltpu.VMEM(first_full.shape, jnp.bfloat16),
        pltpu.VMEM((count, rows, width), jnp.bfloat16),
    ]
    results = pl.pallas_call(
        kernel,
        out_shape=shapes,
        in_specs=[INSIDE] * 3 + [ANY] + [INSIDE] * 4 + [ANY] * len(matrices),
        out_specs=[INSIDE] * (3 + number),
        scratch_shapes=scratch,
        compiler_params=kernel_params(4),
        cost_estimate=pl.CostEstimate(
            flops=60_000_000, bytes_accessed=200_000_000, transcendentals=0
        ),
        name="closing",
    )(grad_first, first_full, normed, ready_before, source, gain, grad_middle, gain_grads, *matrices)
    return results[:3], results[3:]


def silu_back(gate, up, grad):
    sigmoid_part = 1.0 / (1.0 + jnp.exp(-gate))
    silu_part = gate * sigmoid_part
    slope = sigmoid_part * (1.0 + gate * (1.0 - sigmoid_part))
    return silu_part * up, grad * up * slope, grad * silu_part


def row_copies(source, target, send, recv, copies):
    return [
        remote(source(k), target(k), send.at[k], recv.at[k], plane_device(k * copies))
        for k in (3, 1, 2)
    ]


def shared_and_rows(hidden, grads, weights, hidden_slots, grad_slots, gates, copies):
    tokens, width = hidden.shape
    columns = weights.shape[1] // 3
    pieces, slots = hidden_slots.shape[:2]
    exchanged = copies > 0
    tall = max(t for t in (256, 128, tokens) if tokens % t == 0)
    wide_part = 256

    def kernel(*refs):
        hidden_any, grads_any, weights_any, rows_any, grad_rows_any, gates_ref = refs[:6]
        act_out, back_out, weight_grads = refs[6:9]
        outputs = refs[9:12]
        scratch = refs[12:] if exchanged else refs[9:]
        hid, grd, wts, both, load = scratch[:5]
        loads = [
            pltpu.make_async_copy(hidden_any, hid, load.at[0]),
            pltpu.make_async_copy(weights_any, wts, load.at[1]),
            pltpu.make_async_copy(grads_any, grd, load.at[2]),
        ]
        moves = []
        if exchanged:
            semaphores = scratch[5:]
            meet([k * copies for k in (1, 2, 3)], False)
            for i, source in enumerate((gates_ref, rows_any, grad_rows_any)):
                moves += row_copies(
                    lambda k, source=source: source.at[k],
                    lambda k, i=i: outputs[i].at[k - 1],
                    semaphores[2 * i],
                    semaphores[2 * i + 1],
                    copies,
                )
            for move in moves:
                move.start()
        for copy in loads:
            copy.start()
        for copy in loads:
            copy.wait()

        def rows_tile(i, carry):
            span = pl.ds(pl.multiple_of(i * tall, 16), tall)
            gate = product(hid[span], wts[:, :columns])
            up = product(hid[span], wts[:, columns : 2 * columns])
            grad = product(grd[span], wts[:, 2 * columns :])
            act, dgate, dup = silu_back(gate, up, grad)
            act_out[span] = low(act)
            both[span, :columns] = low(dgate)
            both[span, columns:] = low(dup)
            back_out[span] = product_right(both[span], wts[:, : 2 * columns])
            return carry

        lax.fori_loop(0, tokens // tall, rows_tile, 0)

        def weights_tile(i, carry):
            span = pl.ds(pl.multiple_of(i * wide_part, wide_part), wide_part)
            weight_grads[span, : 2 * columns] = low(product_left(hid[:, span], both[...]))
            weight_grads[span, 2 * columns :] = low(product_left(grd[:, span], act_out[...]))
            return carry

        lax.fori_loop(0, width // wide_part, weights_tile, 0)
        for move in moves:
            move.wait()

    shapes = [
        jax.ShapeDtypeStruct((tokens, columns), jnp.bfloat16),
        jax.ShapeDtypeStruct((tokens, width), jnp.float32),
        jax.ShapeDtypeStruct(weights.shape, jnp.bfloat16),
    ]
    out_specs = [INSIDE] * 3
    scratch = [
        pltpu.VMEM(hidden.shape, jnp.bfloat16),
        pltpu.VMEM(grads.shape, jnp.bfloat16),
        pltpu.VMEM(weights.shape, jnp.bfloat16),
        pltpu.VMEM((tokens, 2 * columns), jnp.bfloat16),
        pltpu.SemaphoreType.DMA((3,)),
    ]
    if exchanged:
        shapes += [jax.ShapeDtypeStruct((3,) + x.shape[1:], x.dtype) for x in (gates, hidden_slots, grad_slots)]
        out_specs += [INSIDE, ANY, ANY]
        scratch += [pltpu.SemaphoreType.DMA((4,))] * 6
    results = pl.pallas_call(
        kernel,
        out_shape=shapes,
        in_specs=[ANY] * 5 + [INSIDE],
        out_specs=out_specs,
        scratch_shapes=scratch,
        compiler_params=kernel_params(5) if exchanged else pltpu.CompilerParams(vmem_limit_bytes=60 << 20),
        cost_estimate=pl.CostEstimate(
            flops=12 * tokens * width * columns, bytes_accessed=120_000_000, transcendentals=0
        ),
        name="shared_and_rows",
    )(hidden, grads, weights, hidden_slots, grad_slots, gates)
    return results[:3], results[3:]


def routed_expert(hidden_slots, grad_slots, hidden_far, grad_far, gates, weights, copies):
    slots, width = hidden_slots.shape[1:]
    gate_full, up_full, down_full = weights
    units = gate_full.shape[1]
    exchanged = copies > 0

    def kernel(*refs):
        far = 2 if exchanged else 0
        hidden_any, grad_any = refs[:2]
        hidden_far_any, grad_far_any = refs[2:4] if exchanged else (None, None)
        gates_ref, wg_any, wu_any, wd_any = refs[2 + far : 6 + far]
        pair_back, result_back, scale_back, dwg, dwu, dwd = refs[6 + far : 12 + far]
        scratch = refs[12 + far :]
        wg, wu, wd, hid, grd, act, dgate, dup, pair, result, scale = scratch[:11]
        tile_up, tile_down, load, own, store = scratch[11:16]
        semaphores = scratch[16:]

        def piece(ref, ref_far, k):
            return ref.at[k] if k == 0 or not exchanged else ref_far.at[k - 1]

        if exchanged:
            meet([k * copies for k in (1, 2, 3)], False)
        loads = {}

        def fetch(number, source, target):
            loads[number] = pltpu.make_async_copy(source, target, load.at[number])
            loads[number].start()

        def fetch_rows(number, source, source_far, target, k):
            span = pl.ds(k * slots, slots)
            fetch(number + k, piece(source, source_far, k), target.at[span])

        fetch(0, wg_any, wg)
        fetch_rows(3, hidden_any, hidden_far_any, hid, 3)
        loads[0].wait()
        loads[6].wait()
        fetch(1, wu_any, wu)
        fetch(2, wd_any, wd)
        for k in (3, 2, 1, 0):
            fetch_rows(7, grad_any, grad_far_any, grd, k)
            if k < 3:
                fetch_rows(3, hidden_any, hidden_far_any, hid, k)

        def back(k, which):
            source, target = ((pair, pair_back), (result, result_back), (scale, scale_back))[which]
            return remote(
                source.at[k],
                target.at[k],
                semaphores[2 * which].at[k],
                semaphores[2 * which + 1].at[k],
                plane_device(k * copies),
            )

        def deliver(k, which):
            if exchanged:
                pl.when(k > 0)(lambda: back(k, which).start())

        def first(i, carry):
            k = 3 - i
            span = pl.ds(pl.multiple_of(k * slots, 16), slots)

            def ready(*numbers):
                @pl.when(i == 0)
                def _():
                    for number in numbers:
                        loads[number].wait()

            gate = product(hid[span], wg[...])
            ready(1)
            up = product(hid[span], wu[...])
            ready(2, 10, 9, 8, 7, 5, 4, 3)
            grad = product_right(grd[span], wd[...])
            gates_here = gates_ref[span]
            act_part, dgate_part, dup_part = silu_back(gate, up, grad)
            scale[k] = jnp.broadcast_to(
                jnp.sum(act_part * grad, axis=-1, keepdims=True), scale.shape[1:]
            )
            act[span] = low(act_part * gates_here)
            dgate[span] = low(dgate_part * gates_here)
            dup[span] = low(dup_part * gates_here)
            pair[k] = low(product_right(dgate[span], wg[...]) + product_right(dup[span], wu[...]))
            deliver(k, 0)
            deliver(k, 2)
            result[k] = low(product(act[span], wd[...]))
            deliver(k, 1)
            return carry

        lax.fori_loop(0, 4, first, 0)
        kept = []
        for which, (source, target) in enumerate(
            ((pair, pair_back), (result, result_back), (scale, scale_back))
        ):
            for k in range(1 if exchanged else 4):
                copy = pltpu.make_async_copy(source.at[k], target.at[k], own.at[which, k])
                copy.start()
                kept.append(copy)

        def tiles(count, rows, buffer, target, compute):
            def put(i, slot):
                start = pl.multiple_of(i * rows, 16)
                return pltpu.make_async_copy(
                    buffer.at[slot], target.at[pl.ds(start, rows)], store.at[slot]
                )

            def tile(i, carry):
                slot = lax.rem(i, 2)
                pl.when(i >= 2)(lambda: put(i - 2, slot).wait())
                buffer[slot] = compute(pl.ds(pl.multiple_of(i * rows, rows), rows))
                put(i, slot).start()
                return carry

            lax.fori_loop(0, count, tile, 0)
            for i in (count - 2, count - 1):
                put(i, i % 2).wait()

        tiles(width // 256, 256, tile_up, dwg, lambda s: low(product_left(hid[:, s], dgate[...])))
        tiles(width // 256, 256, tile_up, dwu, lambda s: low(product_left(hid[:, s], dup[...])))
        tiles(units // 128, 128, tile_down, dwd, lambda s: low(product_left(act[:, s], grd[...])))
        for copy in kept:
            copy.wait()
        if exchanged:
            for which in (0, 2, 1):
                for k in (3, 2, 1):
                    back(k, which).wait()

    shapes = [
        jax.ShapeDtypeStruct((4, slots, width), jnp.bfloat16),
        jax.ShapeDtypeStruct((4, slots, width), jnp.bfloat16),
        jax.ShapeDtypeStruct((4, slots, 128), jnp.float32),
    ] + [jax.ShapeDtypeStruct(w.shape, jnp.bfloat16) for w in weights]
    rows = 4 * slots
    scratch = [pltpu.VMEM(w.shape, jnp.bfloat16) for w in weights]
    scratch += [pltpu.VMEM((rows, width), jnp.bfloat16)] * 2
    scratch += [pltpu.VMEM((rows, units), jnp.bfloat16)] * 3
    scratch += [pltpu.VMEM((4, slots, width), jnp.bfloat16)] * 2
    scratch += [pltpu.VMEM((4, slots, 128), jnp.float32)]
    scratch += [
        pltpu.VMEM((2, 256, units), jnp.bfloat16),
        pltpu.VMEM((2, 128, width), jnp.bfloat16),
        pltpu.SemaphoreType.DMA((11,)),
        pltpu.SemaphoreType.DMA((3, 4)),
        pltpu.SemaphoreType.DMA((2,)),
    ]
    if exchanged:
        scratch += [pltpu.SemaphoreType.DMA((4,))] * 6
    operands = [hidden_slots, grad_slots] + ([hidden_far, grad_far] if exchanged else [])
    results = pl.pallas_call(
        kernel,
        out_shape=shapes,
        in_specs=[ANY] * len(operands) + [INSIDE] + [ANY] * 3,
        out_specs=[ANY] * 6,
        scratch_shapes=scratch,
        compiler_params=pltpu.CompilerParams(
            collective_id=6, has_side_effects=True, vmem_limit_bytes=60 << 20
        )
        if exchanged
        else pltpu.CompilerParams(vmem_limit_bytes=60 << 20),
        cost_estimate=pl.CostEstimate(
            flops=18 * rows * units * width, bytes_accessed=200_000_000, transcendentals=0
        ),
        name="routed_expert",
    )(*operands, gates, *weights)
    return results


def attention_back(branch, out, probs, expanded, query_nope, query_rope, keys, up):
    groups, rows, width = branch.shape
    heads, key_count = probs.shape[1], probs.shape[3]
    rope = query_rope.shape[2]
    score_scale = (NOPE + ROPE) ** (-0.5)

    def kernel(*refs):
        branch_ref, out_ref, probs_ref, exp_ref, nope_ref, rope_ref, keys_ref, up_ref = refs[:8]
        dnope, drope, dkeys, dup, dexp = refs[8:]
        fold = rope_fold(rope)
        tiled = low(product_right(keys_ref[:, LATENT:], fold))
        dmixed = low(product(branch_ref[...], out_ref[...]))
        drope_sum = jnp.zeros((rows, rope), jnp.float32)
        dkey_sum = jnp.zeros((key_count, rope), jnp.float32)
        for h in range(heads):
            nope_span = slice(h * NOPE, (h + 1) * NOPE)
            key_span = slice(h * (NOPE + VDIM), h * (NOPE + VDIM) + NOPE)
            value_span = slice(h * (NOPE + VDIM) + NOPE, (h + 1) * (NOPE + VDIM))
            mask = head_mask(h, heads, rope)
            weights = probs_ref[h]
            part = dmixed[:, h * VDIM : (h + 1) * VDIM]
            dprobs = product_right(part, exp_ref[:, value_span])
            wide_weights = wide(weights)
            delta = jnp.sum(wide_weights * dprobs, axis=-1, keepdims=True)
            dscore = low(wide_weights * (dprobs - delta) * score_scale)
            dexp[:, key_span] = low(product_left(dscore, nope_ref[:, nope_span]))
            dexp[:, value_span] = low(product_left(weights, part))
            dnope[:, nope_span] = low(product(dscore, exp_ref[:, key_span]))
            drope_sum = drope_sum + product(dscore, tiled) * mask
            dkey_sum = dkey_sum + product_left(dscore, rope_ref[...] * low(mask))
        drope[...] = drope_sum
        dkeys[:, :LATENT] = product_right(dexp[...], up_ref[...])
        dkeys[:, LATENT:] = product(low(dkey_sum), fold)
        grad_up = product_left(keys_ref[:, :LATENT], dexp[...])

        @pl.when(pl.program_id(0) == 0)
        def _():
            dup[...] = grad_up

        @pl.when(pl.program_id(0) > 0)
        def _():
            dup[...] = dup[...] + grad_up

    def group(array):
        shape = array.shape
        return pl.BlockSpec(
            (None,) + tuple(shape[1:]), lambda g, n=len(shape) - 1: (g,) + (0,) * n
        )

    def whole(array):
        return pl.BlockSpec(array.shape, lambda g: (0, 0))

    shapes = [
        jax.ShapeDtypeStruct((groups, rows, heads * NOPE), jnp.bfloat16),
        jax.ShapeDtypeStruct((groups, rows, rope), jnp.float32),
        jax.ShapeDtypeStruct((groups, key_count, LATENT + ROPE), jnp.float32),
        jax.ShapeDtypeStruct(up.shape, jnp.float32),
    ]
    operands = [branch, out, probs, expanded, query_nope, query_rope, keys, up]
    return pl.pallas_call(
        kernel,
        grid=(groups,),
        out_shape=shapes,
        in_specs=[whole(x) if x is out or x is up else group(x) for x in operands],
        out_specs=[group(x) for x in shapes[:3]] + [whole(up)],
        scratch_shapes=[pltpu.VMEM((key_count, heads * (NOPE + VDIM)), jnp.bfloat16)],
        compiler_params=pltpu.CompilerParams(vmem_limit_bytes=40 << 20),
        cost_estimate=pl.CostEstimate(
            flops=20_000_000_000, bytes_accessed=30_000_000, transcendentals=0
        ),
        name="attention_back",
    )(*operands)


def body(
    tokens,
    routes,
    grad_out,
    attn_gain,
    query_weight,
    latent_down,
    latent_gain,
    latent_up,
    out_weight,
    ffn_gain,
    router_weight,
    shared_gate,
    shared_up,
    shared_down,
    expert_gate,
    expert_up,
    expert_down,
):
    contexts = lax.axis_size(CONTEXT_AXIS)
    context_index = lax.axis_index(CONTEXT_AXIS)
    groups_local = lax.axis_size(EXPERT_AXIS)
    expert_index = lax.axis_index(EXPERT_AXIS)
    plane_count = lax.axis_size(PLANE)
    plane_index = lax.axis_index(PLANE)
    local_experts = expert_gate.shape[0]
    experts_all = router_weight.shape[1]
    copies = plane_count // local_experts
    expert_own = plane_index // copies
    query_cols = query_weight.shape[1]
    heads_local = query_cols // (NOPE + ROPE)
    down_cols = LATENT + ROPE
    shard_rows = query_weight.shape[0]
    latent_rows = latent_up.shape[0]
    prompt_len = PROMPT_DEV * contexts
    capacity = (TOK_DEV * TOPK * 9 + 8 * experts_all - 1) // (8 * experts_all)
    slots = groups_local * capacity
    slots = -(-slots // 16) * 16 if local_experts > 1 else -(-slots // 64) * 64
    token_count = groups_local * TOK_DEV
    score_scale = (NOPE + ROPE) ** (-0.5)

    half_rope = ROPE // 2
    rope_cols = heads_local * half_rope
    nope_cols = heads_local * NOPE

    def query_split(columns):
        each = columns.reshape(columns.shape[0], heads_local, NOPE + ROPE)
        parts = (each[..., :NOPE], each[..., NOPE : NOPE + half_rope], each[..., NOPE + half_rope :])
        return [part.reshape(columns.shape[0], -1) for part in parts]

    def query_join(columns):
        rows = columns.shape[0]
        parts = (
            columns[:, :nope_cols],
            columns[:, nope_cols : nope_cols + rope_cols],
            columns[:, nope_cols + rope_cols :],
        )
        each = [part.reshape(rows, heads_local, -1) for part in parts]
        return jnp.concatenate(each, axis=-1).reshape(rows, query_cols)

    used_cols = query_cols + down_cols
    extra_cols = experts_all + 3
    pad_cols = -(used_cols + extra_cols) % 128
    gains = jnp.stack(
        [
            wide(attn_gain),
            wide(ffn_gain),
            jnp.pad(wide(latent_gain), (0, shard_rows - latent_gain.shape[0])),
        ]
        + [jnp.zeros((shard_rows,), jnp.float32)] * 5
    )
    first_local = jnp.concatenate(
        [
            *query_split(query_weight),
            latent_down,
            router_weight,
            jnp.zeros((shard_rows, 3 + pad_cols), jnp.bfloat16),
        ],
        axis=1,
    )
    shared_cols = shared_gate.shape[1]
    shared_pad = -(-shared_cols // 128) * 128

    def padded(weight):
        return jnp.pad(weight, ((0, 0), (0, shared_pad - shared_cols)))

    shared_own = jnp.concatenate(
        [padded(shared_gate), padded(shared_up), padded(shared_down.T)], axis=1
    )
    shared_whole = lax.all_gather(shared_own, PLANE, axis=0, tiled=True)
    gains_all, normed_all, (first_full, up_local, out_local) = opening(
        tokens[0], gains, [first_local, latent_up, out_weight.T]
    )
    full_router = first_full[:, used_cols : used_cols + experts_all]
    full_attn_gain = gains_all[:, 0].reshape(D)
    full_ffn_gain = gains_all[:, 1].reshape(D)
    full_latent_gain = gains_all[:, 2, : latent_gain.shape[0]].reshape(LATENT)

    within = jnp.arange(TOK_DEV, dtype=jnp.int32)
    query_places = jnp.where(
        within < PROMPT_DEV, context_index * PROMPT_DEV + within, prompt_len + within - PROMPT_DEV
    )
    cosine, sine_part = rotary_tables(query_places.astype(jnp.float32), ROPE // 2)
    source = wide(tokens[0])

    def pack_latent(comp_rows, latent_scale):
        return jnp.concatenate(
            [
                norm_rows(comp_rows[..., :LATENT], latent_scale),
                rotate(comp_rows[..., LATENT:], cosine[None], sine_part[None]),
            ],
            axis=-1,
        )

    routes_all = axis_gather(routes[0], EXPERT_AXIS)
    first_product = product(normed_all, first_full)
    compressed = first_product[..., query_cols:used_cols]
    packed = low(pack_latent(compressed, wide(full_latent_gain)))
    key_count = prompt_len + CONT_LEN
    keys = jnp.zeros((groups_local, contexts + 1, PROMPT_DEV, down_cols), jnp.bfloat16)
    prompt_own = packed[:, :PROMPT_DEV]
    for mask in range(contexts):
        came = swap(prompt_own, CONTEXT_AXIS, mask) if mask else prompt_own
        keys = lax.dynamic_update_slice(
            keys, came[:, None], (0, jnp.bitwise_xor(context_index, mask), 0, 0)
        )
    keys = lax.dynamic_update_slice(
        keys, packed[:, None, PROMPT_DEV:], (0, contexts, 0, 0)
    ).reshape(groups_local, key_count, down_cols)
    query_nope = low(first_product[..., :nope_cols])
    cosine_heads = jnp.tile(cosine, (1, heads_local))[None]
    sine_heads = jnp.tile(sine_part, (1, heads_local))[None]
    lower = first_product[..., nope_cols : nope_cols + rope_cols]
    upper = first_product[..., nope_cols + rope_cols : query_cols]
    query_rope = low(
        jnp.concatenate(
            [
                lower * cosine_heads - upper * sine_heads,
                upper * cosine_heads + lower * sine_heads,
            ],
            axis=-1,
        )
    )
    slot_experts = expert_index * local_experts + (
        expert_own ^ jnp.arange(local_experts, dtype=jnp.int32)
    )
    expert_cols = jnp.arange(experts_all, dtype=jnp.int32)[:, None] == slot_experts[None, :]
    chosen_slots = jnp.any(routes_all[..., None] == slot_experts, axis=2)
    before = (within[:, None] > within[None, :]).astype(jnp.bfloat16)
    rank = jnp.einsum(
        "ts,gsl->gtl",
        before,
        chosen_slots.astype(jnp.bfloat16),
        preferred_element_type=jnp.float32,
    ).astype(jnp.int32)
    slot_of = jnp.where(
        chosen_slots,
        rank + capacity * jnp.arange(groups_local, dtype=jnp.int32)[:, None, None],
        -1,
    ).reshape(token_count, local_experts)
    picked = (
        slot_of.T[:, None, :] == jnp.arange(slots, dtype=jnp.int32)[None, :, None]
    )
    picked_low = picked.astype(jnp.bfloat16).reshape(local_experts * slots, token_count)
    piece_slots = slots * local_experts // 4
    (middle, hidden_all, grad_all, mixed_all, probs, expanded), fetched = middle_sum(
        query_nope,
        query_rope,
        keys,
        up_local,
        out_local,
        tokens[0],
        full_ffn_gain[None],
        [expert_gate, expert_up, expert_down],
        grad_out[0],
    )
    gate_full, up_full, down_full = fetched
    hidden_flat = hidden_all.reshape(token_count, D)

    grad_flat = grad_all.reshape(token_count, D)
    hidden_slots = low(product(picked_low, hidden_flat)).reshape(4, piece_slots, D)
    grad_slots = low(product(picked_low, grad_flat)).reshape(4, piece_slots, D)
    logits = product(hidden_flat, full_router)
    expert_probs = jax.nn.softmax(logits, axis=-1)
    gate_tokens = jnp.sum(jnp.where(expert_cols[None], expert_probs[:, :, None], 0.0), axis=1)
    gate_slots = jnp.sum(jnp.where(picked, gate_tokens.T[:, None, :], 0.0), axis=-1)
    gate_slots = gate_slots.reshape(4, piece_slots)
    gates_padded = jnp.broadcast_to(
        jnp.pad(gate_slots, ((0, 0), (0, -piece_slots % 128)))[:, None], (4, 8, -(-piece_slots // 128) * 128)
    )
    row_hops = copies if local_experts > 1 else 0
    (act_shared, shared_hidden, shared_grads), far = shared_and_rows(
        hidden_flat, grad_flat, shared_whole, hidden_slots, grad_slots, gates_padded, row_hops
    )
    gates_far, hidden_far, grad_far = far if far else (None, None, None)
    if far:
        gate_slots = jnp.concatenate([gate_slots[:1], gates_far[:, 0, :piece_slots]], axis=0)
    pair_back, result, scale_back, *expert_partials = routed_expert(
        hidden_slots,
        grad_slots,
        hidden_far,
        grad_far,
        gate_slots.reshape(-1, 1),
        [gate_full, up_full, down_full],
        row_hops,
    )
    grad_gate_back = scale_back[:, :, 0].reshape(local_experts, slots)
    grad_routed = product_left(picked_low, pair_back.reshape(-1, D))
    grad_gate_tokens = jnp.sum(jnp.where(picked, grad_gate_back[:, :, None], 0.0), axis=1).T
    grad_spread = jnp.sum(
        jnp.where(expert_cols[None], grad_gate_tokens[:, None, :], 0.0), axis=-1
    )
    weighted = jnp.sum(expert_probs * grad_spread, axis=-1, keepdims=True)
    grad_logits = expert_probs * (grad_spread - weighted)
    grad_router = lax.dot_general(
        grad_logits,
        wide(hidden_flat),
        (((0,), (0,)), ((), ())),
        precision=lax.Precision.HIGHEST,
    )
    grad_from_router = lax.dot_general(
        grad_logits,
        wide(full_router),
        (((1,), (1,)), ((), ())),
        precision=lax.Precision.HIGHEST,
    )
    grad_hidden_part = low(
        shared_hidden + grad_routed + grad_from_router
    )
    grad_middle, grad_ffn_gain, branch_all, expert_grads, (result, shared_grads) = branch_sum(
        grad_hidden_part.reshape(groups_local, TOK_DEV, D),
        middle,
        full_ffn_gain[None],
        grad_out[0],
        expert_partials,
        local_experts,
        [result.reshape(-1, D), shared_grads],
    )
    shared_grads = wide(lax.psum_scatter(shared_grads, PLANE, scatter_dimension=0, tiled=True))
    routed_term = product_left(picked_low, result)
    branch_out = low(
        product_right(act_shared, shared_whole[:, 2 * shared_pad :]) + routed_term
    )
    grad_out_weight = low(
        product_left(
            branch_all.reshape(token_count, D), mixed_all.reshape(token_count, heads_local * VDIM)
        )
    )
    grad_nope, grad_rope, grad_keys, grad_latent_up = attention_back(
        branch_all,
        out_local,
        probs,
        expanded,
        query_nope,
        query_rope,
        keys,
        up_local,
    )
    lower, upper = grad_rope[..., :rope_cols], grad_rope[..., rope_cols:]
    grad_query_raw = jnp.concatenate(
        [
            grad_nope,
            low(lower * cosine_heads + upper * sine_heads),
            low(upper * cosine_heads - lower * sine_heads),
        ],
        axis=-1,
    )
    grad_keys = grad_keys.reshape(groups_local, contexts + 1, PROMPT_DEV, down_cols)

    def keys_of(mask):
        return lax.dynamic_index_in_dim(
            grad_keys, jnp.bitwise_xor(context_index, mask), 1, keepdims=False
        )

    prompt_sum = keys_of(0)
    for mask in range(1, contexts):
        prompt_sum = prompt_sum + wide(swap(low(keys_of(mask)), CONTEXT_AXIS, mask))
    grad_packed = jnp.concatenate([prompt_sum, grad_keys[:, contexts]], axis=1)
    _, pack_back = jax.vjp(pack_latent, compressed, wide(full_latent_gain))
    grad_compressed, grad_latent_gain = pack_back(grad_packed)
    grad_first = jnp.concatenate(
        [
            grad_query_raw,
            low(grad_compressed),
            jnp.zeros((groups_local, TOK_DEV, first_full.shape[1] - used_cols), jnp.bfloat16),
        ],
        axis=-1,
    )
    gain_rows = jnp.concatenate(
        [
            jnp.zeros((plane_count, 1, shard_rows), jnp.float32),
            grad_ffn_gain.reshape(plane_count, 1, shard_rows),
            jnp.pad(
                grad_latent_gain.reshape(plane_count, 1, latent_rows),
                ((0, 0), (0, 0), (0, shard_rows - latent_rows)),
            ),
            grad_router.reshape(experts_all, plane_count, shard_rows).transpose(1, 0, 2),
            jnp.zeros((plane_count, -(3 + experts_all) % 8, shard_rows), jnp.float32),
        ],
        axis=1,
    )
    block_out = low(
        middle + axis_scatter(branch_out.reshape(groups_local, TOK_DEV, D), EXPERT_AXIS)
    )
    (grad_tokens, gain_sum, down_own), sums = closing(
        grad_first.reshape(token_count, -1),
        first_full,
        normed_all.reshape(token_count, D),
        block_out,
        tokens[0],
        full_attn_gain[None],
        grad_middle,
        gain_rows,
        [low(grad_latent_up), grad_out_weight],
        query_cols // 128 * 128,
    )
    first_sum, up_sum, out_sum = sums
    small_rows = shard_rows // groups_local
    small_own = lax.dynamic_slice_in_dim(gain_sum, expert_index * small_rows, small_rows, 1)
    latent_small = latent_rows // groups_local
    latent_own = lax.dynamic_slice_in_dim(gain_sum[2], expert_index * latent_small, latent_small, 0)
    down_start = query_cols % 128
    return (
        block_out[None],
        grad_tokens[None],
        small_own[0],
        query_join(first_sum[:, :query_cols]),
        down_own[:, down_start : down_start + down_cols],
        latent_own,
        up_sum,
        out_sum.T,
        small_own[1],
        small_own[3 : 3 + experts_all].T,
        shared_grads[:, :shared_cols],
        shared_grads[:, shared_pad : shared_pad + shared_cols],
        shared_grads[:, 2 * shared_pad : 2 * shared_pad + shared_cols].T,
        *expert_grads,
    )


def solution(mesh):
    in_specs = (
        P((DP_AXIS, EXPERT_AXIS), CONTEXT_AXIS, None),
        P((DP_AXIS, EXPERT_AXIS), CONTEXT_AXIS, None),
        P((DP_AXIS, EXPERT_AXIS), CONTEXT_AXIS, None),
        P((DP_AXIS, CONTEXT_AXIS)),
        P((DP_AXIS, CONTEXT_AXIS), EXPERT_AXIS),
        P((DP_AXIS, CONTEXT_AXIS), None),
        P((DP_AXIS, CONTEXT_AXIS)),
        P((DP_AXIS, CONTEXT_AXIS), EXPERT_AXIS),
        P(EXPERT_AXIS, (DP_AXIS, CONTEXT_AXIS)),
        P((DP_AXIS, CONTEXT_AXIS)),
        P((DP_AXIS, CONTEXT_AXIS), None),
        P((DP_AXIS, CONTEXT_AXIS), EXPERT_AXIS),
        P((DP_AXIS, CONTEXT_AXIS), EXPERT_AXIS),
        P(EXPERT_AXIS, (DP_AXIS, CONTEXT_AXIS)),
        P(EXPERT_AXIS, (DP_AXIS, CONTEXT_AXIS), None),
        P(EXPERT_AXIS, (DP_AXIS, CONTEXT_AXIS), None),
        P(EXPERT_AXIS, (DP_AXIS, CONTEXT_AXIS), None),
    )
    out_specs = (
        P((DP_AXIS, EXPERT_AXIS), CONTEXT_AXIS, None),
        P((DP_AXIS, EXPERT_AXIS), CONTEXT_AXIS, None),
        P((DP_AXIS, CONTEXT_AXIS, EXPERT_AXIS)),
        P((DP_AXIS, CONTEXT_AXIS), EXPERT_AXIS),
        P((DP_AXIS, CONTEXT_AXIS, EXPERT_AXIS), None),
        P((DP_AXIS, CONTEXT_AXIS, EXPERT_AXIS)),
        P((DP_AXIS, CONTEXT_AXIS), EXPERT_AXIS),
        P(EXPERT_AXIS, (DP_AXIS, CONTEXT_AXIS)),
        P((DP_AXIS, CONTEXT_AXIS, EXPERT_AXIS)),
        P((DP_AXIS, CONTEXT_AXIS, EXPERT_AXIS), None),
        P((DP_AXIS, CONTEXT_AXIS), EXPERT_AXIS),
        P((DP_AXIS, CONTEXT_AXIS), EXPERT_AXIS),
        P(EXPERT_AXIS, (DP_AXIS, CONTEXT_AXIS)),
        P(EXPERT_AXIS, (DP_AXIS, CONTEXT_AXIS), None),
        P(EXPERT_AXIS, (DP_AXIS, CONTEXT_AXIS), None),
        P(EXPERT_AXIS, (DP_AXIS, CONTEXT_AXIS), None),
    )
    return jax.shard_map(body, mesh=mesh, in_specs=in_specs, out_specs=out_specs, check_vma=False)
```
